256 devices in a mesh: sec: 64 (over z_lo, x, y, core), tp: 4 (over z_hi).
Axes of the slice: x: 4, y: 4, z: 8 (z_hi: 4, z_lo: 2; z = z_hi * 2 + z_lo), core: 2. Of those that a mesh axis runs over, the one named last changes fastest.
Arguments:
- pixels: bfloat16 [12288, 3072], P('sec'), may hold values from -6 to 6
- w_encode: bfloat16 [3072, 2048], P(None, 'tp'), may hold values from -0.109375 to 0.109375
- w_latent: bfloat16 [2048, 64], P('tp'), may hold values from -0.25 to 0.25
- source_row: int32 [12288], P('sec'), may hold values from 0 to 12287, each once
- w_embed: bfloat16 [64, 3072], replicated, may hold values from -0.75 to 0.75
- mod_shift: float32 [3072], replicated, may hold values from -3 to 3
- mod_scale: float32 [3072], replicated, may hold values from 0.1 to 1.9
- gate: float32 [3072], replicated, may hold values from 0.1 to 1.9
- q_gain: float32 [128], replicated, may hold values from 1.5 to 3
- k_gain: float32 [128], replicated, may hold values from 1.5 to 3
- w_qkv: bfloat16 [3, 3072, 1536], P(None, 'sec', 'tp'), may hold values from -0.109375 to 0.109375
- w_out: bfloat16 [1536, 3072], P('tp', 'sec'), may hold values from -0.15625 to 0.15625
Outputs:
- latents: bfloat16 [12288, 64], P('sec')
- block_out: bfloat16 [12288, 3072], P('sec', 'tp')
The draws below stay inside these ranges and needn't reach their ends.
Inputs may be any that keep to these rules, and one draw needn't show every extreme that they name: `source_row`: each latent row appears exactly once.
All inputs are finite; a program needn't handle non-finite values.
Results may differ from the reference program's by a relative error of at most 0.04.
Values may be sent and summed in bfloat16 or wider, within the bound.
A program may use at most 128 MiB of HBM per device.

```python
import math
import jax
import jax.numpy as jnp
from jax import lax

D = 3072
HEADS_WIN = 12
HD = 128
PIX = 3072
VCH = 2048
LAT = 64
TOKENS = 12288


def block_scale(key, shape, pieces, least, largest):
    gain = 1.0
    for dim, parts in pieces:
        draws = jax.random.uniform(jax.random.fold_in(jax.random.fold_in(key, 6), dim), (parts,), jnp.float32, least / len(pieces), largest / len(pieces))
        gain = gain * jnp.repeat(jnp.exp(draws), shape[dim] // parts).reshape((-1,) + (1,) * (len(shape) - 1 - dim))
    return gain


def centred(own_key, extent, spread, reach, cuts=(), held_as=jnp.bfloat16):
    drawn = spread * jax.random.normal(own_key, extent, jnp.float32)
    if cuts:
        drawn = drawn * block_scale(own_key, extent, cuts, -0.22, 0.18)
    return jnp.clip(drawn, -reach, reach).astype(held_as)


def setup_inputs(seed: int = 0) -> dict:
    keys = jax.random.split(jax.random.key(seed), 13)
    pixels = centred(keys[0], (TOKENS, PIX), 1.0, 6.0, ((0, 64),))
    w_encode = centred(keys[1], (PIX, VCH), PIX ** -0.5, 0.109375, ((1, 4),))
    w_latent = centred(keys[2], (VCH, LAT), (VCH // 4) ** -0.5, 0.25, ((0, 4),))
    source_row = jax.random.permutation(keys[3], TOKENS).astype(jnp.int32)
    w_embed = centred(keys[4], (LAT, D), LAT ** -0.5, 0.75)
    mod_shift = centred(keys[5], (D,), 0.5, 3.0, (), jnp.float32)
    mod_scale = jnp.clip(1.0 + 0.18 * jax.random.normal(keys[6], (D,), jnp.float32), 0.1, 1.9)
    gate = jnp.clip(1.0 + 0.18 * jax.random.normal(keys[7], (D,), jnp.float32), 0.1, 1.9)
    q_gain = jnp.clip(jnp.exp(jax.random.uniform(keys[8], (HD,), jnp.float32, math.log(1.5), math.log(3.0))), 1.5, 3.0)
    k_gain = jnp.clip(jnp.exp(jax.random.uniform(keys[9], (HD,), jnp.float32, math.log(1.5), math.log(3.0))), 1.5, 3.0)
    w_qkv = centred(keys[10], (3, D, HEADS_WIN * HD), D ** -0.5, 0.109375, ((1, 64), (2, 4)))
    w_out = centred(keys[11], (HEADS_WIN * HD, D), (HEADS_WIN * HD) ** -0.5, 0.15625, ((0, 4), (1, 64)))
    return {"pixels": pixels, "w_encode": w_encode, "w_latent": w_latent, "source_row": source_row, "w_embed": w_embed, "mod_shift": mod_shift, "mod_scale": mod_scale, "gate": gate, "q_gain": q_gain, "k_gain": k_gain, "w_qkv": w_qkv, "w_out": w_out}


def one_head(operands):
    query, keyrow, valrow = operands
    scores = jnp.dot(query, keyrow.T, preferred_element_type=jnp.float32) * (1.0 / jnp.sqrt(jnp.float32(HD)))
    expos = jnp.exp(scores - lax.optimization_barrier(jnp.max(scores, axis=1, keepdims=True)))
    total = lax.optimization_barrier(jnp.sum(expos, axis=1, keepdims=True))
    summed = jnp.dot(expos.astype(jnp.bfloat16), valrow, preferred_element_type=jnp.float32)
    return (summed / total).astype(jnp.bfloat16)

def head_norm(values, gains):
    shaped = values.reshape(values.shape[0], HEADS_WIN, HD)
    return shaped * lax.rsqrt(lax.optimization_barrier(jnp.mean(shaped * shaped, axis=2, keepdims=True)) + 1e-06) * gains

def reference(pixels, w_encode, w_latent, source_row, w_embed, mod_shift, mod_scale, gate, q_gain, k_gain, w_qkv, w_out):
    hidden = jax.nn.silu(jnp.dot(pixels, w_encode, preferred_element_type=jnp.float32)).astype(jnp.bfloat16)
    encoded = jnp.dot(hidden, w_latent, preferred_element_type=jnp.float32).astype(jnp.bfloat16)
    latents = encoded[source_row]
    embedded = jnp.dot(latents, w_embed, preferred_element_type=jnp.float32)
    center = embedded - lax.optimization_barrier(jnp.mean(embedded, axis=1, keepdims=True))
    normed = center * lax.rsqrt(lax.optimization_barrier(jnp.mean(center * center, axis=1, keepdims=True)) + 1e-06)
    modulated = (normed * mod_scale + mod_shift).astype(jnp.bfloat16)
    query = head_norm(jnp.dot(modulated, w_qkv[0], preferred_element_type=jnp.float32), q_gain).astype(jnp.bfloat16)
    keyrow = head_norm(jnp.dot(modulated, w_qkv[1], preferred_element_type=jnp.float32), k_gain).astype(jnp.bfloat16)
    valrow = jnp.dot(modulated, w_qkv[2], preferred_element_type=jnp.float32).astype(jnp.bfloat16)
    valrow = valrow.reshape(TOKENS, HEADS_WIN, HD)
    attended = lax.map(one_head, (query.transpose(1, 0, 2), keyrow.transpose(1, 0, 2), valrow.transpose(1, 0, 2)))
    attended = attended.transpose(1, 0, 2).reshape(TOKENS, HEADS_WIN * HD)
    projected = jnp.dot(attended, w_out, preferred_element_type=jnp.float32)
    block_out = (embedded + gate * projected).astype(jnp.bfloat16)
    return (latents, block_out)
```

```python
import functools

import jax
import jax.numpy as jnp
from jax import lax
from jax.experimental import pallas as pl
from jax.experimental.pallas import tpu as pltpu
from jax.sharding import PartitionSpec as P

MESH = pl.DeviceIdType.MESH
HD = 128
HEADS = 3
LAT = 64
ROWS = 192
LANES = 256
WID = HEADS * HD
F32 = jnp.float32
BF16 = jnp.bfloat16
NT = (((1,), (1,)), ((), ()))
NN = (((1,), (0,)), ((), ()))
TN = (((0,), (0,)), ((), ()))
PIECE = 128
STAT = 64
MROW = 80
EPS = 1e-6
TOP = 100.0
LOG2E = 1.4426950408889634
VMEM_LIMIT = 48 * 1024 * 1024


def dot(a, b, dims):
    return lax.dot_general(a, b, dims, preferred_element_type=F32)


def split(value):
    high = value.astype(BF16).astype(F32)
    return high, value - high


def barrier_with(greet, waits):
    barrier = pltpu.get_barrier_semaphore()
    for device in greet:
        pl.semaphore_signal(barrier, inc=1, device_id=device, device_id_type=MESH)
    pl.semaphore_wait(barrier, waits)


def remote(src, dst, send, recv, device):
    return pltpu.make_async_remote_copy(
        src_ref=src, dst_ref=dst, send_sem=send, recv_sem=recv, device_id=device, device_id_type=MESH
    )


def reduce_kernel(lat_ref, wp_ref, lat_out, w_out, lat_in, core_in, half, x_in, y_in, total, send, recv):
    s = lax.axis_index("sec")
    t = lax.axis_index("tp")
    z = s // 32
    x = (s // 8) % 4
    y = (s // 2) % 4
    c = s % 2
    sibling = {"sec": s + 1 - 2 * c}
    tp_peers = [{"tp": (t + k) % 4} for k in range(1, 4)]
    x_at = [(x + k) % 4 for k in range(1, 4)]
    x_peers = [{"sec": s + (xx - x) * 8} for xx in x_at]
    b = z * 4 + y
    b_at = [(b + k) % 8 for k in range(1, 8)]
    b_peers = [{"sec": (bb // 4) * 32 + x * 8 + (bb % 4) * 2 + c} for bb in b_at]
    everyone = tp_peers + [sibling] + x_peers + b_peers
    barrier_with(everyone, len(everyone))

    tp_copies = []
    for k in range(3):
        copy = remote(lat_ref, lat_in.at[t], send.at[k], recv.at[k], tp_peers[k])
        copy.start()
        tp_copies.append(copy)
    other = pl.multiple_of((1 - c) * 576, 576)
    mine = pl.multiple_of(c * 576, 576)
    core_copy = remote(wp_ref.at[pl.ds(other, 576)], core_in, send.at[3], recv.at[3], sibling)
    core_copy.start()
    lat_in[t] = lat_ref[...]
    core_copy.wait_recv()
    half[...] = (wp_ref[pl.ds(mine, 576), :].astype(F32) + core_in[...].astype(F32)).astype(BF16)
    x_copies = []
    for k in range(3):
        rows = pl.ds(pl.multiple_of(x_at[k] * 144, 144), 144)
        copy = remote(half.at[rows], x_in.at[x], send.at[4 + k], recv.at[4 + k], x_peers[k])
        copy.start()
        x_copies.append(copy)
    x_in[x] = half[pl.ds(pl.multiple_of(x * 144, 144), 144), :]
    for copy in x_copies:
        copy.wait_recv()
    added = x_in[0].astype(F32)
    for k in range(1, 4):
        added += x_in[k].astype(F32)
    y_in[b] = added.astype(BF16)
    b_copies = []
    for k in range(7):
        copy = remote(y_in.at[b], y_in.at[b], send.at[7 + k], recv.at[7 + k], b_peers[k])
        copy.start()
        b_copies.append(copy)
    for copy in tp_copies:
        copy.wait_recv()
    summed = lat_in[0].astype(F32)
    for k in range(1, 4):
        summed += lat_in[k].astype(F32)
    lat_out[...] = summed.astype(BF16)
    for copy in b_copies:
        copy.wait_recv()
    added = y_in[0].astype(F32)
    for k in range(1, 8):
        added += y_in[k].astype(F32)
    place = pl.ds(pl.multiple_of(c * 576 + x * 144, 144), 144)
    total[place, :] = added.astype(BF16)
    g_copies = []
    for k in range(3):
        copy = remote(total.at[place], total.at[place], send.at[14 + k], recv.at[14 + k], x_peers[k])
        copy.start()
        g_copies.append(copy)
    for copy in g_copies:
        copy.wait_recv()
    last = remote(total.at[pl.ds(mine, 576)], total.at[pl.ds(mine, 576)], send.at[17], recv.at[17], sibling)
    last.start()
    last.wait_recv()
    w_out[...] = total[...]
    for copy in tp_copies + [core_copy] + x_copies + b_copies + g_copies + [last]:
        copy.wait_send()


def reduce_call(lat_part, w_part):
    whole = pl.BlockSpec(memory_space=pltpu.VMEM)
    return pl.pallas_call(
        reduce_kernel,
        out_shape=(
            jax.ShapeDtypeStruct((LAT, LANES), BF16),
            jax.ShapeDtypeStruct((3 * WID, HD), BF16),
        ),
        in_specs=[whole] * 2,
        out_specs=(whole, whole),
        scratch_shapes=[
            pltpu.VMEM((4, LAT, LANES), BF16),
            pltpu.VMEM((576, HD), BF16),
            pltpu.VMEM((576, HD), BF16),
            pltpu.VMEM((4, 144, HD), BF16),
            pltpu.VMEM((8, 144, HD), BF16),
            pltpu.VMEM((1152, HD), BF16),
            pltpu.SemaphoreType.DMA((18,)),
            pltpu.SemaphoreType.DMA((18,)),
        ],
        compiler_params=pltpu.CompilerParams(collective_id=0, has_side_effects=True, vmem_limit_bytes=VMEM_LIMIT),
    )(lat_part, w_part)


def owner_kernel(lat_ref, w_ref, embed_ref, wo_ref, piece_ref, m_ref):
    lat = lat_ref[...]
    embedded = dot(embed_ref[...], lat, TN)
    center = embedded - jnp.mean(embedded, axis=0, keepdims=True)
    rstd = lax.rsqrt(jnp.mean(center * center, axis=0, keepdims=True) + EPS)
    piece_ref[0:LAT, :] = lat
    stats = [rstd]
    keys = w_ref[WID : 2 * WID, :]
    raw = dot(keys[:, 0:LAT], lat, NN) * rstd + keys[:, LAT : LAT + 1].astype(F32)
    for h in range(HEADS):
        part = raw[h * HD : (h + 1) * HD, :]
        stats.append(lax.rsqrt(jnp.mean(part * part, axis=0, keepdims=True) + EPS))
    row = lax.broadcasted_iota(jnp.int32, (16, LANES), 0)
    block = jnp.zeros((16, LANES), F32)
    for i, value in enumerate(stats):
        high, low = split(value)
        block = jnp.where(row == 2 * i, high, block)
        block = jnp.where(row == 2 * i + 1, low, block)
    piece_ref[STAT : STAT + 16, :] = block.astype(BF16)
    lane = lax.broadcasted_iota(jnp.int32, (48, HD), 1)
    terms = [
        dot(wo_ref[h * HD : (h + 1) * HD, :], w_ref[2 * WID + h * HD : 2 * WID + (h + 1) * HD, :], TN)
        for h in range(HEADS)
    ]
    first = jnp.where(lane < LAT, terms[0], pltpu.roll(terms[1], LAT, 1))
    second = jnp.where(lane < LAT, terms[2], terms[0] + terms[1] + terms[2])
    m_ref[:, 0:HD] = first.astype(BF16)
    m_ref[:, HD:LANES] = second.astype(BF16)


def owner_call(lat, weights, w_embed, w_out):
    return pl.pallas_call(
        owner_kernel,
        out_shape=(jax.ShapeDtypeStruct((MROW, LANES), BF16), jax.ShapeDtypeStruct((48, LANES), BF16)),
        compiler_params=pltpu.CompilerParams(vmem_limit_bytes=VMEM_LIMIT),
    )(lat, weights, w_embed, w_out)


def gather_kernel(piece_ref, m_ref, slots, own, send, recv, local_sem):
    s = lax.axis_index("sec")
    t = lax.axis_index("tp")
    z = s // 32
    x = (s // 8) % 4
    y = (s // 2) % 4
    c = s % 2
    u = x + c * (y - x)
    v = y + c * (x - y)
    u_stride = 8 - 6 * c
    v_stride = 2 + 6 * c
    sibling = {"sec": s + 1 - 2 * c}
    z_peer = {"sec": s + (1 - 2 * z) * 32}
    u_peers = [{"sec": s + ((u + k) % 4 - u) * u_stride} for k in range(1, 4)]
    v_peers = [{"sec": s + ((v + k) % 4 - v) * v_stride} for k in range(1, 4)]
    m_to = {"tp": s // 16, "sec": ((s % 16) * 4 + t + 1) % 64}
    back = (s + 63) % 64
    m_from = {"tp": back % 4, "sec": t * 16 + back // 4}
    around = [sibling, z_peer] + u_peers + v_peers
    barrier_with(around + [m_from], len(around) + 1)

    move = remote(m_ref, own.at[pl.ds(MROW, 48)], send.at[0], recv.at[0], m_to)
    move.start()
    own[0:MROW, :] = piece_ref[...]
    move.wait_recv()
    at = (v * 4 + u) * 2 + z
    keep = pltpu.make_async_copy(own, slots.at[c, at], local_sem)
    keep.start()
    z_copy = remote(own, slots.at[c, at], send.at[1], recv.at[1], z_peer)
    z_copy.start()
    keep.wait()
    z_copy.wait_recv()
    copies = [move, z_copy]
    pair = pl.ds((v * 4 + u) * 2, 2)
    u_copies = []
    for k in range(3):
        copy = remote(slots.at[c, pair], slots.at[c, pair], send.at[2 + k], recv.at[2 + k], u_peers[k])
        copy.start()
        u_copies.append(copy)
    for copy in u_copies:
        copy.wait_recv()
    group = pl.ds(v * 8, 8)
    v_copies = []
    for k in range(3):
        copy = remote(slots.at[c, group], slots.at[c, group], send.at[5 + k], recv.at[5 + k], v_peers[k])
        copy.start()
        v_copies.append(copy)
    cross = remote(slots.at[c, group], slots.at[c, group], send.at[8], recv.at[8], sibling)
    cross.start()
    crossing = [cross]
    for k in range(3):
        v_copies[k].wait_recv()
        came = pl.ds(((v + 3 - k) % 4) * 8, 8)
        cross = remote(slots.at[c, came], slots.at[c, came], send.at[9 + k], recv.at[9 + k], sibling)
        cross.start()
        crossing.append(cross)
    for copy in crossing:
        copy.wait_recv()
    for copy in copies + u_copies + v_copies + crossing:
        copy.wait_send()


def gather_call(piece, m_part):
    whole = pl.BlockSpec(memory_space=pltpu.VMEM)
    return pl.pallas_call(
        gather_kernel,
        out_shape=jax.ShapeDtypeStruct((2, 32, PIECE, LANES), BF16),
        in_specs=[whole] * 2,
        out_specs=pl.BlockSpec(memory_space=pl.ANY),
        scratch_shapes=[
            pltpu.VMEM((PIECE, LANES), BF16),
            pltpu.SemaphoreType.DMA((12,)),
            pltpu.SemaphoreType.DMA((12,)),
            pltpu.SemaphoreType.DMA,
        ],
        compiler_params=pltpu.CompilerParams(collective_id=1, has_side_effects=True, vmem_limit_bytes=VMEM_LIMIT),
    )(piece, m_part)


def merged(slots, at, rows):
    lane = lax.broadcasted_iota(jnp.int32, (rows.size, HD), 1)
    left = slots[0, at, rows, :]
    right = slots[1, at, rows, :]
    middle = jnp.where(lane < LAT, left[:, HD:].astype(F32), right[:, :HD].astype(F32)).astype(BF16)
    return jnp.concatenate([left[:, :HD], middle, right[:, HD:]], axis=1)


def chunk_of(slots, i, rows):
    return jnp.concatenate([merged(slots, 2 * i, rows), merged(slots, 2 * i + 1, rows)], axis=1)


def attend_kernel(
    slots, src_ref, w_ref, embed_ref, qg_ref, kg_ref, lat_ref, mixed_ref, latq, queries, accum, best
):
    chunk = 768
    lat_rows = pl.ds(0, LAT)
    stat_rows = pl.ds(STAT, 16)
    lane = lax.broadcasted_iota(jnp.int32, (1, chunk), 1)
    source = src_ref[...]

    latq[...] = jnp.zeros_like(latq)

    def pick(i, carry):
        v = i // 4
        u = i % 4
        base0 = u * 8 * ROWS + v * 2 * ROWS
        base1 = v * 8 * ROWS + u * 2 * ROWS + ROWS
        upper = lane // 384
        inner = lane - upper * 384
        token = inner + upper * (32 * ROWS) + jnp.where(inner < ROWS, base0, base1 - ROWS)
        hit = jnp.where(source == token, 1.0, 0.0).astype(BF16)
        latq[:, 0:LAT] += dot(hit, chunk_of(slots, i, lat_rows), NT)
        return carry

    lax.fori_loop(0, 16, pick, 0)
    rows = latq[...].astype(BF16)
    lat_ref[...] = rows[:, 0:LAT]
    embedded = dot(rows[:, 0:LAT], embed_ref[...], NN)
    center = embedded - jnp.mean(embedded, axis=1, keepdims=True)
    rstd = lax.rsqrt(jnp.mean(center * center, axis=1, keepdims=True) + EPS)
    unit = jnp.where(lax.broadcasted_iota(jnp.int32, (16, HD), 1) == LAT, 1.0, 0.0).astype(BF16)
    wide = lax.broadcasted_iota(jnp.int32, (ROWS, HD), 1)
    for h in range(HEADS):
        wq = w_ref[h * HD : (h + 1) * HD, :]
        wk = w_ref[WID + h * HD : WID + (h + 1) * HD, :]
        raw = rstd * dot(rows, wq, NT) + dot(unit, wq, NT)[0:1, :]
        q = raw * lax.rsqrt(jnp.mean(raw * raw, axis=1, keepdims=True) + EPS) * qg_ref[...]
        qk = q * kg_ref[...] * (LOG2E / HD**0.5)
        bound = jnp.sqrt(jnp.sum(qk * qk, axis=1, keepdims=True)) * (1.02 * HD**0.5)
        shift = jnp.maximum(bound - TOP, 0.0)
        high, low = split(qk)
        folded = dot(high.astype(BF16), wk, NN) + dot(low.astype(BF16), wk, NN)
        beta_high, beta_low = split(folded[:, LAT : LAT + 1])
        value = jnp.where(wide < LAT, folded, 0.0)
        value = jnp.where((wide == LAT) | (wide == LAT + 1), beta_high, value)
        value = jnp.where(wide == LAT + 2, beta_low, value)
        value = jnp.where(wide == LAT + 3, -shift, value)
        queries[h] = value.astype(BF16)

    index = lax.broadcasted_iota(jnp.int32, (16, chunk), 0)

    def operands(i):
        lat = chunk_of(slots, i, lat_rows).astype(F32)
        stat = chunk_of(slots, i, stat_rows).astype(F32)
        scale = stat[0:1, :] + stat[1:2, :]
        scaled = lat * scale
        ones = jnp.where(index == 0, 1.0, 0.0)
        vals = jnp.concatenate([scaled.astype(BF16), ones.astype(BF16)], axis=0)
        keys = []
        for h in range(HEADS):
            high = stat[2 + 2 * h : 3 + 2 * h, :]
            low = stat[3 + 2 * h : 4 + 2 * h, :]
            tail = jnp.where((index == 0) | (index == 2), high, 0.0)
            tail = jnp.where(index == 1, low, tail)
            tail = jnp.where(index == 3, 1.0, tail)
            keys.append(jnp.concatenate([(scaled * (high + low)).astype(BF16), tail.astype(BF16)], axis=0))
        return keys, vals

    accum[...] = jnp.zeros_like(accum)

    def attend(i, carry):
        keys, vals = operands(i)
        for h in range(HEADS):
            weights = jnp.exp2(dot(queries[h][:, 0:MROW], keys[h], NN)).astype(BF16)
            accum[h, :, 0:MROW] += dot(weights, vals, NT)
        return carry

    lax.fori_loop(0, 16, attend, 0)
    least = jnp.min(accum[:, :, LAT : LAT + 1])

    @pl.when(jnp.logical_not(least > 2.0**-60))
    def _():
        accum[...] = jnp.zeros_like(accum)
        best[...] = jnp.full_like(best, -1e30)

        def exact(i, carry):
            keys, vals = operands(i)
            for h in range(HEADS):
                scores = dot(queries[h][:, 0:MROW], keys[h], NN)
                old = best[h, :, 0:1]
                new = jnp.maximum(old, jnp.max(scores, axis=1, keepdims=True))
                weights = jnp.exp2(scores - new).astype(BF16)
                accum[h, :, 0:MROW] = accum[h, :, 0:MROW] * jnp.exp2(old - new) + dot(weights, vals, NT)
                best[h] = jnp.broadcast_to(new, (ROWS, HD))
            return carry

        lax.fori_loop(0, 16, exact, 0)

    parts = [accum[h] / accum[h, :, LAT : LAT + 1] for h in range(HEADS)]
    first = jnp.where(wide < LAT, parts[0], pltpu.roll(parts[1], LAT, 1))
    second = jnp.where(wide < LAT, parts[2], jnp.where(wide == LAT, 1.0, 0.0))
    mixed_ref[:, 0:HD] = first.astype(BF16)
    mixed_ref[:, HD:LANES] = second.astype(BF16)


def attend_call(slots, source, weights, w_embed, q_gain, k_gain):
    return pl.pallas_call(
        attend_kernel,
        out_shape=(jax.ShapeDtypeStruct((ROWS, LAT), BF16), jax.ShapeDtypeStruct((ROWS, LANES), BF16)),
        scratch_shapes=[
            pltpu.VMEM((ROWS, HD), F32),
            pltpu.VMEM((HEADS, ROWS, HD), BF16),
            pltpu.VMEM((HEADS, ROWS, HD), F32),
            pltpu.VMEM((HEADS, ROWS, HD), F32),
        ],
        compiler_params=pltpu.CompilerParams(vmem_limit_bytes=VMEM_LIMIT),
    )(slots, source, weights, w_embed, q_gain, k_gain)


def heads_kernel(mixed_ref, out_ref, held, send, recv):
    t = lax.axis_index("tp")
    peers = [{"tp": (t + k) % 4} for k in range(1, 4)]
    barrier_with(peers, 3)
    copies = []
    for k in range(3):
        copy = remote(mixed_ref, held.at[t], send.at[k], recv.at[k], peers[k])
        copy.start()
        copies.append(copy)
    held[t] = mixed_ref[...]
    for copy in copies:
        copy.wait_recv()
    out_ref[...] = held[...]
    for copy in copies:
        copy.wait_send()


def heads_call(mixed):
    whole = pl.BlockSpec(memory_space=pltpu.VMEM)
    return pl.pallas_call(
        heads_kernel,
        out_shape=jax.ShapeDtypeStruct((4, ROWS, LANES), BF16),
        in_specs=[whole],
        out_specs=whole,
        scratch_shapes=[
            pltpu.VMEM((4, ROWS, LANES), BF16),
            pltpu.SemaphoreType.DMA((3,)),
            pltpu.SemaphoreType.DMA((3,)),
        ],
        compiler_params=pltpu.CompilerParams(collective_id=2, has_side_effects=True, vmem_limit_bytes=VMEM_LIMIT),
    )(mixed)


def project_kernel(mixed_ref, slots, lat_ref, embed_ref, gate_ref, out_ref, assembled):
    for place in range(64):
        c, rest = place // 32, place % 32
        v, u, z = rest // 8, (rest // 2) % 4, rest % 2
        x, y = (u, v) if c == 0 else (v, u)
        back = (z * 32 + x * 8 + y * 2 + c + 63) % 64
        assembled[back % 4, (back // 4) * 48 : (back // 4) * 48 + 48, :] = slots[c, rest, MROW:PIECE, :]
    total = dot(mixed_ref[0], assembled[0], NT)
    for k in range(1, 4):
        total += dot(mixed_ref[k], assembled[k], NT)
    embedded = dot(lat_ref[...], embed_ref[...], NN)
    out_ref[...] = (embedded + gate_ref[...] * total).astype(BF16)


def project_call(mixed, slots, latents, embed_part, gate_part):
    return pl.pallas_call(
        project_kernel,
        out_shape=jax.ShapeDtypeStruct((ROWS, 768), BF16),
        scratch_shapes=[pltpu.VMEM((4, 768, LANES), BF16)],
        compiler_params=pltpu.CompilerParams(vmem_limit_bytes=VMEM_LIMIT),
    )(mixed, slots, latents, embed_part, gate_part)


def per_device(
    pixels, w_encode, w_latent, source_row, w_embed, mod_shift, mod_scale, gate, q_gain, k_gain, w_qkv, w_out
):
    s = lax.axis_index("sec")
    t = lax.axis_index("tp")
    hidden = jax.nn.silu(jnp.dot(pixels, w_encode, preferred_element_type=F32)).astype(BF16)
    part = lax.dot_general(w_latent, hidden, (((0,), (1,)), ((), ())), preferred_element_type=F32)
    zero = jnp.zeros((LAT, LANES), BF16)
    lat_part = lax.dynamic_update_slice(zero, part.astype(BF16), (0, LAT * (s % 2)))

    wide = w_embed.astype(F32)
    columns = lax.dynamic_slice_in_dim(wide, s * 48, 48, 1) - jnp.mean(wide, axis=1, keepdims=True)
    columns = columns * lax.dynamic_slice_in_dim(mod_scale, s * 48, 48, 0)[None, :]
    shift = lax.dynamic_slice_in_dim(mod_shift, s * 48, 48, 0)[None, :]
    left = jnp.concatenate([columns, shift, jnp.zeros((HD - LAT - 1, 48), F32)], axis=0)
    w_part = jnp.einsum("idc,fd->icf", w_qkv.astype(F32), left, precision=lax.Precision.HIGHEST)
    w_part = w_part.reshape(3 * WID, HD).astype(BF16)

    lat, weights = reduce_call(lat_part, w_part)
    piece, m_part = owner_call(lat, weights, w_embed, w_out)
    slots = gather_call(piece, m_part)
    latents, mixed = attend_call(
        slots, source_row.reshape(ROWS, 1), weights, w_embed, q_gain.reshape(1, HD), k_gain.reshape(1, HD)
    )
    every = heads_call(mixed)
    embed_part = lax.dynamic_slice_in_dim(w_embed, t * 768, 768, 1)
    gate_part = lax.dynamic_slice_in_dim(gate, t * 768, 768, 0).reshape(1, 768)
    return latents, project_call(every, slots, latents, embed_part, gate_part)


def solution(mesh):
    placed = (
        P("sec", None), P(None, "tp"), P("tp", None), P("sec"), P(), P(), P(), P(), P(), P(),
        P(None, "sec", "tp"), P("tp", "sec"),
    )
    return jax.shard_map(
        per_device, mesh=mesh, in_specs=placed, out_specs=(P("sec", None), P("sec", "tp")), check_vma=False
    )
```

```python
import jax
import jax.numpy as jnp
from jax import lax
from jax.experimental import pallas as pl
from jax.experimental.pallas import tpu as pltpu
from jax.sharding import PartitionSpec as P

MESH = pl.DeviceIdType.MESH
HD = 128
HEADS = 3
LAT = 64
ROWS = 192
LANES = 256
WID = HEADS * HD
DIM = 3072
FEAT = 80
CHUNK = 768
CHUNKS = 16
STEP = 8
MCOLS = 48
QUARTER = 768
PARTS = 4
DEPTH = DIM // PARTS
F32 = jnp.float32
BF16 = jnp.bfloat16
NT = (((1,), (1,)), ((), ()))
NN = (((1,), (0,)), ((), ()))
TN = (((0,), (0,)), ((), ()))
EPS = 1e-6
LOG2E = 1.4426950408889634
VMEM_LIMIT = 58 * 1024 * 1024


def dot(a, b, dims):
    return lax.dot_general(a, b, dims, preferred_element_type=F32)


def split(value):
    high = value.astype(BF16).astype(F32)
    return high, value - high


def kernel(
    pixels, w_encode, w_latent, source, w_embed, mod_shift, mod_scale, gate, q_gain, k_gain, w_qkv, w_out,
    lat_out, block_out,
    pix_v, enc_v, wlat_v, src_v, emb_v, shift_v, scale_v, gate_v, qg_v, kg_v, wqkv_v, wout_v,
    wide, wp, lat_in, core_in, half, x_in, y_in, weights,
    slots, m_in, m_slots, latq, square, queries, keys, vals, s_even, s_odd, running, top, accum,
    first, second, assembled,
    load, send, recv,
):
    s = lax.axis_index("sec")
    t = lax.axis_index("tp")
    z = s // 32
    x = (s // 8) % 4
    y = (s // 2) % 4
    c = s % 2
    u = x + c * (y - x)
    v = y + c * (x - y)
    b = z * 4 + y
    at = (v * 4 + u) * 2 + z
    sibling = {"sec": s + 1 - 2 * c}
    tp_peers = [{"tp": (t + k) % 4} for k in range(1, 4)]
    x_at = [(x + k) % 4 for k in range(1, 4)]
    x_peers = [{"sec": s + (xx - x) * 8} for xx in x_at]
    b_at = [(b + k) % 8 for k in range(1, 8)]
    b_peers = [{"sec": (bb // 4) * 32 + x * 8 + (bb % 4) * 2 + c} for bb in b_at]
    z_peer = {"sec": s + (1 - 2 * z) * 32}
    u_peers = [{"sec": s + ((u + k) % 4 - u) * (8 - 6 * c)} for k in range(1, 4)]
    v_peers = [{"sec": s + ((v + k) % 4 - v) * (2 + 6 * c)} for k in range(1, 4)]
    m_to = {"tp": s // 16, "sec": ((s % 16) * 4 + t + 1) % 64}
    back = (s + 63) % 64
    m_from = {"tp": back % 4, "sec": t * 16 + back // 4}

    sent = []
    used = [0]

    def push(src, dst, device):
        i = used[0]
        used[0] += 1
        copy = pltpu.make_async_remote_copy(
            src_ref=src, dst_ref=dst, send_sem=send.at[i], recv_sem=recv.at[i], device_id=device, device_id_type=MESH
        )
        copy.start()
        sent.append(copy)
        return copy

    loads = [0]

    def fetch(src, dst):
        copy = pltpu.make_async_copy(src, dst, load.at[loads[0]])
        loads[0] += 1
        copy.start()
        return copy

    early = [fetch(w_embed, emb_v), fetch(w_qkv, wqkv_v), fetch(mod_scale, scale_v), fetch(mod_shift, shift_v)]
    parts = []
    for k in range(PARTS):
        depth = pl.ds(k * DEPTH, DEPTH)
        parts.append((fetch(pixels.at[:, depth], pix_v.at[k]), fetch(w_encode.at[depth], enc_v.at[k])))
    wlat_load = fetch(w_latent, wlat_v)
    late = [
        fetch(source, src_v), fetch(gate, gate_v), fetch(q_gain, qg_v), fetch(k_gain, kg_v), fetch(w_out, wout_v)
    ]

    barrier = pltpu.get_barrier_semaphore()
    greet = tp_peers + [sibling] + x_peers + b_peers + [m_from]
    for device in greet:
        pl.semaphore_signal(barrier, inc=1, device_id=device, device_id_type=MESH)

    for copy in early:
        copy.wait()
    block = (3 * s) // 8 - s // 62
    base = pl.ds(pl.multiple_of(block * HD, HD), LANES)
    mean = jnp.mean(emb_v[...].astype(F32), axis=1, keepdims=True)
    wide[0:LAT, :] = (emb_v[:, base].astype(F32) - mean) * scale_v[:, base]
    wide[LAT:HD, :] = jnp.where(
        lax.broadcasted_iota(jnp.int32, (LAT, LANES), 0) == 0, jnp.broadcast_to(shift_v[:, base], (LAT, LANES)), 0.0
    )
    offset = s * MCOLS - block * HD
    turned = pltpu.roll(wide[...], (LANES - offset) % LANES, 1)[:, 0:HD].T
    high, low = split(turned[0:MCOLS, :])
    high, low = high.astype(BF16), low.astype(BF16)
    for i in range(3):
        wp[i * WID : (i + 1) * WID, :] = (dot(wqkv_v[i], high, TN) + dot(wqkv_v[i], low, TN)).astype(BF16)

    pl.semaphore_wait(barrier, len(greet))
    mine = pl.ds(pl.multiple_of(c * 576, 576), 576)
    other = pl.ds(pl.multiple_of((1 - c) * 576, 576), 576)
    w_core = push(wp.at[other], core_in, sibling)

    total = jnp.zeros((ROWS, 512), F32)
    for k in range(PARTS):
        parts[k][0].wait()
        parts[k][1].wait()
        total += dot(pix_v[k], enc_v[k], NN)
    hidden = jax.nn.silu(total).astype(BF16)
    wlat_load.wait()
    wide[...] = jnp.zeros_like(wide)
    wide[0:LAT, 0:ROWS] = dot(wlat_v[...], hidden, NT)
    lat_in[t] = pltpu.roll(wide[0:LAT, :], LAT * c, 1).astype(BF16)
    lat_tp = [push(lat_in.at[t], lat_in.at[t], device) for device in tp_peers]

    w_core.wait_recv()
    half[...] = (wp[mine, :].astype(F32) + core_in[...].astype(F32)).astype(BF16)
    w_x = []
    for k in range(3):
        w_x.append(push(half.at[pl.ds(pl.multiple_of(x_at[k] * 144, 144), 144)], x_in.at[x], x_peers[k]))
    x_in[x] = half[pl.ds(pl.multiple_of(x * 144, 144), 144), :]

    for copy in lat_tp:
        copy.wait_recv()
    summed = lat_in[0].astype(F32)
    for k in range(1, 4):
        summed += lat_in[k].astype(F32)
    lat = summed.astype(BF16)
    embedded = dot(emb_v[...], lat, TN)
    center = embedded - jnp.mean(embedded, axis=0, keepdims=True)
    rstd = lax.rsqrt(jnp.mean(center * center, axis=0, keepdims=True) + EPS)
    rstd = jnp.broadcast_to(rstd, (LAT, LANES))
    row = lax.broadcasted_iota(jnp.int32, (LAT, LANES), 0)
    lane = lax.broadcasted_iota(jnp.int32, (LAT, LANES), 1)
    high, low = split(rstd)
    piece = lat.astype(F32)
    spare = (lane >= ROWS * (1 - c)) & (lane < ROWS * (1 - c) + LAT)
    for k in range(3):
        turn = (ROWS * (1 - c) - LAT * c - LAT * k + 2 * LANES) % LANES
        piece = jnp.where(spare & (row == k), pltpu.roll(high, turn, 1), piece)
        piece = jnp.where(spare & (row == k + 3), pltpu.roll(low, turn, 1), piece)
    slots[c, at] = piece.astype(BF16)
    lat_z = push(slots.at[c, at], slots.at[c, at], z_peer)

    for copy in w_x:
        copy.wait_recv()
    added = x_in[0].astype(F32)
    for k in range(1, 4):
        added += x_in[k].astype(F32)
    y_in[b] = added.astype(BF16)
    w_b = [push(y_in.at[b], y_in.at[b], device) for device in b_peers]

    lat_z.wait_recv()
    pair = pl.ds((v * 4 + u) * 2, 2)
    lat_u = [push(slots.at[c, pair], slots.at[c, pair], device) for device in u_peers]

    for copy in w_b:
        copy.wait_recv()
    added = y_in[0].astype(F32)
    for k in range(1, 8):
        added += y_in[k].astype(F32)
    place = pl.ds(pl.multiple_of(c * 576 + x * 144, 144), 144)
    weights[place, :] = added.astype(BF16)
    w_g = [push(weights.at[place], weights.at[place], device) for device in x_peers]

    for copy in lat_u:
        copy.wait_recv()
    group = pl.ds(v * 8, 8)
    lat_v = [push(slots.at[c, group], slots.at[c, group], device) for device in v_peers]
    lat_c = [push(slots.at[c, group], slots.at[c, group], sibling)]

    for copy in w_g:
        copy.wait_recv()
    w_last = push(weights.at[mine], weights.at[mine], sibling)
    for copy in late:
        copy.wait()
    square[...] = jnp.zeros_like(square)
    square[:, 0:ROWS] = jnp.broadcast_to(src_v[...].astype(F32), (HD, ROWS))
    origin = square[...].T[0:ROWS, 0:1].astype(jnp.int32)
    latq[...] = jnp.zeros_like(latq)
    w_last.wait_recv()

    wide_m = lax.broadcasted_iota(jnp.int32, (MCOLS, HD), 1)
    terms = [
        dot(wout_v[:, h * HD : (h + 1) * HD], weights[2 * WID + h * HD : 2 * WID + (h + 1) * HD, :], NN)
        for h in range(HEADS)
    ]
    m_in[0, :, 0:HD] = jnp.where(wide_m < LAT, terms[0], pltpu.roll(terms[1], LAT, 1)).astype(BF16)
    m_in[0, :, HD:LANES] = jnp.where(wide_m < LAT, terms[2], terms[0] + terms[1] + terms[2]).astype(BF16)
    m_move = push(m_in.at[0], m_in.at[1], m_to)

    lane_t = lax.broadcasted_iota(jnp.int32, (1, HD), 1)
    lane_c = lax.broadcasted_iota(jnp.int32, (1, CHUNK), 1)
    tail_row = lax.broadcasted_iota(jnp.int32, (16, CHUNK), 0)

    def prepare(k, g0, g1):
        def one(i, carry):
            lats, scales = [], []
            for zz in range(2):
                left = slots[0, g0 * 8 + 2 * i + zz]
                right = slots[1, g1 * 8 + 2 * i + zz]
                middle = jnp.where(lane_t < LAT, left[:, HD:].astype(F32), right[:, :HD].astype(F32))
                lats += [left[:, :HD].astype(F32), middle, right[:, HD:].astype(F32)]
                sl = left[0:16, HD:].astype(F32)
                sr = right[0:16, :HD].astype(F32)
                sl = sl[0:3] + sl[3:6]
                sr = sr[0:3] + sr[3:6]
                tl = pltpu.roll(sl, LAT, 1)
                tr = pltpu.roll(sr, LAT, 1)
                scales += [
                    jnp.where(lane_t < LAT, tl[0:1], sl[1:2]),
                    jnp.where(lane_t < LAT, tl[2:3], tr[0:1]),
                    jnp.where(lane_t < LAT, sr[1:2], tr[2:3]),
                ]
            lat_c32 = jnp.concatenate(lats, axis=1)
            scale_row = jnp.concatenate(scales, axis=1)
            lat_cb = lat_c32.astype(BF16)
            upper = lane_c // 384
            inner = lane_c - upper * 384
            base0 = i * 8 * ROWS + g0 * 2 * ROWS
            base1 = g1 * 8 * ROWS + i * 2 * ROWS + ROWS
            token = inner + upper * (32 * ROWS) + jnp.where(inner < ROWS, base0, base1 - ROWS)
            hit = jnp.where(origin == token, 1.0, 0.0).astype(BF16)
            latq[0:ROWS, 0:LAT] += dot(hit, lat_cb, NT)
            n = 4 * k + i
            scaled = lat_c32 * scale_row
            vals[n, 0:LAT, :] = scaled.astype(BF16)
            vals[n, LAT:FEAT, :] = jnp.where(tail_row == 0, 1.0, 0.0).astype(BF16)
            for h in range(HEADS):
                wk = weights[WID + h * HD : WID + (h + 1) * HD, :]
                raw = dot(wk[:, 0:LAT], lat_cb, NN) * scale_row + wk[:, LAT : LAT + 1].astype(F32)
                inv = lax.rsqrt(jnp.mean(raw * raw, axis=0, keepdims=True) + EPS)
                ih, il = split(inv)
                tail = jnp.where((tail_row == 0) | (tail_row == 2), ih, 0.0)
                tail = jnp.where(tail_row == 1, il, tail)
                keys[h, n, 0:LAT, :] = (scaled * inv).astype(BF16)
                keys[h, n, LAT:FEAT, :] = tail.astype(BF16)
            return carry

        lax.fori_loop(0, 4, one, 0)

    for k in range(4):
        if k:
            lat_v[k - 1].wait_recv()
            came = pl.ds(((v + 4 - k) % 4) * 8, 8)
            lat_c.append(push(slots.at[c, came], slots.at[c, came], sibling))
        lat_c[k].wait_recv()
        prepare(k, (y + 4 - k) % 4, (x + 4 - k) % 4)
        if k == 1:
            m_move.wait_recv()
            m_slots[c, at] = m_in[1]
            m_z = push(m_slots.at[c, at], m_slots.at[c, at], z_peer)
    m_z.wait_recv()
    m_u = [push(m_slots.at[c, pair], m_slots.at[c, pair], device) for device in u_peers]

    rows = latq[0:ROWS, :].astype(BF16)
    lat_out[...] = latq[...].T[0:LAT, 0:ROWS].astype(BF16)
    embedded = dot(rows[:, 0:LAT], emb_v[...], NN)
    center = embedded - jnp.mean(embedded, axis=1, keepdims=True)
    rstd = lax.rsqrt(jnp.mean(center * center, axis=1, keepdims=True) + EPS)
    unit = jnp.where(lax.broadcasted_iota(jnp.int32, (16, HD), 1) == LAT, 1.0, 0.0).astype(BF16)
    lane_q = lax.broadcasted_iota(jnp.int32, (ROWS, HD), 1)
    for h in range(HEADS):
        wq = weights[h * HD : (h + 1) * HD, :]
        wk = weights[WID + h * HD : WID + (h + 1) * HD, :]
        raw = rstd * dot(rows, wq, NT) + dot(unit, wq, NT)[0:1, :]
        q = raw * lax.rsqrt(jnp.mean(raw * raw, axis=1, keepdims=True) + EPS) * qg_v[...]
        high, low = split(q * kg_v[...] * (LOG2E / HD**0.5))
        folded = dot(high.astype(BF16), wk, NN) + dot(low.astype(BF16), wk, NN)
        bias_high, bias_low = split(folded[:, LAT : LAT + 1])
        value = jnp.where(lane_q < LAT, folded, 0.0)
        value = jnp.where((lane_q == LAT) | (lane_q == LAT + 1), bias_high, value)
        value = jnp.where(lane_q == LAT + 2, bias_low, value)
        queries[h] = value.astype(BF16)

    scores = [s_even, s_odd]
    running[...] = jnp.full_like(running, -jnp.inf)
    accum[...] = jnp.zeros_like(accum)

    def score(i, h):
        most = running[h]
        for j in range(STEP):
            n = i * STEP + j
            part = dot(queries[h][:, 0:FEAT], keys[h, n], NN)
            scores[h % 2][n] = part
            for k in range(CHUNK // HD):
                most = jnp.maximum(most, part[:, k * HD : (k + 1) * HD])
        running[h] = most

    def weigh(i, h):
        most = top[h]
        added = accum[h, :, 0:FEAT]
        for j in range(STEP):
            n = i * STEP + j
            w = jnp.concatenate(
                [jnp.exp2(scores[h % 2][n, :, k * HD : (k + 1) * HD] - most).astype(BF16) for k in range(CHUNK // HD)],
                axis=1,
            )
            added += dot(w, vals[n], NT)
        accum[h, :, 0:FEAT] = added

    def start(i, carry):
        score(i, 0)
        return carry

    lax.fori_loop(0, CHUNKS // STEP, start, 0)
    for copy in m_u:
        copy.wait_recv()
    m_v = [push(m_slots.at[c, group], m_slots.at[c, group], device) for device in v_peers]
    m_c = [push(m_slots.at[c, group], m_slots.at[c, group], sibling)]
    mixed = []
    for h in range(HEADS):
        top[h] = jnp.broadcast_to(jnp.max(running[h], axis=1, keepdims=True), (ROWS, HD))

        def both(i, carry):
            weigh(i, h)
            if h + 1 < HEADS:
                score(i, h + 1)
            return carry

        lax.fori_loop(0, CHUNKS // STEP, both, 0)
        mixed.append(accum[h] / accum[h, :, LAT : LAT + 1])
        if h == 1:
            first[t] = jnp.where(lane_q < LAT, mixed[0], pltpu.roll(mixed[1], LAT, 1)).astype(BF16)
            o_first = [push(first.at[t], first.at[t], device) for device in tp_peers]
            for k in range(1, 4):
                m_v[k - 1].wait_recv()
                came = pl.ds(((v + 4 - k) % 4) * 8, 8)
                m_c.append(push(m_slots.at[c, came], m_slots.at[c, came], sibling))
    lower = pltpu.roll(mixed[2][ROWS // 2 :, :], LAT, 1)
    second[t] = jnp.where(lane_q[0 : ROWS // 2] < LAT, mixed[2][0 : ROWS // 2, :], lower).astype(BF16)
    o_second = [push(second.at[t], second.at[t], device) for device in tp_peers]

    for copy in m_c:
        copy.wait_recv()
    for slot in range(64):
        cc, rest = slot // 32, slot % 32
        vv, uu, zz = rest // 8, (rest // 2) % 4, rest % 2
        xx, yy = (uu, vv) if cc == 0 else (vv, uu)
        origin_at = (zz * 32 + xx * 8 + yy * 2 + cc + 63) % 64
        assembled[origin_at % 4, pl.ds((origin_at // 4) * MCOLS, MCOLS), :] = m_slots[cc, rest]
    quarter = pl.ds(pl.multiple_of(t * QUARTER, QUARTER), QUARTER)
    embedded = dot(rows[:, 0:LAT], emb_v[:, quarter], NN)
    for copy in o_first:
        copy.wait_recv()
    total = dot(first[0], assembled[0, :, 0:HD], NT)
    for k in range(1, 4):
        total += dot(first[k], assembled[k, :, 0:HD], NT)
    for copy in o_second:
        copy.wait_recv()
    one = jnp.where(lane_q == LAT, 1.0, 0.0)
    for k in range(4):
        packed = second[k].astype(F32)
        whole = jnp.concatenate([packed, pltpu.roll(packed, LAT, 1)], axis=0)
        whole = jnp.where(lane_q < LAT, whole, one).astype(BF16)
        total += dot(whole, assembled[k, :, HD:LANES], NT)
    block_out[...] = (embedded + gate_v[:, quarter] * total).astype(BF16)
    for copy in sent:
        copy.wait_send()


COPIES = 47
LOADS = 18


def per_device(
    pixels, w_encode, w_latent, source_row, w_embed, mod_shift, mod_scale, gate, q_gain, k_gain, w_qkv, w_out
):
    operands = (
        pixels, w_encode, w_latent.T, source_row.reshape(1, ROWS), w_embed, mod_shift.reshape(1, DIM),
        mod_scale.reshape(1, DIM), gate.reshape(1, DIM), q_gain.reshape(1, HD), k_gain.reshape(1, HD), w_qkv, w_out.T,
    )
    vmem = pltpu.VMEM
    scratch = [
        vmem((PARTS, ROWS, DEPTH), BF16),
        vmem((PARTS, DEPTH, 512), BF16),
        vmem((LAT, 512), BF16),
        vmem((1, ROWS), jnp.int32),
        vmem((LAT, DIM), BF16),
        vmem((1, DIM), F32),
        vmem((1, DIM), F32),
        vmem((1, DIM), F32),
        vmem((1, HD), F32),
        vmem((1, HD), F32),
        vmem((3, MCOLS, WID), BF16),
        vmem((MCOLS, WID), BF16),
        vmem((HD, LANES), F32),
        vmem((3 * WID, HD), BF16),
        vmem((4, LAT, LANES), BF16),
        vmem((576, HD), BF16),
        vmem((576, HD), BF16),
        vmem((4, 144, HD), BF16),
        vmem((8, 144, HD), BF16),
        vmem((3 * WID, HD), BF16),
        vmem((2, 32, LAT, LANES), BF16),
        vmem((2, MCOLS, LANES), BF16),
        vmem((2, 32, MCOLS, LANES), BF16),
        vmem((LANES, HD), F32),
        vmem((HD, LANES), F32),
        vmem((HEADS, ROWS, HD), BF16),
        vmem((HEADS, CHUNKS, FEAT, CHUNK), BF16),
        vmem((CHUNKS, FEAT, CHUNK), BF16),
        vmem((CHUNKS, ROWS, CHUNK), F32),
        vmem((CHUNKS, ROWS, CHUNK), F32),
        vmem((HEADS, ROWS, HD), F32),
        vmem((HEADS, ROWS, HD), F32),
        vmem((HEADS, ROWS, HD), F32),
        vmem((4, ROWS, HD), BF16),
        vmem((4, ROWS // 2, HD), BF16),
        vmem((4, QUARTER, LANES), BF16),
        pltpu.SemaphoreType.DMA((LOADS,)),
        pltpu.SemaphoreType.DMA((COPIES,)),
        pltpu.SemaphoreType.DMA((COPIES,)),
    ]
    lat, out = pl.pallas_call(
        kernel,
        out_shape=(jax.ShapeDtypeStruct((LAT, ROWS), BF16), jax.ShapeDtypeStruct((ROWS, QUARTER), BF16)),
        in_specs=[pl.BlockSpec(memory_space=pl.ANY)] * len(operands),
        out_specs=(pl.BlockSpec(memory_space=pltpu.VMEM), pl.BlockSpec(memory_space=pltpu.VMEM)),
        scratch_shapes=scratch,
        compiler_params=pltpu.CompilerParams(collective_id=0, has_side_effects=True, vmem_limit_bytes=VMEM_LIMIT),
    )(*operands)
    return lat.T, out


def solution(mesh):
    placed = (
        P("sec", None), P(None, "tp"), P("tp", None), P("sec"), P(), P(), P(), P(), P(), P(),
        P(None, "sec", "tp"), P("tp", "sec"),
    )
    return jax.shard_map(
        per_device, mesh=mesh, in_specs=placed, out_specs=(P("sec", None), P("sec", "tp")), check_vma=False
    )
```

```python
import jax
import jax.numpy as jnp
from jax import lax
from jax.experimental import pallas as pl
from jax.experimental.pallas import tpu as pltpu
from jax.sharding import PartitionSpec as P

MESH = pl.DeviceIdType.MESH
HD = 128
HEADS = 3
LAT = 64
ROWS = 192
LANES = 256
WID = HEADS * HD
DIM = 3072
FEAT = 80
CHUNK = 768
CHUNKS = 16
MCOLS = 48
QUARTER = 768
PARTS = 4
DEPTH = DIM // PARTS
F32 = jnp.float32
BF16 = jnp.bfloat16
NT = (((1,), (1,)), ((), ()))
NN = (((1,), (0,)), ((), ()))
TN = (((0,), (0,)), ((), ()))
EPS = 1e-6
LOG2E = 1.4426950408889634
VMEM_LIMIT = 58 * 1024 * 1024


def dot(a, b, dims):
    return lax.dot_general(a, b, dims, preferred_element_type=F32)


def split(value):
    high = value.astype(BF16).astype(F32)
    return high, value - high


def kernel(
    pixels, w_encode, w_latent, source, w_embed, mod_shift, mod_scale, gate, q_gain, k_gain, w_qkv, w_out,
    lat_out, block_out,
    pix_v, enc_v, wlat_v, src_v, emb_v, shift_v, scale_v, gate_v, qg_v, kg_v, wqkv_v, wout_v,
    wide, centred, centred_t, wp, lat_in, core_in, half, x_in, y_in, weights,
    slots, m_in, m_slots, latq, square, queries, keys, vals, s_even, s_odd, running, top, accum,
    first, second, assembled,
    load, send, recv,
):
    s = lax.axis_index("sec")
    t = lax.axis_index("tp")
    z = s // 32
    x = (s // 8) % 4
    y = (s // 2) % 4
    c = s % 2
    u = x + c * (y - x)
    v = y + c * (x - y)
    b = z * 4 + y
    at = (v * 4 + u) * 2 + z
    sibling = {"sec": s + 1 - 2 * c}
    tp_peers = [{"tp": (t + k) % 4} for k in range(1, 4)]
    x_at = [(x + k) % 4 for k in range(1, 4)]
    x_peers = [{"sec": s + (xx - x) * 8} for xx in x_at]
    b_at = [(b + k) % 8 for k in range(1, 8)]
    b_peers = [{"sec": (bb // 4) * 32 + x * 8 + (bb % 4) * 2 + c} for bb in b_at]
    z_peer = {"sec": s + (1 - 2 * z) * 32}
    u_peers = [{"sec": s + ((u + k) % 4 - u) * (8 - 6 * c)} for k in range(1, 4)]
    v_peers = [{"sec": s + ((v + k) % 4 - v) * (2 + 6 * c)} for k in range(1, 4)]
    m_to = {"tp": s // 16, "sec": ((s % 16) * 4 + t + 1) % 64}
    back = (s + 63) % 64
    m_from = {"tp": back % 4, "sec": t * 16 + back // 4}

    sent = []
    used = [0]

    def push(src, dst, device):
        i = used[0]
        used[0] += 1
        copy = pltpu.make_async_remote_copy(
            src_ref=src, dst_ref=dst, send_sem=send.at[i], recv_sem=recv.at[i], device_id=device, device_id_type=MESH
        )
        copy.start()
        sent.append(copy)
        return copy

    loads = [0]

    def fetch(src, dst):
        copy = pltpu.make_async_copy(src, dst, load.at[loads[0]])
        loads[0] += 1
        copy.start()
        return copy

    early = [fetch(w_embed, emb_v), fetch(w_qkv, wqkv_v), fetch(mod_scale, scale_v), fetch(mod_shift, shift_v)]
    parts = []
    for k in range(PARTS):
        depth = pl.ds(k * DEPTH, DEPTH)
        parts.append((fetch(pixels.at[:, depth], pix_v.at[k]), fetch(w_encode.at[depth], enc_v.at[k])))
    wlat_load = fetch(w_latent, wlat_v)
    late = [
        fetch(source, src_v), fetch(gate, gate_v), fetch(q_gain, qg_v), fetch(k_gain, kg_v), fetch(w_out, wout_v)
    ]

    barrier = pltpu.get_barrier_semaphore()
    greet = tp_peers + [sibling] + x_peers + b_peers + [m_from]
    for device in greet:
        pl.semaphore_signal(barrier, inc=1, device_id=device, device_id_type=MESH)

    for copy in early:
        copy.wait()
    block = (3 * s) // 8 - s // 62
    base = pl.ds(pl.multiple_of(block * HD, HD), LANES)
    mean = jnp.mean(emb_v[...].astype(F32), axis=1, keepdims=True)
    wide[0:LAT, :] = (emb_v[:, base].astype(F32) - mean) * scale_v[:, base]
    wide[LAT:HD, :] = jnp.where(
        lax.broadcasted_iota(jnp.int32, (LAT, LANES), 0) < 2, jnp.broadcast_to(shift_v[:, base], (LAT, LANES)), 0.0
    )
    offset = s * MCOLS - block * HD
    turned = pltpu.roll(wide[...], (LANES - offset) % LANES, 1)[:, 0:HD].T
    high, low = split(turned[0:MCOLS, :])
    high, low = high.astype(BF16), low.astype(BF16)
    for i in range(3):
        wp[i * WID : (i + 1) * WID, :] = (dot(wqkv_v[i], high, TN) + dot(wqkv_v[i], low, TN)).astype(BF16)

    total = jnp.zeros((ROWS, 512), F32)
    for k in range(PARTS):
        parts[k][0].wait()
        parts[k][1].wait()
        total += dot(pix_v[k], enc_v[k], NN)
    hidden = jax.nn.silu(total).astype(BF16)
    wlat_load.wait()
    wide[...] = jnp.zeros_like(wide)
    wide[0:LAT, 0:ROWS] = dot(wlat_v[...], hidden, NT)
    lat_in[t] = pltpu.roll(wide[0:LAT, :], LAT * c, 1).astype(BF16)

    pl.semaphore_wait(barrier, len(greet))
    mine = pl.ds(pl.multiple_of(c * 576, 576), 576)
    other = pl.ds(pl.multiple_of((1 - c) * 576, 576), 576)
    w_core = push(wp.at[other], core_in, sibling)
    lat_tp = [push(lat_in.at[t], lat_in.at[t], device) for device in tp_peers]

    high, low = split(emb_v[...].astype(F32) - mean)
    both_terms = jnp.concatenate([high, low], axis=0)
    centred[...] = both_terms.astype(BF16)
    centred_t[...] = both_terms.T.astype(BF16)

    w_core.wait_recv()
    half[...] = (wp[mine, :].astype(F32) + core_in[...].astype(F32)).astype(BF16)
    w_x = []
    for k in range(3):
        w_x.append(push(half.at[pl.ds(pl.multiple_of(x_at[k] * 144, 144), 144)], x_in.at[x], x_peers[k]))
    x_in[x] = half[pl.ds(pl.multiple_of(x * 144, 144), 144), :]

    for copy in late:
        copy.wait()
    square[...] = jnp.zeros_like(square)
    square[:, 0:ROWS] = jnp.broadcast_to(src_v[...].astype(F32), (HD, ROWS))
    origin = square[...].T[0:ROWS, 0:1].astype(jnp.int32)
    latq[...] = jnp.zeros_like(latq)

    for copy in lat_tp:
        copy.wait_recv()
    summed = lat_in[0].astype(F32)
    for k in range(1, 4):
        summed += lat_in[k].astype(F32)
    lat = summed.astype(BF16)
    twice = jnp.concatenate([lat, lat], axis=0)
    squares = jnp.zeros((1, LANES), F32)
    for k in range(PARTS):
        center = dot(centred_t[k * DEPTH : (k + 1) * DEPTH, :], twice, NN)
        squares += jnp.sum(center * center, axis=0, keepdims=True)
    rstd = lax.rsqrt(squares * (1.0 / DIM) + EPS)
    rstd = jnp.broadcast_to(rstd, (LAT, LANES))
    row = lax.broadcasted_iota(jnp.int32, (LAT, LANES), 0)
    lane = lax.broadcasted_iota(jnp.int32, (LAT, LANES), 1)
    high, low = split(rstd)
    piece = lat.astype(F32)
    spare = (lane >= ROWS * (1 - c)) & (lane < ROWS * (1 - c) + LAT)
    for k in range(3):
        turn = (ROWS * (1 - c) - LAT * c - LAT * k + 2 * LANES) % LANES
        piece = jnp.where(spare & (row == k), pltpu.roll(high, turn, 1), piece)
        piece = jnp.where(spare & (row == k + 3), pltpu.roll(low, turn, 1), piece)
    slots[c, at] = piece.astype(BF16)
    lat_z = push(slots.at[c, at], slots.at[c, at], z_peer)

    for copy in w_x:
        copy.wait_recv()
    added = x_in[0].astype(F32)
    for k in range(1, 4):
        added += x_in[k].astype(F32)
    y_in[b] = added.astype(BF16)
    w_b = [push(y_in.at[b], y_in.at[b], device) for device in b_peers]

    lat_z.wait_recv()
    pair = pl.ds((v * 4 + u) * 2, 2)
    lat_u = [push(slots.at[c, pair], slots.at[c, pair], device) for device in u_peers]

    for copy in w_b:
        copy.wait_recv()
    added = y_in[0].astype(F32)
    for k in range(1, 8):
        added += y_in[k].astype(F32)
    place = pl.ds(pl.multiple_of(c * 576 + x * 144, 144), 144)
    weights[place, :] = added.astype(BF16)
    w_g = [push(weights.at[place], weights.at[place], device) for device in x_peers]

    for copy in lat_u:
        copy.wait_recv()
    group = pl.ds(v * 8, 8)
    right, left = v_peers[0], v_peers[2]

    def halves(which):
        return [pl.ds(which * 8, 4), pl.ds(which * 8 + 4, 4)]

    def forward(place, device):
        return push(slots.at[c, place], slots.at[c, place], device)

    own_a, own_b = halves(v)
    right_a = forward(own_a, right)
    left_b = forward(own_b, left)
    right_b = forward(own_b, right)
    left_a = forward(own_a, left)
    lat_c = [forward(group, sibling)]

    for copy in w_g:
        copy.wait_recv()
    w_last = push(weights.at[mine], weights.at[mine], sibling)
    w_last.wait_recv()

    wide_m = lax.broadcasted_iota(jnp.int32, (MCOLS, HD), 1)
    terms = [
        dot(wout_v[:, h * HD : (h + 1) * HD], weights[2 * WID + h * HD : 2 * WID + (h + 1) * HD, :], NN)
        for h in range(HEADS)
    ]
    m_in[0, :, 0:HD] = jnp.where(wide_m < LAT, terms[0], pltpu.roll(terms[1], LAT, 1)).astype(BF16)
    m_in[0, :, HD:LANES] = jnp.where(wide_m < LAT, terms[2], terms[0] + terms[1] + terms[2]).astype(BF16)
    m_move = push(m_in.at[0], m_in.at[1], m_to)

    lane_t = lax.broadcasted_iota(jnp.int32, (1, HD), 1)
    lane_c = lax.broadcasted_iota(jnp.int32, (1, CHUNK), 1)
    tail_row = lax.broadcasted_iota(jnp.int32, (16, CHUNK), 0)

    def prepare(k, g0, g1):
        for i in range(4):
            n = 4 * k + i
            lats, scales = [], []
            for zz in range(2):
                near = slots[0, g0 * 8 + 2 * i + zz]
                far = slots[1, g1 * 8 + 2 * i + zz]
                middle = jnp.where(lane_t < LAT, near[:, HD:].astype(F32), far[:, :HD].astype(F32))
                lats += [near[:, :HD].astype(F32), middle, far[:, HD:].astype(F32)]
                sl = near[0:16, HD:].astype(F32)
                sr = far[0:16, :HD].astype(F32)
                sl = sl[0:3] + sl[3:6]
                sr = sr[0:3] + sr[3:6]
                tl = pltpu.roll(sl, LAT, 1)
                tr = pltpu.roll(sr, LAT, 1)
                scales += [
                    jnp.where(lane_t < LAT, tl[0:1], sl[1:2]),
                    jnp.where(lane_t < LAT, tl[2:3], tr[0:1]),
                    jnp.where(lane_t < LAT, sr[1:2], tr[2:3]),
                ]
            lat_c32 = jnp.concatenate(lats, axis=1)
            scale_row = jnp.concatenate(scales, axis=1)
            lat_cb = lat_c32.astype(BF16)
            upper = lane_c // 384
            inner = lane_c - upper * 384
            base0 = i * 8 * ROWS + g0 * 2 * ROWS
            base1 = g1 * 8 * ROWS + i * 2 * ROWS + ROWS
            token = inner + upper * (32 * ROWS) + jnp.where(inner < ROWS, base0, base1 - ROWS)
            hit = jnp.where(origin == token, 1.0, 0.0).astype(BF16)
            latq[0:ROWS, 0:LAT] += dot(hit, lat_cb, NT)
            scaled = lat_c32 * scale_row
            vals[n, 0:LAT, :] = scaled.astype(BF16)
            vals[n, LAT:FEAT, :] = jnp.where(tail_row == 0, 1.0, 0.0).astype(BF16)
            high, low = split(1.0 / scale_row)
            spread = jnp.where(tail_row == 0, high, 0.0)
            spread = jnp.where(tail_row == 1, low, spread)
            lat_x = jnp.concatenate([lat_cb, spread.astype(BF16)], axis=0)
            for h in range(HEADS):
                raw = dot(weights[WID + h * HD : WID + (h + 1) * HD, 0:FEAT], lat_x, NN)
                power = jnp.mean(raw * raw, axis=0, keepdims=True)
                inv = lax.rsqrt(power * (scale_row * scale_row) + EPS)
                ih, il = split(inv)
                tail = jnp.where((tail_row == 0) | (tail_row == 2), ih, 0.0)
                tail = jnp.where(tail_row == 1, il, tail)
                keys[h, n, 0:LAT, :] = (scaled * inv).astype(BF16)
                keys[h, n, LAT:FEAT, :] = tail.astype(BF16)

    for k, turn in enumerate((0, 1, 3, 2)):
        came = (v + 4 - turn) % 4
        if turn == 1:
            right_a.wait_recv()
            relay_a = forward(halves(came)[0], right)
            left_b.wait_recv()
            relay_b = forward(halves((v + 1) % 4)[1], left)
            right_b.wait_recv()
        elif turn == 3:
            left_a.wait_recv()
        elif turn == 2:
            relay_a.wait_recv()
            relay_b.wait_recv()
        if k:
            lat_c.append(forward(pl.ds(came * 8, 8), sibling))
        lat_c[k].wait_recv()
        prepare(k, (y + 4 - turn) % 4, (x + 4 - turn) % 4)
        if k == 1:
            m_move.wait_recv()
            m_slots[c, at] = m_in[1]
            m_z = push(m_slots.at[c, at], m_slots.at[c, at], z_peer)
    m_z.wait_recv()
    m_u = [push(m_slots.at[c, pair], m_slots.at[c, pair], device) for device in u_peers]

    rows = latq[0:ROWS, :].astype(BF16)
    lat_out[...] = latq[...].T[0:LAT, 0:ROWS].astype(BF16)
    twice = (latq[0:ROWS, :] + pltpu.roll(latq[0:ROWS, :], LAT, 1)).astype(BF16)
    squares = jnp.zeros((ROWS, 1), F32)
    for k in range(PARTS):
        center = dot(twice, centred[:, k * DEPTH : (k + 1) * DEPTH], NN)
        squares += jnp.sum(center * center, axis=1, keepdims=True)
    rstd = lax.rsqrt(squares * (1.0 / DIM) + EPS)
    unit = jnp.where(lax.broadcasted_iota(jnp.int32, (16, HD), 1) == LAT, 1.0, 0.0).astype(BF16)
    lane_q = lax.broadcasted_iota(jnp.int32, (ROWS, HD), 1)
    for h in range(HEADS):
        wq = weights[h * HD : (h + 1) * HD, :]
        wk = weights[WID + h * HD : WID + (h + 1) * HD, :]
        raw = rstd * dot(rows, wq, NT) + dot(unit, wq, NT)[0:1, :]
        q = raw * lax.rsqrt(jnp.mean(raw * raw, axis=1, keepdims=True) + EPS) * qg_v[...]
        high, low = split(q * kg_v[...] * (LOG2E / HD**0.5))
        folded = dot(high.astype(BF16), wk, NN) + dot(low.astype(BF16), wk, NN)
        bias_high, bias_low = split(folded[:, LAT : LAT + 1])
        value = jnp.where(lane_q < LAT, folded, 0.0)
        value = jnp.where((lane_q == LAT) | (lane_q == LAT + 1), bias_high, value)
        value = jnp.where(lane_q == LAT + 2, bias_low, value)
        queries[h] = value.astype(BF16)

    scores = [s_even, s_odd]
    running[...] = jnp.full_like(running, -jnp.inf)
    accum[...] = jnp.zeros_like(accum)

    def score(n, h, most):
        part = dot(queries[h][:, 0:FEAT], keys[h, n], NN)
        scores[h % 2][n] = part
        for k in range(CHUNK // HD):
            most = jnp.maximum(most, part[:, k * HD : (k + 1) * HD])
        return most

    def weigh(n, h, most):
        w = jnp.concatenate(
            [jnp.exp2(scores[h % 2][n, :, k * HD : (k + 1) * HD] - most).astype(BF16) for k in range(CHUNK // HD)],
            axis=1,
        )
        return dot(w, vals[n], NT)

    most = running[0]
    for n in range(CHUNKS):
        most = score(n, 0, most)
    running[0] = most
    for copy in m_u:
        copy.wait_recv()
    m_v = [push(m_slots.at[c, group], m_slots.at[c, group], device) for device in v_peers]
    m_c = [push(m_slots.at[c, group], m_slots.at[c, group], sibling)]
    mixed = []
    for h in range(HEADS):
        top[h] = jnp.broadcast_to(jnp.max(running[h], axis=1, keepdims=True), (ROWS, HD))

        most = top[h]
        added = accum[h, :, 0:FEAT]
        if h + 1 < HEADS:
            following = running[h + 1]
        for n in range(CHUNKS):
            if h + 1 < HEADS:
                following = score(n, h + 1, following)
            added += weigh(n, h, most)
        accum[h, :, 0:FEAT] = added
        if h + 1 < HEADS:
            running[h + 1] = following
        mixed.append(accum[h] / accum[h, :, LAT : LAT + 1])
        if h == 1:
            first[t] = jnp.where(lane_q < LAT, mixed[0], pltpu.roll(mixed[1], LAT, 1)).astype(BF16)
            o_first = [push(first.at[t], first.at[t], device) for device in tp_peers]
            for k in range(1, 4):
                m_v[k - 1].wait_recv()
                came = pl.ds(((v + 4 - k) % 4) * 8, 8)
                m_c.append(push(m_slots.at[c, came], m_slots.at[c, came], sibling))
    lower = pltpu.roll(mixed[2][ROWS // 2 :, :], LAT, 1)
    second[t] = jnp.where(lane_q[0 : ROWS // 2] < LAT, mixed[2][0 : ROWS // 2, :], lower).astype(BF16)
    o_second = [push(second.at[t], second.at[t], device) for device in tp_peers]

    for copy in m_c:
        copy.wait_recv()
    for slot in range(64):
        cc, rest = slot // 32, slot % 32
        vv, uu, zz = rest // 8, (rest // 2) % 4, rest % 2
        xx, yy = (uu, vv) if cc == 0 else (vv, uu)
        origin_at = (zz * 32 + xx * 8 + yy * 2 + cc + 63) % 64
        assembled[origin_at % 4, pl.ds((origin_at // 4) * MCOLS, MCOLS), :] = m_slots[cc, rest]
    quarter = pl.ds(pl.multiple_of(t * QUARTER, QUARTER), QUARTER)
    embedded = dot(rows[:, 0:LAT], emb_v[:, quarter], NN)
    for copy in o_first:
        copy.wait_recv()
    total = dot(first[0], assembled[0, :, 0:HD], NT)
    for k in range(1, 4):
        total += dot(first[k], assembled[k, :, 0:HD], NT)
    for copy in o_second:
        copy.wait_recv()
    one = jnp.where(lane_q == LAT, 1.0, 0.0)
    for k in range(4):
        packed = second[k].astype(F32)
        whole = jnp.concatenate([packed, pltpu.roll(packed, LAT, 1)], axis=0)
        whole = jnp.where(lane_q < LAT, whole, one).astype(BF16)
        total += dot(whole, assembled[k, :, HD:LANES], NT)
    block_out[...] = (embedded + gate_v[:, quarter] * total).astype(BF16)
    for copy in sent:
        copy.wait_send()


def leave(lat_ref, block_ref, lat_to, block_to, sem):
    copies = [
        pltpu.make_async_copy(lat_ref, lat_to, sem.at[0]),
        pltpu.make_async_copy(block_ref, block_to, sem.at[1]),
    ]
    for copy in copies:
        copy.start()
    for copy in copies:
        copy.wait()


COPIES = 50
LOADS = 18


def per_device(
    pixels, w_encode, w_latent, source_row, w_embed, mod_shift, mod_scale, gate, q_gain, k_gain, w_qkv, w_out
):
    operands = (
        pixels, w_encode, w_latent.T, source_row.reshape(1, ROWS), w_embed, mod_shift.reshape(1, DIM),
        mod_scale.reshape(1, DIM), gate.reshape(1, DIM), q_gain.reshape(1, HD), k_gain.reshape(1, HD), w_qkv, w_out.T,
    )
    vmem = pltpu.VMEM
    scratch = [
        vmem((PARTS, ROWS, DEPTH), BF16),
        vmem((PARTS, DEPTH, 512), BF16),
        vmem((LAT, 512), BF16),
        vmem((1, ROWS), jnp.int32),
        vmem((LAT, DIM), BF16),
        vmem((1, DIM), F32),
        vmem((1, DIM), F32),
        vmem((1, DIM), F32),
        vmem((1, HD), F32),
        vmem((1, HD), F32),
        vmem((3, MCOLS, WID), BF16),
        vmem((MCOLS, WID), BF16),
        vmem((HD, LANES), F32),
        vmem((HD, DIM), BF16),
        vmem((DIM, HD), BF16),
        vmem((3 * WID, HD), BF16),
        vmem((4, LAT, LANES), BF16),
        vmem((576, HD), BF16),
        vmem((576, HD), BF16),
        vmem((4, 144, HD), BF16),
        vmem((8, 144, HD), BF16),
        vmem((3 * WID, HD), BF16),
        vmem((2, 32, LAT, LANES), BF16),
        vmem((2, MCOLS, LANES), BF16),
        vmem((2, 32, MCOLS, LANES), BF16),
        vmem((LANES, HD), F32),
        vmem((HD, LANES), F32),
        vmem((HEADS, ROWS, HD), BF16),
        vmem((HEADS, CHUNKS, FEAT, CHUNK), BF16),
        vmem((CHUNKS, FEAT, CHUNK), BF16),
        vmem((CHUNKS, ROWS, CHUNK), F32),
        vmem((CHUNKS, ROWS, CHUNK), F32),
        vmem((HEADS, ROWS, HD), F32),
        vmem((HEADS, ROWS, HD), F32),
        vmem((HEADS, ROWS, HD), F32),
        vmem((4, ROWS, HD), BF16),
        vmem((4, ROWS // 2, HD), BF16),
        vmem((4, QUARTER, LANES), BF16),
        pltpu.SemaphoreType.DMA((LOADS,)),
        pltpu.SemaphoreType.DMA((COPIES,)),
        pltpu.SemaphoreType.DMA((COPIES,)),
    ]
    lat, out = pl.pallas_call(
        kernel,
        out_shape=(jax.ShapeDtypeStruct((LAT, ROWS), BF16), jax.ShapeDtypeStruct((ROWS, QUARTER), BF16)),
        in_specs=[pl.BlockSpec(memory_space=pl.ANY)] * len(operands),
        out_specs=(pl.BlockSpec(memory_space=pltpu.VMEM), pl.BlockSpec(memory_space=pltpu.VMEM)),
        scratch_shapes=scratch,
        compiler_params=pltpu.CompilerParams(collective_id=0, has_side_effects=True, vmem_limit_bytes=VMEM_LIMIT),
    )(*operands)
    lat, out = pl.pallas_call(
        leave,
        out_shape=(jax.ShapeDtypeStruct((LAT, ROWS), BF16), jax.ShapeDtypeStruct((ROWS, QUARTER), BF16)),
        in_specs=[pl.BlockSpec(memory_space=pl.ANY)] * 2,
        out_specs=(pl.BlockSpec(memory_space=pl.ANY), pl.BlockSpec(memory_space=pl.ANY)),
        scratch_shapes=[pltpu.SemaphoreType.DMA((2,))],
    )(lat, out)
    return lat.T, out


def solution(mesh):
    placed = (
        P("sec", None), P(None, "tp"), P("tp", None), P("sec"), P(), P(), P(), P(), P(), P(),
        P(None, "sec", "tp"), P("tp", "sec"),
    )
    return jax.shard_map(
        per_device, mesh=mesh, in_specs=placed, out_specs=(P("sec", None), P("sec", "tp")), check_vma=False
    )
```

```python
import jax
import jax.numpy as jnp
from jax import lax
from jax.experimental import pallas as pl
from jax.experimental.pallas import tpu as pltpu
from jax.sharding import PartitionSpec as P

MESH = pl.DeviceIdType.MESH
HD = 128
HEADS = 3
LAT = 64
ROWS = 192
LANES = 256
WID = HEADS * HD
DIM = 3072
FEAT = 80
CHUNK = 768
CHUNKS = 16
MCOLS = 48
QUARTER = 768
PARTS = 4
DEPTH = DIM // PARTS
F32 = jnp.float32
BF16 = jnp.bfloat16
NT = (((1,), (1,)), ((), ()))
NN = (((1,), (0,)), ((), ()))
TN = (((0,), (0,)), ((), ()))
EPS = 1e-6
LOG2E = 1.4426950408889634
VMEM_LIMIT = 58 * 1024 * 1024


def dot(a, b, dims):
    return lax.dot_general(a, b, dims, preferred_element_type=F32)


def split(value):
    high = value.astype(BF16).astype(F32)
    return high, value - high


def kernel(
    pixels, w_encode, w_latent, source, w_embed, mod_shift, mod_scale, gate, q_gain, k_gain, w_qkv, w_out,
    lat_out, block_out,
    pix_v, enc_v, wlat_v, src_v, emb_v, shift_v, scale_v, gate_v, qg_v, kg_v, wqkv_v, wout_v,
    wide, centred, centred_t, wp, lat_in, core_in, half, x_in, y_in, weights,
    slots, m_in, m_slots, latq, square, queries, keys, vals, s_even, s_odd, running, top, accum,
    first, second, assembled,
    load, send, recv,
):
    s = lax.axis_index("sec")
    t = lax.axis_index("tp")
    z = s // 32
    x = (s // 8) % 4
    y = (s // 2) % 4
    c = s % 2
    b = z * 4 + y
    at = z * (x * 4 + y) + (1 - z) * (y * 4 + x)
    sibling = {"sec": s + 1 - 2 * c}
    tp_peers = [{"tp": (t + k) % 4} for k in range(1, 4)]
    x_at = [(x + k) % 4 for k in range(1, 4)]
    x_peers = [{"sec": s + (xx - x) * 8} for xx in x_at]
    b_at = [(b + k) % 8 for k in range(1, 8)]
    b_peers = [{"sec": (bb // 4) * 32 + x * 8 + (bb % 4) * 2 + c} for bb in b_at]
    y_peers = [{"sec": s + ((y + k) % 4 - y) * 2} for k in range(1, 4)]
    cross_x = [{"sec": s + (1 - 2 * z) * 32 + (xx - x) * 8} for xx in x_at]
    inner = z * y + (1 - z) * x
    stride = 8 - 6 * z
    plane_peers = [{"sec": s + ((inner + k) % 4 - inner) * stride} for k in range(1, 4)]
    plane_peers += [
        {"sec": s + (1 - 2 * z) * 32 + ((inner + k) % 4 - inner) * stride} for k in range(4)
    ]
    m_to = {"tp": s // 16, "sec": ((s % 16) * 4 + t + 1) % 64}
    back = (s + 63) % 64
    m_from = {"tp": back % 4, "sec": t * 16 + back // 4}

    sent = []
    used = [0]

    def push(src, dst, device):
        i = used[0]
        used[0] += 1
        copy = pltpu.make_async_remote_copy(
            src_ref=src, dst_ref=dst, send_sem=send.at[i], recv_sem=recv.at[i], device_id=device, device_id_type=MESH
        )
        copy.start()
        sent.append(copy)
        return copy

    def spread_plane(ref):
        return [push(ref.at[z, c, at], ref.at[z, c, at], device) for device in plane_peers]

    by_y = pl.ds(y * 4, 4)
    by_x = pl.ds(x * 4, 4)

    def spread_rest(ref):
        pairs = []
        for k in range(3):
            pairs.append(
                (
                    push(ref.at[0, c, by_y], ref.at[0, c, by_y], y_peers[k]),
                    push(ref.at[1, c, by_x], ref.at[1, c, by_x], x_peers[k]),
                )
            )
        return pairs

    def hand_over(ref, k):
        from_y = pl.ds(((y + 4 - k) % 4) * 4, 4)
        from_x = pl.ds(((x + 4 - k) % 4) * 4, 4)
        return (
            push(ref.at[0, c, from_y], ref.at[0, c, from_y], sibling),
            push(ref.at[1, c, from_x], ref.at[1, c, from_x], sibling),
        )

    loads = [0]

    def fetch(src, dst):
        copy = pltpu.make_async_copy(src, dst, load.at[loads[0]])
        loads[0] += 1
        copy.start()
        return copy

    early = [fetch(w_embed, emb_v), fetch(w_qkv, wqkv_v), fetch(mod_scale, scale_v), fetch(mod_shift, shift_v)]
    parts = []
    for k in range(PARTS):
        depth = pl.ds(k * DEPTH, DEPTH)
        parts.append((fetch(pixels.at[:, depth], pix_v.at[k]), fetch(w_encode.at[depth], enc_v.at[k])))
    wlat_load = fetch(w_latent, wlat_v)
    late = [
        fetch(source, src_v), fetch(gate, gate_v), fetch(q_gain, qg_v), fetch(k_gain, kg_v), fetch(w_out, wout_v)
    ]

    barrier = pltpu.get_barrier_semaphore()
    greet = tp_peers + [sibling] + x_peers + b_peers + cross_x + [m_from]
    for device in greet:
        pl.semaphore_signal(barrier, inc=1, device_id=device, device_id_type=MESH)

    for copy in early:
        copy.wait()
    block = (3 * s) // 8 - s // 62
    base = pl.ds(pl.multiple_of(block * HD, HD), LANES)
    mean = jnp.mean(emb_v[...].astype(F32), axis=1, keepdims=True)
    wide[0:LAT, :] = (emb_v[:, base].astype(F32) - mean) * scale_v[:, base]
    wide[LAT:HD, :] = jnp.where(
        lax.broadcasted_iota(jnp.int32, (LAT, LANES), 0) < 2, jnp.broadcast_to(shift_v[:, base], (LAT, LANES)), 0.0
    )
    offset = s * MCOLS - block * HD
    turned = pltpu.roll(wide[...], (LANES - offset) % LANES, 1)[:, 0:HD].T
    high, low = split(turned[0:MCOLS, :])
    high, low = high.astype(BF16), low.astype(BF16)
    for i in range(3):
        wp[i * WID : (i + 1) * WID, :] = (dot(wqkv_v[i], high, TN) + dot(wqkv_v[i], low, TN)).astype(BF16)

    total = jnp.zeros((ROWS, 512), F32)
    for k in range(PARTS):
        parts[k][0].wait()
        parts[k][1].wait()
        total += dot(pix_v[k], enc_v[k], NN)
    hidden = jax.nn.silu(total).astype(BF16)
    wlat_load.wait()
    wide[...] = jnp.zeros_like(wide)
    wide[0:LAT, 0:ROWS] = dot(wlat_v[...], hidden, NT)
    lat_in[t] = pltpu.roll(wide[0:LAT, :], LAT * c, 1).astype(BF16)

    pl.semaphore_wait(barrier, len(greet))
    mine = pl.ds(pl.multiple_of(c * 576, 576), 576)
    other = pl.ds(pl.multiple_of((1 - c) * 576, 576), 576)
    w_core = push(wp.at[other], core_in, sibling)
    lat_tp = [push(lat_in.at[t], lat_in.at[t], device) for device in tp_peers]

    high, low = split(emb_v[...].astype(F32) - mean)
    both_terms = jnp.concatenate([high, low], axis=0)
    centred[...] = both_terms.astype(BF16)
    centred_t[...] = both_terms.T.astype(BF16)

    w_core.wait_recv()
    half[...] = (wp[mine, :].astype(F32) + core_in[...].astype(F32)).astype(BF16)
    w_x = []
    for k in range(3):
        w_x.append(push(half.at[pl.ds(pl.multiple_of(x_at[k] * 144, 144), 144)], x_in.at[x], x_peers[k]))
    x_in[x] = half[pl.ds(pl.multiple_of(x * 144, 144), 144), :]

    for copy in late:
        copy.wait()
    square[...] = jnp.zeros_like(square)
    square[:, 0:ROWS] = jnp.broadcast_to(src_v[...].astype(F32), (HD, ROWS))
    origin = square[...].T[0:ROWS, 0:1].astype(jnp.int32)
    latq[...] = jnp.zeros_like(latq)

    for copy in lat_tp:
        copy.wait_recv()
    summed = lat_in[0].astype(F32)
    for k in range(1, 4):
        summed += lat_in[k].astype(F32)
    lat = summed.astype(BF16)
    twice = jnp.concatenate([lat, lat], axis=0)
    squares = jnp.zeros((1, LANES), F32)
    for k in range(PARTS):
        center = dot(centred_t[k * DEPTH : (k + 1) * DEPTH, :], twice, NN)
        squares += jnp.sum(center * center, axis=0, keepdims=True)
    rstd = lax.rsqrt(squares * (1.0 / DIM) + EPS)
    rstd = jnp.broadcast_to(rstd, (LAT, LANES))
    row = lax.broadcasted_iota(jnp.int32, (LAT, LANES), 0)
    lane = lax.broadcasted_iota(jnp.int32, (LAT, LANES), 1)
    high, low = split(rstd)
    piece = lat.astype(F32)
    spare = (lane >= ROWS * (1 - c)) & (lane < ROWS * (1 - c) + LAT)
    for k in range(3):
        turn = (ROWS * (1 - c) - LAT * c - LAT * k + 2 * LANES) % LANES
        piece = jnp.where(spare & (row == k), pltpu.roll(high, turn, 1), piece)
        piece = jnp.where(spare & (row == k + 3), pltpu.roll(low, turn, 1), piece)
    slots[z, c, at] = piece.astype(BF16)
    lat_plane = spread_plane(slots)

    for copy in w_x:
        copy.wait_recv()
    added = x_in[0].astype(F32)
    for k in range(1, 4):
        added += x_in[k].astype(F32)
    y_in[b] = added.astype(BF16)
    w_b = [push(y_in.at[b], y_in.at[b], device) for device in b_peers]

    for copy in w_b:
        copy.wait_recv()
    added = y_in[0].astype(F32)
    for k in range(1, 8):
        added += y_in[k].astype(F32)
    place = pl.ds(pl.multiple_of(c * 576 + x * 144, 144), 144)
    weights[place, :] = added.astype(BF16)
    w_g = [push(weights.at[place], weights.at[place], device) for device in x_peers]

    for copy in lat_plane:
        copy.wait_recv()
    lat_rest = spread_rest(slots)
    lat_c = [hand_over(slots, 0)]

    for copy in w_g:
        copy.wait_recv()
    w_last = push(weights.at[mine], weights.at[mine], sibling)
    w_last.wait_recv()

    wide_m = lax.broadcasted_iota(jnp.int32, (MCOLS, HD), 1)
    terms = [
        dot(wout_v[:, h * HD : (h + 1) * HD], weights[2 * WID + h * HD : 2 * WID + (h + 1) * HD, :], NN)
        for h in range(HEADS)
    ]
    m_in[0, :, 0:HD] = jnp.where(wide_m < LAT, terms[0], pltpu.roll(terms[1], LAT, 1)).astype(BF16)
    m_in[0, :, HD:LANES] = jnp.where(wide_m < LAT, terms[2], terms[0] + terms[1] + terms[2]).astype(BF16)
    m_move = push(m_in.at[0], m_in.at[1], m_to)

    lane_t = lax.broadcasted_iota(jnp.int32, (1, HD), 1)
    lane_c = lax.broadcasted_iota(jnp.int32, (1, CHUNK), 1)
    tail_row = lax.broadcasted_iota(jnp.int32, (16, CHUNK), 0)

    def prepare(k, g0, g1):
        for i in range(4):
            n = 4 * k + i
            lats, scales = [], []
            for zz in range(2):
                near = slots[zz, 0, (g1 if zz else g0) * 4 + i]
                far = slots[zz, 1, (g1 if zz else g0) * 4 + i]
                middle = jnp.where(lane_t < LAT, near[:, HD:].astype(F32), far[:, :HD].astype(F32))
                lats += [near[:, :HD].astype(F32), middle, far[:, HD:].astype(F32)]
                sl = near[0:16, HD:].astype(F32)
                sr = far[0:16, :HD].astype(F32)
                sl = sl[0:3] + sl[3:6]
                sr = sr[0:3] + sr[3:6]
                tl = pltpu.roll(sl, LAT, 1)
                tr = pltpu.roll(sr, LAT, 1)
                scales += [
                    jnp.where(lane_t < LAT, tl[0:1], sl[1:2]),
                    jnp.where(lane_t < LAT, tl[2:3], tr[0:1]),
                    jnp.where(lane_t < LAT, sr[1:2], tr[2:3]),
                ]
            lat_c32 = jnp.concatenate(lats, axis=1)
            scale_row = jnp.concatenate(scales, axis=1)
            lat_cb = lat_c32.astype(BF16)
            start = jnp.where(lane_c < 384, (i * 8 + g0 * 2) * ROWS, (32 + g1 * 8 + i * 2) * ROWS - 384)
            token = lane_c + start
            hit = jnp.where(origin == token, 1.0, 0.0).astype(BF16)
            latq[0:ROWS, 0:LAT] += dot(hit, lat_cb, NT)
            scaled = lat_c32 * scale_row
            vals[n, 0:LAT, :] = scaled.astype(BF16)
            vals[n, LAT:FEAT, :] = jnp.where(tail_row == 0, 1.0, 0.0).astype(BF16)
            high, low = split(1.0 / scale_row)
            spread = jnp.where(tail_row == 0, high, 0.0)
            spread = jnp.where(tail_row == 1, low, spread)
            lat_x = jnp.concatenate([lat_cb, spread.astype(BF16)], axis=0)
            for h in range(HEADS):
                raw = dot(weights[WID + h * HD : WID + (h + 1) * HD, 0:FEAT], lat_x, NN)
                power = jnp.mean(raw * raw, axis=0, keepdims=True)
                inv = lax.rsqrt(power * (scale_row * scale_row) + EPS)
                ih, il = split(inv)
                tail = jnp.where((tail_row == 0) | (tail_row == 2), ih, 0.0)
                tail = jnp.where(tail_row == 1, il, tail)
                keys[h, n, 0:LAT, :] = (scaled * inv).astype(BF16)
                keys[h, n, LAT:FEAT, :] = tail.astype(BF16)

    for k in range(4):
        if k:
            for copy in lat_rest[k - 1]:
                copy.wait_recv()
            lat_c.append(hand_over(slots, k))
        for copy in lat_c[k]:
            copy.wait_recv()
        prepare(k, (y + 4 - k) % 4, (x + 4 - k) % 4)
    m_move.wait_recv()
    m_slots[z, c, at] = m_in[1]
    m_plane = spread_plane(m_slots)

    rows = latq[0:ROWS, :].astype(BF16)
    lat_out[...] = latq[...].T[0:LAT, 0:ROWS].astype(BF16)
    twice = (latq[0:ROWS, :] + pltpu.roll(latq[0:ROWS, :], LAT, 1)).astype(BF16)
    squares = jnp.zeros((ROWS, 1), F32)
    for k in range(PARTS):
        center = dot(twice, centred[:, k * DEPTH : (k + 1) * DEPTH], NN)
        squares += jnp.sum(center * center, axis=1, keepdims=True)
    rstd = lax.rsqrt(squares * (1.0 / DIM) + EPS)
    unit = jnp.where(lax.broadcasted_iota(jnp.int32, (16, HD), 1) == LAT, 1.0, 0.0).astype(BF16)
    lane_q = lax.broadcasted_iota(jnp.int32, (ROWS, HD), 1)
    for h in range(HEADS):
        wq = weights[h * HD : (h + 1) * HD, :]
        wk = weights[WID + h * HD : WID + (h + 1) * HD, :]
        raw = rstd * dot(rows, wq, NT) + dot(unit, wq, NT)[0:1, :]
        q = raw * lax.rsqrt(jnp.mean(raw * raw, axis=1, keepdims=True) + EPS) * qg_v[...]
        high, low = split(q * kg_v[...] * (LOG2E / HD**0.5))
        folded = dot(high.astype(BF16), wk, NN) + dot(low.astype(BF16), wk, NN)
        bias_high, bias_low = split(folded[:, LAT : LAT + 1])
        value = jnp.where(lane_q < LAT, folded, 0.0)
        value = jnp.where((lane_q == LAT) | (lane_q == LAT + 1), bias_high, value)
        value = jnp.where(lane_q == LAT + 2, bias_low, value)
        queries[h] = value.astype(BF16)

    scores = [s_even, s_odd]
    running[...] = jnp.full_like(running, -jnp.inf)
    accum[...] = jnp.zeros_like(accum)

    def score(n, h, most):
        part = dot(queries[h][:, 0:FEAT], keys[h, n], NN)
        scores[h % 2][n] = part
        for k in range(CHUNK // HD):
            most = jnp.maximum(most, part[:, k * HD : (k + 1) * HD])
        return most

    def weigh(n, h, most):
        w = jnp.concatenate(
            [jnp.exp2(scores[h % 2][n, :, k * HD : (k + 1) * HD] - most).astype(BF16) for k in range(CHUNK // HD)],
            axis=1,
        )
        return dot(w, vals[n], NT)

    most = running[0]
    for n in range(CHUNKS):
        most = score(n, 0, most)
    running[0] = most
    mixed = []
    for h in range(HEADS):
        top[h] = jnp.broadcast_to(jnp.max(running[h], axis=1, keepdims=True), (ROWS, HD))

        most = top[h]
        added = accum[h, :, 0:FEAT]
        if h + 1 < HEADS:
            following = running[h + 1]
        for n in range(CHUNKS):
            if h + 1 < HEADS:
                following = score(n, h + 1, following)
            added += weigh(n, h, most)
        accum[h, :, 0:FEAT] = added
        if h + 1 < HEADS:
            running[h + 1] = following
        mixed.append(accum[h] / accum[h, :, LAT : LAT + 1])
        if h == 0:
            for copy in m_plane:
                copy.wait_recv()
            m_rest = spread_rest(m_slots)
        if h == 1:
            first[t] = jnp.where(lane_q < LAT, mixed[0], pltpu.roll(mixed[1], LAT, 1)).astype(BF16)
            o_first = [push(first.at[t], first.at[t], device) for device in tp_peers]
    lower = pltpu.roll(mixed[2][ROWS // 2 :, :], LAT, 1)
    second[t] = jnp.where(lane_q[0 : ROWS // 2] < LAT, mixed[2][0 : ROWS // 2, :], lower).astype(BF16)
    o_second = [push(second.at[t], second.at[t], device) for device in tp_peers]

    m_c = list(hand_over(m_slots, 0))
    for k in range(1, 4):
        for copy in m_rest[k - 1]:
            copy.wait_recv()
        m_c += hand_over(m_slots, k)
    for copy in m_c:
        copy.wait_recv()
    for slot in range(64):
        zz, cc, outer, step = slot // 32, (slot // 16) % 2, (slot // 4) % 4, slot % 4
        xx, yy = (outer, step) if zz else (step, outer)
        origin_at = (zz * 32 + xx * 8 + yy * 2 + cc + 63) % 64
        assembled[origin_at % 4, pl.ds((origin_at // 4) * MCOLS, MCOLS), :] = m_slots[zz, cc, outer * 4 + step]
    quarter = pl.ds(pl.multiple_of(t * QUARTER, QUARTER), QUARTER)
    embedded = dot(rows[:, 0:LAT], emb_v[:, quarter], NN)
    for copy in o_first:
        copy.wait_recv()
    total = dot(first[0], assembled[0, :, 0:HD], NT)
    for k in range(1, 4):
        total += dot(first[k], assembled[k, :, 0:HD], NT)
    for copy in o_second:
        copy.wait_recv()
    one = jnp.where(lane_q == LAT, 1.0, 0.0)
    for k in range(4):
        packed = second[k].astype(F32)
        whole = jnp.concatenate([packed, pltpu.roll(packed, LAT, 1)], axis=0)
        whole = jnp.where(lane_q < LAT, whole, one).astype(BF16)
        total += dot(whole, assembled[k, :, HD:LANES], NT)
    block_out[...] = (embedded + gate_v[:, quarter] * total).astype(BF16)
    for copy in sent:
        copy.wait_send()


def leave(lat_ref, block_ref, lat_to, block_to):
    lat_to[...] = lat_ref[...]
    block_to[...] = block_ref[...]


COPIES = 67
LOADS = 18


def per_device(
    pixels, w_encode, w_latent, source_row, w_embed, mod_shift, mod_scale, gate, q_gain, k_gain, w_qkv, w_out
):
    operands = (
        pixels, w_encode, w_latent.T, source_row.reshape(1, ROWS), w_embed, mod_shift.reshape(1, DIM),
        mod_scale.reshape(1, DIM), gate.reshape(1, DIM), q_gain.reshape(1, HD), k_gain.reshape(1, HD), w_qkv, w_out.T,
    )
    vmem = pltpu.VMEM
    scratch = [
        vmem((PARTS, ROWS, DEPTH), BF16),
        vmem((PARTS, DEPTH, 512), BF16),
        vmem((LAT, 512), BF16),
        vmem((1, ROWS), jnp.int32),
        vmem((LAT, DIM), BF16),
        vmem((1, DIM), F32),
        vmem((1, DIM), F32),
        vmem((1, DIM), F32),
        vmem((1, HD), F32),
        vmem((1, HD), F32),
        vmem((3, MCOLS, WID), BF16),
        vmem((MCOLS, WID), BF16),
        vmem((HD, LANES), F32),
        vmem((HD, DIM), BF16),
        vmem((DIM, HD), BF16),
        vmem((3 * WID, HD), BF16),
        vmem((4, LAT, LANES), BF16),
        vmem((576, HD), BF16),
        vmem((576, HD), BF16),
        vmem((4, 144, HD), BF16),
        vmem((8, 144, HD), BF16),
        vmem((3 * WID, HD), BF16),
        vmem((2, 2, 16, LAT, LANES), BF16),
        vmem((2, MCOLS, LANES), BF16),
        vmem((2, 2, 16, MCOLS, LANES), BF16),
        vmem((LANES, HD), F32),
        vmem((HD, LANES), F32),
        vmem((HEADS, ROWS, HD), BF16),
        vmem((HEADS, CHUNKS, FEAT, CHUNK), BF16),
        vmem((CHUNKS, FEAT, CHUNK), BF16),
        vmem((CHUNKS, ROWS, CHUNK), F32),
        vmem((CHUNKS, ROWS, CHUNK), F32),
        vmem((HEADS, ROWS, HD), F32),
        vmem((HEADS, ROWS, HD), F32),
        vmem((HEADS, ROWS, HD), F32),
        vmem((4, ROWS, HD), BF16),
        vmem((4, ROWS // 2, HD), BF16),
        vmem((4, QUARTER, LANES), BF16),
        pltpu.SemaphoreType.DMA((LOADS,)),
        pltpu.SemaphoreType.DMA((COPIES,)),
        pltpu.SemaphoreType.DMA((COPIES,)),
    ]
    lat, out = pl.pallas_call(
        kernel,
        out_shape=(jax.ShapeDtypeStruct((LAT, ROWS), BF16), jax.ShapeDtypeStruct((ROWS, QUARTER), BF16)),
        in_specs=[pl.BlockSpec(memory_space=pl.ANY)] * len(operands),
        out_specs=(pl.BlockSpec(memory_space=pltpu.VMEM), pl.BlockSpec(memory_space=pltpu.VMEM)),
        scratch_shapes=scratch,
        compiler_params=pltpu.CompilerParams(collective_id=0, has_side_effects=True, vmem_limit_bytes=VMEM_LIMIT),
    )(*operands)
    lat, out = pl.pallas_call(
        leave,
        out_shape=(jax.ShapeDtypeStruct((LAT, ROWS), BF16), jax.ShapeDtypeStruct((ROWS, QUARTER), BF16)),
    )(lat, out)
    return lat.T, out


def solution(mesh):
    placed = (
        P("sec", None), P(None, "tp"), P("tp", None), P("sec"), P(), P(), P(), P(), P(), P(),
        P(None, "sec", "tp"), P("tp", "sec"),
    )
    return jax.shard_map(
        per_device, mesh=mesh, in_specs=placed, out_specs=(P("sec", None), P("sec", "tp")), check_vma=False
    )
```

```python
import jax
import jax.numpy as jnp
from jax import lax
from jax.experimental import pallas as pl
from jax.experimental.pallas import tpu as pltpu
from jax.sharding import PartitionSpec as P

MESH = pl.DeviceIdType.MESH
HD = 128
HEADS = 3
LAT = 64
ROWS = 192
LANES = 256
WID = HEADS * HD
DIM = 3072
FEAT = 80
CHUNK = 768
CHUNKS = 16
MCOLS = 48
QUARTER = 768
PARTS = 4
DEPTH = DIM // PARTS
F32 = jnp.float32
BF16 = jnp.bfloat16
NT = (((1,), (1,)), ((), ()))
NN = (((1,), (0,)), ((), ()))
TN = (((0,), (0,)), ((), ()))
EPS = 1e-6
LOG2E = 1.4426950408889634
VMEM_LIMIT = 58 * 1024 * 1024


def dot(a, b, dims):
    return lax.dot_general(a, b, dims, preferred_element_type=F32)


def split(value):
    high = value.astype(BF16).astype(F32)
    return high, value - high


def kernel(
    pixels, w_encode, w_latent, source, w_embed, mod_shift, mod_scale, gate, q_gain, k_gain, w_qkv, w_out,
    lat_out, block_out,
    pix_v, enc_v, wlat_v, src_v, emb_v, shift_v, scale_v, gate_v, qg_v, kg_v, wqkv_v, wout_v,
    wide, centred, centred_t, wp, lat_in, x_in, y_in, weights,
    slots, m_in, m_slots, latq, square, queries, keys, vals, s_even, s_odd, running, top, accum,
    first, second, assembled,
    load, send, recv,
):
    s = lax.axis_index("sec")
    t = lax.axis_index("tp")
    z = s // 32
    x = (s // 8) % 4
    y = (s // 2) % 4
    c = s % 2
    b = z * 4 + y
    at = z * (x * 4 + y) + (1 - z) * (y * 4 + x)
    sibling = {"sec": s + 1 - 2 * c}
    tp_peers = [{"tp": (t + k) % 4} for k in range(1, 4)]
    x_at = [(x + k) % 4 for k in range(1, 4)]
    x_peers = [{"sec": s + (xx - x) * 8} for xx in x_at]
    b_at = [(b + k) % 8 for k in range(1, 8)]
    b_peers = [{"sec": (bb // 4) * 32 + x * 8 + (bb % 4) * 2 + c} for bb in b_at]
    y_peers = [{"sec": s + ((y + k) % 4 - y) * 2} for k in range(1, 4)]
    cross_x = [{"sec": s + (1 - 2 * z) * 32 + (xx - x) * 8} for xx in x_at]
    inner = z * y + (1 - z) * x
    stride = 8 - 6 * z
    plane_peers = [{"sec": s + ((inner + k) % 4 - inner) * stride} for k in range(1, 4)]
    plane_peers += [
        {"sec": s + (1 - 2 * z) * 32 + ((inner + k) % 4 - inner) * stride} for k in range(4)
    ]
    m_peer = {"tp": s // 16, "sec": (t // 2) * 32 + (2 * (t % 2) + x % 2) * 8 + y * 2 + 1 - c}
    a = x * 2 + c
    a_at = [(a + k) % 8 for k in range(1, 8)]
    a_peers = [{"sec": z * 32 + (aa // 2) * 8 + y * 2 + aa % 2} for aa in a_at]

    sent = []
    used = [0]

    def push(src, dst, device):
        i = used[0]
        used[0] += 1
        copy = pltpu.make_async_remote_copy(
            src_ref=src, dst_ref=dst, send_sem=send.at[i], recv_sem=recv.at[i], device_id=device, device_id_type=MESH
        )
        copy.start()
        sent.append(copy)
        return copy

    def spread_plane(ref):
        return [push(ref.at[z, c, at], ref.at[z, c, at], device) for device in plane_peers]

    by_y = pl.ds(y * 4, 4)
    by_x = pl.ds(x * 4, 4)

    def spread_rest(ref):
        pairs = []
        for k in range(3):
            pairs.append(
                (
                    push(ref.at[0, c, by_y], ref.at[0, c, by_y], y_peers[k]),
                    push(ref.at[1, c, by_x], ref.at[1, c, by_x], x_peers[k]),
                )
            )
        return pairs

    def hand_over(ref, k):
        from_y = pl.ds(((y + 4 - k) % 4) * 4, 4)
        from_x = pl.ds(((x + 4 - k) % 4) * 4, 4)
        return (
            push(ref.at[0, c, from_y], ref.at[0, c, from_y], sibling),
            push(ref.at[1, c, from_x], ref.at[1, c, from_x], sibling),
        )

    barrier = pltpu.get_barrier_semaphore()
    greet = [m_peer] + tp_peers + b_peers + cross_x + a_peers
    for device in greet:
        pl.semaphore_signal(barrier, inc=1, device_id=device, device_id_type=MESH)

    loads = [0]

    def fetch(src, dst):
        copy = pltpu.make_async_copy(src, dst, load.at[loads[0]])
        loads[0] += 1
        copy.start()
        return copy

    early = [fetch(w_embed, emb_v), fetch(w_qkv, wqkv_v), fetch(mod_scale, scale_v), fetch(mod_shift, shift_v)]
    parts = []
    for k in range(PARTS):
        depth = pl.ds(k * DEPTH, DEPTH)
        parts.append((fetch(pixels.at[:, depth], pix_v.at[k]), fetch(w_encode.at[depth], enc_v.at[k])))
    wlat_load = fetch(w_latent, wlat_v)
    late = [
        fetch(source, src_v), fetch(gate, gate_v), fetch(q_gain, qg_v), fetch(k_gain, kg_v), fetch(w_out, wout_v)
    ]

    for copy in early:
        copy.wait()
    block = (3 * s) // 8 - s // 62
    base = pl.ds(pl.multiple_of(block * HD, HD), LANES)
    mean = jnp.mean(emb_v[...].astype(F32), axis=1, keepdims=True)
    wide[0:LAT, :] = (emb_v[:, base].astype(F32) - mean) * scale_v[:, base]
    wide[LAT:HD, :] = jnp.where(
        lax.broadcasted_iota(jnp.int32, (LAT, LANES), 0) < 2, jnp.broadcast_to(shift_v[:, base], (LAT, LANES)), 0.0
    )
    offset = s * MCOLS - block * HD
    turned = pltpu.roll(wide[...], (LANES - offset) % LANES, 1)[:, 0:HD].T
    high, low = split(turned[0:MCOLS, :])
    high, low = high.astype(BF16), low.astype(BF16)
    for i in range(3):
        wp[i * WID : (i + 1) * WID, :] = (dot(wqkv_v[i], high, TN) + dot(wqkv_v[i], low, TN)).astype(BF16)

    high, low = split(emb_v[...].astype(F32) - mean)
    both_terms = jnp.concatenate([high, low], axis=0)
    centred[...] = both_terms.astype(BF16)
    centred_t[...] = both_terms.T.astype(BF16)

    total = jnp.zeros((ROWS, 512), F32)
    for k in range(PARTS):
        parts[k][0].wait()
        parts[k][1].wait()
        total += dot(pix_v[k], enc_v[k], NN)
    hidden = jax.nn.silu(total).astype(BF16)
    wlat_load.wait()
    wide[...] = jnp.zeros_like(wide)
    wide[0:LAT, 0:ROWS] = dot(wlat_v[...], hidden, NT)
    lat_in[t] = pltpu.roll(wide[0:LAT, :], LAT * c, 1).astype(BF16)

    for copy in late:
        copy.wait()
    square[...] = jnp.zeros_like(square)
    square[:, 0:ROWS] = jnp.broadcast_to(src_v[...].astype(F32), (HD, ROWS))
    origin = square[...].T[0:ROWS, 0:1].astype(jnp.int32)
    latq[...] = jnp.zeros_like(latq)
    place = pl.ds(pl.multiple_of(a * 144, 144), 144)

    pl.semaphore_wait(barrier, len(greet))
    lat_tp = [push(lat_in.at[t], lat_in.at[t], device) for device in tp_peers]

    w_x = []
    for k in range(7):
        w_x.append(push(wp.at[pl.ds(pl.multiple_of(a_at[k] * 144, 144), 144)], x_in.at[a], a_peers[k]))
    x_in[a] = wp[place, :]
    for copy in w_x:
        copy.wait_recv()
    added = x_in[0].astype(F32)
    for k in range(1, 8):
        added += x_in[k].astype(F32)
    y_in[b] = added.astype(BF16)
    w_b = [push(y_in.at[b], y_in.at[b], device) for device in b_peers]

    for copy in lat_tp:
        copy.wait_recv()
    summed = lat_in[0].astype(F32)
    for k in range(1, 4):
        summed += lat_in[k].astype(F32)
    lat = summed.astype(BF16)
    twice = jnp.concatenate([lat, lat], axis=0)
    squares = jnp.zeros((1, LANES), F32)
    for k in range(PARTS):
        center = dot(centred_t[k * DEPTH : (k + 1) * DEPTH, :], twice, NN)
        squares += jnp.sum(center * center, axis=0, keepdims=True)
    rstd = lax.rsqrt(squares * (1.0 / DIM) + EPS)
    rstd = jnp.broadcast_to(rstd, (LAT, LANES))
    row = lax.broadcasted_iota(jnp.int32, (LAT, LANES), 0)
    lane = lax.broadcasted_iota(jnp.int32, (LAT, LANES), 1)
    high, low = split(rstd)
    piece = lat.astype(F32)
    spare = (lane >= ROWS * (1 - c)) & (lane < ROWS * (1 - c) + LAT)
    for k in range(3):
        turn = (ROWS * (1 - c) - LAT * c - LAT * k + 2 * LANES) % LANES
        piece = jnp.where(spare & (row == k), pltpu.roll(high, turn, 1), piece)
        piece = jnp.where(spare & (row == k + 3), pltpu.roll(low, turn, 1), piece)
    slots[z, c, at] = piece.astype(BF16)
    lat_plane = spread_plane(slots)

    for copy in w_b:
        copy.wait_recv()
    added = y_in[0].astype(F32)
    for k in range(1, 8):
        added += y_in[k].astype(F32)
    weights[place, :] = added.astype(BF16)
    w_g = [push(weights.at[place], weights.at[place], device) for device in a_peers]

    for copy in lat_plane:
        copy.wait_recv()
    lat_rest = spread_rest(slots)
    lat_c = [hand_over(slots, 0)]

    for copy in w_g:
        copy.wait_recv()

    wide_m = lax.broadcasted_iota(jnp.int32, (MCOLS, HD), 1)
    terms = [
        dot(wout_v[:, h * HD : (h + 1) * HD], weights[2 * WID + h * HD : 2 * WID + (h + 1) * HD, :], NN)
        for h in range(HEADS)
    ]
    m_in[0, :, 0:HD] = jnp.where(wide_m < LAT, terms[0], pltpu.roll(terms[1], LAT, 1)).astype(BF16)
    m_in[0, :, HD:LANES] = jnp.where(wide_m < LAT, terms[2], terms[0] + terms[1] + terms[2]).astype(BF16)
    m_move = push(m_in.at[0], m_in.at[1], m_peer)

    lane_t = lax.broadcasted_iota(jnp.int32, (1, HD), 1)
    lane_c = lax.broadcasted_iota(jnp.int32, (1, CHUNK), 1)
    tail_row = lax.broadcasted_iota(jnp.int32, (16, CHUNK), 0)

    def prepare(k, g0, g1):
        for i in range(4):
            n = 4 * k + i
            lats, scales = [], []
            for zz in range(2):
                near = slots[zz, 0, (g1 if zz else g0) * 4 + i]
                far = slots[zz, 1, (g1 if zz else g0) * 4 + i]
                middle = jnp.where(lane_t < LAT, near[:, HD:].astype(F32), far[:, :HD].astype(F32))
                lats += [near[:, :HD].astype(F32), middle, far[:, HD:].astype(F32)]
                sl = near[0:16, HD:].astype(F32)
                sr = far[0:16, :HD].astype(F32)
                sl = sl[0:3] + sl[3:6]
                sr = sr[0:3] + sr[3:6]
                tl = pltpu.roll(sl, LAT, 1)
                tr = pltpu.roll(sr, LAT, 1)
                scales += [
                    jnp.where(lane_t < LAT, tl[0:1], sl[1:2]),
                    jnp.where(lane_t < LAT, tl[2:3], tr[0:1]),
                    jnp.where(lane_t < LAT, sr[1:2], tr[2:3]),
                ]
            lat_c32 = jnp.concatenate(lats, axis=1)
            scale_row = jnp.concatenate(scales, axis=1)
            lat_cb = lat_c32.astype(BF16)
            start = jnp.where(lane_c < 384, (i * 8 + g0 * 2) * ROWS, (32 + g1 * 8 + i * 2) * ROWS - 384)
            token = lane_c + start
            hit = jnp.where(origin == token, 1.0, 0.0).astype(BF16)
            latq[0:ROWS, 0:LAT] += dot(hit, lat_cb, NT)
            scaled = lat_c32 * scale_row
            vals[n, 0:LAT, :] = scaled.astype(BF16)
            vals[n, LAT:FEAT, :] = jnp.where(tail_row == 0, 1.0, 0.0).astype(BF16)
            high, low = split(1.0 / scale_row)
            spread = jnp.where(tail_row == 0, high, 0.0)
            spread = jnp.where(tail_row == 1, low, spread)
            lat_x = jnp.concatenate([lat_cb, spread.astype(BF16)], axis=0)
            for h in range(HEADS):
                raw = dot(weights[WID + h * HD : WID + (h + 1) * HD, 0:FEAT], lat_x, NN)
                power = jnp.mean(raw * raw, axis=0, keepdims=True)
                inv = lax.rsqrt(power * (scale_row * scale_row) + EPS)
                ih, il = split(inv)
                tail = jnp.where((tail_row == 0) | (tail_row == 2), ih, 0.0)
                tail = jnp.where(tail_row == 1, il, tail)
                keys[h, n, 0:LAT, :] = (scaled * inv).astype(BF16)
                keys[h, n, LAT:FEAT, :] = tail.astype(BF16)

    for k in range(4):
        for copy in lat_c[k]:
            copy.wait_recv()
        prepare(k, (y + 4 - k) % 4, (x + 4 - k) % 4)
        if k == 0:
            for j in range(1, 4):
                for copy in lat_rest[j - 1]:
                    copy.wait_recv()
                lat_c.append(hand_over(slots, j))
        if k == 2:
            m_move.wait_recv()
            m_slots[z, c, at] = m_in[1]
            m_plane = spread_plane(m_slots)

    rows = latq[0:ROWS, :].astype(BF16)
    lat_out[...] = latq[...].T[0:LAT, 0:ROWS].astype(BF16)
    twice = (latq[0:ROWS, :] + pltpu.roll(latq[0:ROWS, :], LAT, 1)).astype(BF16)
    squares = jnp.zeros((ROWS, 1), F32)
    for k in range(PARTS):
        center = dot(twice, centred[:, k * DEPTH : (k + 1) * DEPTH], NN)
        squares += jnp.sum(center * center, axis=1, keepdims=True)
    rstd = lax.rsqrt(squares * (1.0 / DIM) + EPS)
    unit = jnp.where(lax.broadcasted_iota(jnp.int32, (16, HD), 1) == LAT, 1.0, 0.0).astype(BF16)
    lane_q = lax.broadcasted_iota(jnp.int32, (ROWS, HD), 1)
    for h in range(HEADS):
        wq = weights[h * HD : (h + 1) * HD, :]
        wk = weights[WID + h * HD : WID + (h + 1) * HD, :]
        raw = rstd * dot(rows, wq, NT) + dot(unit, wq, NT)[0:1, :]
        q = raw * lax.rsqrt(jnp.mean(raw * raw, axis=1, keepdims=True) + EPS) * qg_v[...]
        high, low = split(q * kg_v[...] * (LOG2E / HD**0.5))
        folded = dot(high.astype(BF16), wk, NN) + dot(low.astype(BF16), wk, NN)
        bias_high, bias_low = split(folded[:, LAT : LAT + 1])
        value = jnp.where(lane_q < LAT, folded, 0.0)
        value = jnp.where((lane_q == LAT) | (lane_q == LAT + 1), bias_high, value)
        value = jnp.where(lane_q == LAT + 2, bias_low, value)
        queries[h] = value.astype(BF16)

    scores = [s_even, s_odd]
    running[...] = jnp.full_like(running, -jnp.inf)
    accum[...] = jnp.zeros_like(accum)

    def score(n, h, most):
        part = dot(queries[h][:, 0:FEAT], keys[h, n], NN)
        scores[h % 2][n] = part
        for k in range(CHUNK // HD):
            most = jnp.maximum(most, part[:, k * HD : (k + 1) * HD])
        return most

    def weigh(n, h, most):
        w = jnp.concatenate(
            [jnp.exp2(scores[h % 2][n, :, k * HD : (k + 1) * HD] - most).astype(BF16) for k in range(CHUNK // HD)],
            axis=1,
        )
        return dot(w, vals[n], NT)

    most = running[0]
    for n in range(CHUNKS):
        most = score(n, 0, most)
    running[0] = most
    mixed = []
    for h in range(HEADS):
        top[h] = jnp.broadcast_to(jnp.max(running[h], axis=1, keepdims=True), (ROWS, HD))

        most = top[h]
        added = accum[h, :, 0:FEAT]
        if h + 1 < HEADS:
            following = running[h + 1]
        for n in range(CHUNKS):
            if h == 0 and n == CHUNKS // 2:
                for copy in m_plane:
                    copy.wait_recv()
                m_rest = spread_rest(m_slots)
            if h + 1 < HEADS:
                following = score(n, h + 1, following)
            added += weigh(n, h, most)
        accum[h, :, 0:FEAT] = added
        if h + 1 < HEADS:
            running[h + 1] = following
        mixed.append(accum[h] / accum[h, :, LAT : LAT + 1])
        if h == 1:
            first[t] = jnp.where(lane_q < LAT, mixed[0], pltpu.roll(mixed[1], LAT, 1)).astype(BF16)
            o_first = [push(first.at[t], first.at[t], device) for device in tp_peers]
    lower = pltpu.roll(mixed[2][ROWS // 2 :, :], LAT, 1)
    second[t] = jnp.where(lane_q[0 : ROWS // 2] < LAT, mixed[2][0 : ROWS // 2, :], lower).astype(BF16)
    o_second = [push(second.at[t], second.at[t], device) for device in tp_peers]

    m_c = list(hand_over(m_slots, 0))
    for k in range(1, 4):
        for copy in m_rest[k - 1]:
            copy.wait_recv()
        m_c += hand_over(m_slots, k)
    for copy in m_c:
        copy.wait_recv()
    for slot in range(64):
        zz, cc, outer, step = slot // 32, (slot // 16) % 2, (slot // 4) % 4, slot % 4
        xx, yy = (outer, step) if zz else (step, outer)
        source_tp, column = 2 * zz + xx // 2, ((xx % 2) * 8 + yy * 2 + 1 - cc) * MCOLS
        assembled[source_tp, pl.ds(column, MCOLS), :] = m_slots[zz, cc, outer * 4 + step]
    quarter = pl.ds(pl.multiple_of(t * QUARTER, QUARTER), QUARTER)
    embedded = dot(rows[:, 0:LAT], emb_v[:, quarter], NN)
    for copy in o_first:
        copy.wait_recv()
    total = dot(first[0], assembled[0, :, 0:HD], NT)
    for k in range(1, 4):
        total += dot(first[k], assembled[k, :, 0:HD], NT)
    for copy in o_second:
        copy.wait_recv()
    one = jnp.where(lane_q == LAT, 1.0, 0.0)
    for k in range(4):
        packed = second[k].astype(F32)
        whole = jnp.concatenate([packed, pltpu.roll(packed, LAT, 1)], axis=0)
        whole = jnp.where(lane_q < LAT, whole, one).astype(BF16)
        total += dot(whole, assembled[k, :, HD:LANES], NT)
    block_out[...] = (embedded + gate_v[:, quarter] * total).astype(BF16)
    for copy in sent:
        copy.wait_send()


def leave(lat_ref, block_ref, lat_to, block_to):
    lat_to[...] = lat_ref[...]
    block_to[...] = block_ref[...]


COPIES = 73
LOADS = 18


def per_device(
    pixels, w_encode, w_latent, source_row, w_embed, mod_shift, mod_scale, gate, q_gain, k_gain, w_qkv, w_out
):
    operands = (
        pixels, w_encode, w_latent.T, source_row.reshape(1, ROWS), w_embed, mod_shift.reshape(1, DIM),
        mod_scale.reshape(1, DIM), gate.reshape(1, DIM), q_gain.reshape(1, HD), k_gain.reshape(1, HD), w_qkv, w_out.T,
    )
    vmem = pltpu.VMEM
    scratch = [
        vmem((PARTS, ROWS, DEPTH), BF16),
        vmem((PARTS, DEPTH, 512), BF16),
        vmem((LAT, 512), BF16),
        vmem((1, ROWS), jnp.int32),
        vmem((LAT, DIM), BF16),
        vmem((1, DIM), F32),
        vmem((1, DIM), F32),
        vmem((1, DIM), F32),
        vmem((1, HD), F32),
        vmem((1, HD), F32),
        vmem((3, MCOLS, WID), BF16),
        vmem((MCOLS, WID), BF16),
        vmem((HD, LANES), F32),
        vmem((HD, DIM), BF16),
        vmem((DIM, HD), BF16),
        vmem((3 * WID, HD), BF16),
        vmem((4, LAT, LANES), BF16),
        vmem((8, 144, HD), BF16),
        vmem((8, 144, HD), BF16),
        vmem((3 * WID, HD), BF16),
        vmem((2, 2, 16, LAT, LANES), BF16),
        vmem((2, MCOLS, LANES), BF16),
        vmem((2, 2, 16, MCOLS, LANES), BF16),
        vmem((LANES, HD), F32),
        vmem((HD, LANES), F32),
        vmem((HEADS, ROWS, HD), BF16),
        vmem((HEADS, CHUNKS, FEAT, CHUNK), BF16),
        vmem((CHUNKS, FEAT, CHUNK), BF16),
        vmem((CHUNKS, ROWS, CHUNK), F32),
        vmem((CHUNKS, ROWS, CHUNK), F32),
        vmem((HEADS, ROWS, HD), F32),
        vmem((HEADS, ROWS, HD), F32),
        vmem((HEADS, ROWS, HD), F32),
        vmem((4, ROWS, HD), BF16),
        vmem((4, ROWS // 2, HD), BF16),
        vmem((4, QUARTER, LANES), BF16),
        pltpu.SemaphoreType.DMA((LOADS,)),
        pltpu.SemaphoreType.DMA((COPIES,)),
        pltpu.SemaphoreType.DMA((COPIES,)),
    ]
    lat, out = pl.pallas_call(
        kernel,
        out_shape=(jax.ShapeDtypeStruct((LAT, ROWS), BF16), jax.ShapeDtypeStruct((ROWS, QUARTER), BF16)),
        in_specs=[pl.BlockSpec(memory_space=pl.ANY)] * len(operands),
        out_specs=(pl.BlockSpec(memory_space=pltpu.VMEM), pl.BlockSpec(memory_space=pltpu.VMEM)),
        scratch_shapes=scratch,
        compiler_params=pltpu.CompilerParams(collective_id=0, has_side_effects=True, vmem_limit_bytes=VMEM_LIMIT),
    )(*operands)
    lat, out = pl.pallas_call(
        leave,
        out_shape=(jax.ShapeDtypeStruct((LAT, ROWS), BF16), jax.ShapeDtypeStruct((ROWS, QUARTER), BF16)),
    )(lat, out)
    return lat.T, out


def solution(mesh):
    placed = (
        P("sec", None), P(None, "tp"), P("tp", None), P("sec"), P(), P(), P(), P(), P(), P(),
        P(None, "sec", "tp"), P("tp", "sec"),
    )
    return jax.shard_map(
        per_device, mesh=mesh, in_specs=placed, out_specs=(P("sec", None), P("sec", "tp")), check_vma=False
    )
```

```python
import jax
import jax.numpy as jnp
from jax import lax
from jax.experimental import pallas as pl
from jax.experimental.pallas import tpu as pltpu
from jax.sharding import PartitionSpec as P

MESH = pl.DeviceIdType.MESH
HD = 128
HEADS = 3
LAT = 64
ROWS = 192
LANES = 256
WID = HEADS * HD
DIM = 3072
FEAT = 80
CHUNK = 768
CHUNKS = 16
MCOLS = 48
QUARTER = 768
PARTS = 4
DEPTH = DIM // PARTS
F32 = jnp.float32
BF16 = jnp.bfloat16
NT = (((1,), (1,)), ((), ()))
NN = (((1,), (0,)), ((), ()))
TN = (((0,), (0,)), ((), ()))
EPS = 1e-6
LOG2E = 1.4426950408889634
VMEM_LIMIT = 58 * 1024 * 1024


def dot(a, b, dims):
    return lax.dot_general(a, b, dims, preferred_element_type=F32)


def split(value):
    high = value.astype(BF16).astype(F32)
    return high, value - high


def kernel(
    pixels, w_encode, w_latent, source, w_embed, mod_shift, mod_scale, gate, q_gain, k_gain, w_qkv, w_out,
    lat_out, block_out,
    pix_v, enc_v, wlat_v, src_v, emb_v, shift_v, scale_v, gate_v, qg_v, kg_v, wqkv_v, wout_v,
    wide, centred, centred_t, wp, lat_in, x_in, y_in, weights,
    slots, m_in, m_slots, latq, square, queries, keys, vals, s_even, s_odd, running, top, accum,
    packed, assembled,
    load, send, recv,
):
    s = lax.axis_index("sec")
    t = lax.axis_index("tp")
    z = s // 32
    x = (s // 8) % 4
    y = (s // 2) % 4
    c = s % 2
    b = z * 4 + y
    at = z * (x * 4 + y) + (1 - z) * (y * 4 + x)
    sibling = {"sec": s + 1 - 2 * c}
    tp_peers = [{"tp": (t + k) % 4} for k in range(1, 4)]
    x_at = [(x + k) % 4 for k in range(1, 4)]
    x_peers = [{"sec": s + (xx - x) * 8} for xx in x_at]
    b_at = [(b + k) % 8 for k in range(1, 8)]
    b_peers = [{"sec": (bb // 4) * 32 + x * 8 + (bb % 4) * 2 + c} for bb in b_at]
    y_peers = [{"sec": s + ((y + k) % 4 - y) * 2} for k in range(1, 4)]
    cross_x = [{"sec": s + (1 - 2 * z) * 32 + (xx - x) * 8} for xx in x_at]
    inner = z * y + (1 - z) * x
    stride = 8 - 6 * z
    plane_peers = [{"sec": s + ((inner + k) % 4 - inner) * stride} for k in range(1, 4)]
    plane_peers += [
        {"sec": s + (1 - 2 * z) * 32 + ((inner + k) % 4 - inner) * stride} for k in range(4)
    ]
    m_peer = {"tp": s // 16, "sec": (t // 2) * 32 + (2 * (t % 2) + x % 2) * 8 + y * 2 + 1 - c}
    a = x * 2 + c
    a_at = [(a + k) % 8 for k in range(1, 8)]
    a_peers = [{"sec": z * 32 + (aa // 2) * 8 + y * 2 + aa % 2} for aa in a_at]

    sent = []
    used = [0]

    def push(src, dst, device):
        i = used[0]
        used[0] += 1
        copy = pltpu.make_async_remote_copy(
            src_ref=src, dst_ref=dst, send_sem=send.at[i], recv_sem=recv.at[i], device_id=device, device_id_type=MESH
        )
        copy.start()
        sent.append(copy)
        return copy

    def spread_plane(ref):
        return [push(ref.at[z, c, at], ref.at[z, c, at], device) for device in plane_peers]

    by_y = pl.ds(y * 4, 4)
    by_x = pl.ds(x * 4, 4)

    def spread_rest(ref):
        pairs = []
        for k in range(3):
            pairs.append(
                (
                    push(ref.at[0, c, by_y], ref.at[0, c, by_y], y_peers[k]),
                    push(ref.at[1, c, by_x], ref.at[1, c, by_x], x_peers[k]),
                )
            )
        return pairs

    def hand_over(ref, k):
        from_y = pl.ds(((y + 4 - k) % 4) * 4, 4)
        from_x = pl.ds(((x + 4 - k) % 4) * 4, 4)
        return (
            push(ref.at[0, c, from_y], ref.at[0, c, from_y], sibling),
            push(ref.at[1, c, from_x], ref.at[1, c, from_x], sibling),
        )

    barrier = pltpu.get_barrier_semaphore()
    greet = [m_peer] + tp_peers + b_peers + cross_x + a_peers
    for device in greet:
        pl.semaphore_signal(barrier, inc=1, device_id=device, device_id_type=MESH)

    loads = [0]

    def fetch(src, dst):
        copy = pltpu.make_async_copy(src, dst, load.at[loads[0]])
        loads[0] += 1
        copy.start()
        return copy

    early = [fetch(w_embed, emb_v), fetch(w_qkv, wqkv_v), fetch(mod_scale, scale_v), fetch(mod_shift, shift_v)]
    parts = []
    for k in range(PARTS):
        depth = pl.ds(k * DEPTH, DEPTH)
        parts.append((fetch(pixels.at[:, depth], pix_v.at[k]), fetch(w_encode.at[depth], enc_v.at[k])))
    wlat_load = fetch(w_latent, wlat_v)
    late = [
        fetch(source, src_v), fetch(gate, gate_v), fetch(q_gain, qg_v), fetch(k_gain, kg_v), fetch(w_out, wout_v)
    ]

    for copy in early:
        copy.wait()
    block = (3 * s) // 8 - s // 62
    base = pl.ds(pl.multiple_of(block * HD, HD), LANES)
    mean = jnp.mean(emb_v[...].astype(F32), axis=1, keepdims=True)
    wide[0:LAT, :] = (emb_v[:, base].astype(F32) - mean) * scale_v[:, base]
    wide[LAT:HD, :] = jnp.where(
        lax.broadcasted_iota(jnp.int32, (LAT, LANES), 0) < 2, jnp.broadcast_to(shift_v[:, base], (LAT, LANES)), 0.0
    )
    offset = s * MCOLS - block * HD
    turned = pltpu.roll(wide[...], (LANES - offset) % LANES, 1)[:, 0:HD].T
    high, low = split(turned[0:MCOLS, :])
    high, low = high.astype(BF16), low.astype(BF16)
    for i in range(3):
        wp[i * WID : (i + 1) * WID, :] = (dot(wqkv_v[i], high, TN) + dot(wqkv_v[i], low, TN)).astype(BF16)

    high, low = split(emb_v[...].astype(F32) - mean)
    both_terms = jnp.concatenate([high, low], axis=0)
    centred[...] = both_terms.astype(BF16)
    centred_t[...] = both_terms.T.astype(BF16)

    total = jnp.zeros((ROWS, 512), F32)
    for k in range(PARTS):
        parts[k][0].wait()
        parts[k][1].wait()
        total += dot(pix_v[k], enc_v[k], NN)
    hidden = jax.nn.silu(total).astype(BF16)
    wlat_load.wait()
    wide[...] = jnp.zeros_like(wide)
    wide[0:LAT, 0:ROWS] = dot(wlat_v[...], hidden, NT)
    lat_in[t] = pltpu.roll(wide[0:LAT, :], LAT * c, 1).astype(BF16)

    for copy in late:
        copy.wait()
    square[...] = jnp.zeros_like(square)
    square[:, 0:ROWS] = jnp.broadcast_to(src_v[...].astype(F32), (HD, ROWS))
    origin = square[...].T[0:ROWS, 0:1].astype(jnp.int32)
    latq[...] = jnp.zeros_like(latq)
    place = pl.ds(pl.multiple_of(a * 144, 144), 144)

    pl.semaphore_wait(barrier, len(greet))
    lat_tp = [push(lat_in.at[t], lat_in.at[t], device) for device in tp_peers]

    w_x = []
    for k in range(7):
        w_x.append(push(wp.at[pl.ds(pl.multiple_of(a_at[k] * 144, 144), 144)], x_in.at[a], a_peers[k]))
    x_in[a] = wp[place, :]
    for copy in w_x:
        copy.wait_recv()
    added = x_in[0].astype(F32)
    for k in range(1, 8):
        added += x_in[k].astype(F32)
    y_in[b] = added.astype(BF16)
    w_b = [push(y_in.at[b], y_in.at[b], device) for device in b_peers]

    for copy in lat_tp:
        copy.wait_recv()
    summed = lat_in[0].astype(F32)
    for k in range(1, 4):
        summed += lat_in[k].astype(F32)
    lat = summed.astype(BF16)
    twice = jnp.concatenate([lat, lat], axis=0)
    squares = jnp.zeros((1, LANES), F32)
    for k in range(PARTS):
        center = dot(centred_t[k * DEPTH : (k + 1) * DEPTH, :], twice, NN)
        squares += jnp.sum(center * center, axis=0, keepdims=True)
    rstd = lax.rsqrt(squares * (1.0 / DIM) + EPS)
    rstd = jnp.broadcast_to(rstd, (LAT, LANES))
    row = lax.broadcasted_iota(jnp.int32, (LAT, LANES), 0)
    lane = lax.broadcasted_iota(jnp.int32, (LAT, LANES), 1)
    high, low = split(rstd)
    piece = lat.astype(F32)
    spare = (lane >= ROWS * (1 - c)) & (lane < ROWS * (1 - c) + LAT)
    for k in range(3):
        turn = (ROWS * (1 - c) - LAT * c - LAT * k + 2 * LANES) % LANES
        piece = jnp.where(spare & (row == k), pltpu.roll(high, turn, 1), piece)
        piece = jnp.where(spare & (row == k + 3), pltpu.roll(low, turn, 1), piece)
    slots[z, c, at] = piece.astype(BF16)
    lat_plane = spread_plane(slots)

    for copy in w_b:
        copy.wait_recv()
    added = y_in[0].astype(F32)
    for k in range(1, 8):
        added += y_in[k].astype(F32)
    weights[place, :] = added.astype(BF16)
    w_g = [push(weights.at[place], weights.at[place], device) for device in a_peers]

    for copy in lat_plane:
        copy.wait_recv()
    lat_rest = spread_rest(slots)
    lat_c = [hand_over(slots, 0)]

    for copy in w_g:
        copy.wait_recv()

    wide_m = lax.broadcasted_iota(jnp.int32, (MCOLS, HD), 1)
    terms = [
        dot(wout_v[:, h * HD : (h + 1) * HD], weights[2 * WID + h * HD : 2 * WID + (h + 1) * HD, :], NN)
        for h in range(HEADS)
    ]
    m_in[0, :, 0:HD] = jnp.where(wide_m < LAT, terms[0], pltpu.roll(terms[1], LAT, 1)).astype(BF16)
    m_in[0, :, HD:LANES] = jnp.where(wide_m < LAT, terms[2], terms[0] + terms[1] + terms[2]).astype(BF16)
    m_move = push(m_in.at[0], m_in.at[1], m_peer)

    lane_t = lax.broadcasted_iota(jnp.int32, (1, HD), 1)
    lane_c = lax.broadcasted_iota(jnp.int32, (1, CHUNK), 1)
    tail_row = lax.broadcasted_iota(jnp.int32, (16, CHUNK), 0)

    def prepare(k, g0, g1):
        for i in range(4):
            n = 4 * k + i
            lats, scales = [], []
            for zz in range(2):
                near = slots[zz, 0, (g1 if zz else g0) * 4 + i]
                far = slots[zz, 1, (g1 if zz else g0) * 4 + i]
                middle = jnp.where(lane_t < LAT, near[:, HD:].astype(F32), far[:, :HD].astype(F32))
                lats += [near[:, :HD].astype(F32), middle, far[:, HD:].astype(F32)]
                sl = near[0:16, HD:].astype(F32)
                sr = far[0:16, :HD].astype(F32)
                sl = sl[0:3] + sl[3:6]
                sr = sr[0:3] + sr[3:6]
                tl = pltpu.roll(sl, LAT, 1)
                tr = pltpu.roll(sr, LAT, 1)
                scales += [
                    jnp.where(lane_t < LAT, tl[0:1], sl[1:2]),
                    jnp.where(lane_t < LAT, tl[2:3], tr[0:1]),
                    jnp.where(lane_t < LAT, sr[1:2], tr[2:3]),
                ]
            lat_c32 = jnp.concatenate(lats, axis=1)
            scale_row = jnp.concatenate(scales, axis=1)
            lat_cb = lat_c32.astype(BF16)
            start = jnp.where(lane_c < 384, (i * 8 + g0 * 2) * ROWS, (32 + g1 * 8 + i * 2) * ROWS - 384)
            token = lane_c + start
            hit = jnp.where(origin == token, 1.0, 0.0).astype(BF16)
            latq[0:ROWS, 0:LAT] += dot(hit, lat_cb, NT)
            scaled = lat_c32 * scale_row
            vals[n, 0:LAT, :] = scaled.astype(BF16)
            vals[n, LAT:FEAT, :] = jnp.where(tail_row == 0, 1.0, 0.0).astype(BF16)
            high, low = split(1.0 / scale_row)
            spread = jnp.where(tail_row == 0, high, 0.0)
            spread = jnp.where(tail_row == 1, low, spread)
            lat_x = jnp.concatenate([lat_cb, spread.astype(BF16)], axis=0)
            for h in range(HEADS):
                raw = dot(weights[WID + h * HD : WID + (h + 1) * HD, 0:FEAT], lat_x, NN)
                power = jnp.mean(raw * raw, axis=0, keepdims=True)
                inv = lax.rsqrt(power * (scale_row * scale_row) + EPS)
                ih, il = split(inv)
                tail = jnp.where((tail_row == 0) | (tail_row == 2), ih, 0.0)
                tail = jnp.where(tail_row == 1, il, tail)
                keys[h, n, 0:LAT, :] = (scaled * inv).astype(BF16)
                keys[h, n, LAT:FEAT, :] = tail.astype(BF16)

    for k in range(4):
        for copy in lat_c[k]:
            copy.wait_recv()
        prepare(k, (y + 4 - k) % 4, (x + 4 - k) % 4)
        if k == 0:
            for j in range(1, 4):
                for copy in lat_rest[j - 1]:
                    copy.wait_recv()
                lat_c.append(hand_over(slots, j))
        if k == 1:
            m_move.wait_recv()
            m_slots[z, c, at] = m_in[1]
            m_plane = spread_plane(m_slots)

    rows = latq[0:ROWS, :].astype(BF16)
    lat_out[...] = latq[...].T[0:LAT, 0:ROWS].astype(BF16)
    twice = (latq[0:ROWS, :] + pltpu.roll(latq[0:ROWS, :], LAT, 1)).astype(BF16)
    squares = jnp.zeros((ROWS, 1), F32)
    for k in range(PARTS):
        center = dot(twice, centred[:, k * DEPTH : (k + 1) * DEPTH], NN)
        squares += jnp.sum(center * center, axis=1, keepdims=True)
    rstd = lax.rsqrt(squares * (1.0 / DIM) + EPS)
    unit = jnp.where(lax.broadcasted_iota(jnp.int32, (16, HD), 1) == LAT, 1.0, 0.0).astype(BF16)
    lane_q = lax.broadcasted_iota(jnp.int32, (ROWS, HD), 1)
    for h in range(HEADS):
        wq = weights[h * HD : (h + 1) * HD, :]
        wk = weights[WID + h * HD : WID + (h + 1) * HD, :]
        raw = rstd * dot(rows, wq, NT) + dot(unit, wq, NT)[0:1, :]
        q = raw * lax.rsqrt(jnp.mean(raw * raw, axis=1, keepdims=True) + EPS) * qg_v[...]
        high, low = split(q * kg_v[...] * (LOG2E / HD**0.5))
        folded = dot(high.astype(BF16), wk, NN) + dot(low.astype(BF16), wk, NN)
        bias_high, bias_low = split(folded[:, LAT : LAT + 1])
        value = jnp.where(lane_q < LAT, folded, 0.0)
        value = jnp.where((lane_q == LAT) | (lane_q == LAT + 1), bias_high, value)
        value = jnp.where(lane_q == LAT + 2, bias_low, value)
        queries[h] = value.astype(BF16)

    scores = [s_even, s_odd]
    running[...] = jnp.full_like(running, -jnp.inf)
    accum[...] = jnp.zeros_like(accum)

    def score(n, h, most):
        part = dot(queries[h][:, 0:FEAT], keys[h, n], NN)
        scores[h % 2][n] = part
        for k in range(CHUNK // HD):
            most = jnp.maximum(most, part[:, k * HD : (k + 1) * HD])
        return most

    def weigh(n, h, most):
        w = jnp.concatenate(
            [jnp.exp2(scores[h % 2][n, :, k * HD : (k + 1) * HD] - most).astype(BF16) for k in range(CHUNK // HD)],
            axis=1,
        )
        return dot(w, vals[n], NT)

    most = running[0]
    for n in range(CHUNKS):
        most = score(n, 0, most)
    running[0] = most
    o_heads = []
    for h in range(HEADS):
        top[h] = jnp.broadcast_to(jnp.max(running[h], axis=1, keepdims=True), (ROWS, HD))

        most = top[h]
        added = accum[h, :, 0:FEAT]
        if h + 1 < HEADS:
            following = running[h + 1]
        for n in range(CHUNKS):
            if h == 0 and n == 4:
                for copy in m_plane:
                    copy.wait_recv()
                m_rest = spread_rest(m_slots)
                m_c = list(hand_over(m_slots, 0))
            if h == 2 and n == CHUNKS // 2:
                for j in range(1, 4):
                    for copy in m_rest[j - 1]:
                        copy.wait_recv()
                    m_c += hand_over(m_slots, j)
            if h + 1 < HEADS:
                following = score(n, h + 1, following)
            added += weigh(n, h, most)
        accum[h, :, 0:FEAT] = added
        if h + 1 < HEADS:
            running[h + 1] = following
        mixed = accum[h] / accum[h, :, LAT : LAT + 1]
        lower = pltpu.roll(mixed[ROWS // 2 :, :], LAT, 1)
        packed[h, t] = jnp.where(lane_q[0 : ROWS // 2] < LAT, mixed[0 : ROWS // 2, :], lower).astype(BF16)
        o_heads.append([push(packed.at[h, t], packed.at[h, t], device) for device in tp_peers])

    for copy in m_c:
        copy.wait_recv()
    for slot in range(64):
        zz, cc, outer, step = slot // 32, (slot // 16) % 2, (slot // 4) % 4, slot % 4
        xx, yy = (outer, step) if zz else (step, outer)
        source_tp, column = 2 * zz + xx // 2, ((xx % 2) * 8 + yy * 2 + 1 - cc) * MCOLS
        assembled[source_tp, pl.ds(column, MCOLS), :] = m_slots[zz, cc, outer * 4 + step]
    quarter = pl.ds(pl.multiple_of(t * QUARTER, QUARTER), QUARTER)
    embedded = dot(rows[:, 0:LAT], emb_v[:, quarter], NN)
    one = jnp.where(lane_q == LAT, 1.0, 0.0)

    def unpacked(h, k):
        both = packed[h, k].astype(F32)
        return jnp.concatenate([both, pltpu.roll(both, LAT, 1)], axis=0)

    for copy in o_heads[0] + o_heads[1]:
        copy.wait_recv()
    total = jnp.zeros((ROWS, QUARTER), F32)
    for k in range(4):
        whole = jnp.where(lane_q < LAT, unpacked(0, k), pltpu.roll(unpacked(1, k), LAT, 1)).astype(BF16)
        total += dot(whole, assembled[k, :, 0:HD], NT)
    for copy in o_heads[2]:
        copy.wait_recv()
    for k in range(4):
        whole = jnp.where(lane_q < LAT, unpacked(2, k), one).astype(BF16)
        total += dot(whole, assembled[k, :, HD:LANES], NT)
    block_out[...] = (embedded + gate_v[:, quarter] * total).astype(BF16)
    for copy in sent:
        copy.wait_send()


def leave(lat_ref, block_ref, lat_to, block_to):
    lat_to[...] = lat_ref[...]
    block_to[...] = block_ref[...]


COPIES = 76
LOADS = 18


def per_device(
    pixels, w_encode, w_latent, source_row, w_embed, mod_shift, mod_scale, gate, q_gain, k_gain, w_qkv, w_out
):
    operands = (
        pixels, w_encode, w_latent.T, source_row.reshape(1, ROWS), w_embed, mod_shift.reshape(1, DIM),
        mod_scale.reshape(1, DIM), gate.reshape(1, DIM), q_gain.reshape(1, HD), k_gain.reshape(1, HD), w_qkv, w_out.T,
    )
    vmem = pltpu.VMEM
    scratch = [
        vmem((PARTS, ROWS, DEPTH), BF16),
        vmem((PARTS, DEPTH, 512), BF16),
        vmem((LAT, 512), BF16),
        vmem((1, ROWS), jnp.int32),
        vmem((LAT, DIM), BF16),
        vmem((1, DIM), F32),
        vmem((1, DIM), F32),
        vmem((1, DIM), F32),
        vmem((1, HD), F32),
        vmem((1, HD), F32),
        vmem((3, MCOLS, WID), BF16),
        vmem((MCOLS, WID), BF16),
        vmem((HD, LANES), F32),
        vmem((HD, DIM), BF16),
        vmem((DIM, HD), BF16),
        vmem((3 * WID, HD), BF16),
        vmem((4, LAT, LANES), BF16),
        vmem((8, 144, HD), BF16),
        vmem((8, 144, HD), BF16),
        vmem((3 * WID, HD), BF16),
        vmem((2, 2, 16, LAT, LANES), BF16),
        vmem((2, MCOLS, LANES), BF16),
        vmem((2, 2, 16, MCOLS, LANES), BF16),
        vmem((LANES, HD), F32),
        vmem((HD, LANES), F32),
        vmem((HEADS, ROWS, HD), BF16),
        vmem((HEADS, CHUNKS, FEAT, CHUNK), BF16),
        vmem((CHUNKS, FEAT, CHUNK), BF16),
        vmem((CHUNKS, ROWS, CHUNK), F32),
        vmem((CHUNKS, ROWS, CHUNK), F32),
        vmem((HEADS, ROWS, HD), F32),
        vmem((HEADS, ROWS, HD), F32),
        vmem((HEADS, ROWS, HD), F32),
        vmem((HEADS, 4, ROWS // 2, HD), BF16),
        vmem((4, QUARTER, LANES), BF16),
        pltpu.SemaphoreType.DMA((LOADS,)),
        pltpu.SemaphoreType.DMA((COPIES,)),
        pltpu.SemaphoreType.DMA((COPIES,)),
    ]
    lat, out = pl.pallas_call(
        kernel,
        out_shape=(jax.ShapeDtypeStruct((LAT, ROWS), BF16), jax.ShapeDtypeStruct((ROWS, QUARTER), BF16)),
        in_specs=[pl.BlockSpec(memory_space=pl.ANY)] * len(operands),
        out_specs=(pl.BlockSpec(memory_space=pltpu.VMEM), pl.BlockSpec(memory_space=pltpu.VMEM)),
        scratch_shapes=scratch,
        compiler_params=pltpu.CompilerParams(collective_id=0, has_side_effects=True, vmem_limit_bytes=VMEM_LIMIT),
    )(*operands)
    lat, out = pl.pallas_call(
        leave,
        out_shape=(jax.ShapeDtypeStruct((LAT, ROWS), BF16), jax.ShapeDtypeStruct((ROWS, QUARTER), BF16)),
    )(lat, out)
    return lat.T, out


def solution(mesh):
    placed = (
        P("sec", None), P(None, "tp"), P("tp", None), P("sec"), P(), P(), P(), P(), P(), P(),
        P(None, "sec", "tp"), P("tp", "sec"),
    )
    return jax.shard_map(
        per_device, mesh=mesh, in_specs=placed, out_specs=(P("sec", None), P("sec", "tp")), check_vma=False
    )
```

```python
import jax
import jax.numpy as jnp
from jax import lax
from jax.experimental import pallas as pl
from jax.experimental.pallas import tpu as pltpu
from jax.sharding import PartitionSpec as P

MESH = pl.DeviceIdType.MESH
HD = 128
HEADS = 3
LAT = 64
ROWS = 192
LANES = 256
WID = HEADS * HD
DIM = 3072
FEAT = 80
CHUNK = 768
CHUNKS = 16
MCOLS = 48
QUARTER = 768
PARTS = 4
DEPTH = DIM // PARTS
F32 = jnp.float32
BF16 = jnp.bfloat16
NT = (((1,), (1,)), ((), ()))
NN = (((1,), (0,)), ((), ()))
TN = (((0,), (0,)), ((), ()))
EPS = 1e-6
WPACK = 640
SHARE = WPACK // 8
LOG2E = 1.4426950408889634
VMEM_LIMIT = 58 * 1024 * 1024


def dot(a, b, dims):
    return lax.dot_general(a, b, dims, preferred_element_type=F32)


def split(value):
    high = value.astype(BF16).astype(F32)
    return high, value - high


def kernel(
    pixels, w_encode, w_latent, source, w_embed, mod_shift, mod_scale, gate, q_gain, k_gain, w_qkv, w_out,
    lat_out, block_out,
    pix_v, enc_v, wlat_v, src_v, emb_v, shift_v, scale_v, gate_v, qg_v, kg_v, wqkv_v, wout_v,
    wide, centred, centred_t, wp, lat_in, x_in, y_in, wsum, weights,
    slots, m_in, m_slots, latq, square, queries, keys, vals, s_even, s_odd, running, top, accum,
    packed, assembled,
    load, send, recv,
):
    s = lax.axis_index("sec")
    t = lax.axis_index("tp")
    z = s // 32
    x = (s // 8) % 4
    y = (s // 2) % 4
    c = s % 2
    b = z * 4 + y
    at = z * (x * 4 + y) + (1 - z) * (y * 4 + x)
    sibling = {"sec": s + 1 - 2 * c}
    tp_peers = [{"tp": (t + k) % 4} for k in range(1, 4)]
    x_at = [(x + k) % 4 for k in range(1, 4)]
    x_peers = [{"sec": s + (xx - x) * 8} for xx in x_at]
    b_at = [(b + k) % 8 for k in range(1, 8)]
    b_peers = [{"sec": (bb // 4) * 32 + x * 8 + (bb % 4) * 2 + c} for bb in b_at]
    y_peers = [{"sec": s + ((y + k) % 4 - y) * 2} for k in range(1, 4)]
    cross_x = [{"sec": s + (1 - 2 * z) * 32 + (xx - x) * 8} for xx in x_at]
    inner = z * y + (1 - z) * x
    stride = 8 - 6 * z
    plane_peers = [{"sec": s + ((inner + k) % 4 - inner) * stride} for k in range(1, 4)]
    plane_peers += [
        {"sec": s + (1 - 2 * z) * 32 + ((inner + k) % 4 - inner) * stride} for k in range(4)
    ]
    m_peer = {"tp": s // 16, "sec": (t // 2) * 32 + (2 * (t % 2) + x % 2) * 8 + y * 2 + 1 - c}
    a = x * 2 + c
    a_at = [(a + k) % 8 for k in range(1, 8)]
    a_peers = [{"sec": z * 32 + (aa // 2) * 8 + y * 2 + aa % 2} for aa in a_at]

    sent = []
    used = [0]

    def push(src, dst, device):
        i = used[0]
        used[0] += 1
        copy = pltpu.make_async_remote_copy(
            src_ref=src, dst_ref=dst, send_sem=send.at[i], recv_sem=recv.at[i], device_id=device, device_id_type=MESH
        )
        copy.start()
        sent.append(copy)
        return copy

    def spread_plane(ref):
        return [push(ref.at[z, c, at], ref.at[z, c, at], device) for device in plane_peers]

    by_y = pl.ds(y * 4, 4)
    by_x = pl.ds(x * 4, 4)

    def spread_rest(ref):
        pairs = []
        for k in range(3):
            pairs.append(
                (
                    push(ref.at[0, c, by_y], ref.at[0, c, by_y], y_peers[k]),
                    push(ref.at[1, c, by_x], ref.at[1, c, by_x], x_peers[k]),
                )
            )
        return pairs

    def hand_over(ref, k):
        from_y = pl.ds(((y + 4 - k) % 4) * 4, 4)
        from_x = pl.ds(((x + 4 - k) % 4) * 4, 4)
        return (
            push(ref.at[0, c, from_y], ref.at[0, c, from_y], sibling),
            push(ref.at[1, c, from_x], ref.at[1, c, from_x], sibling),
        )

    barrier = pltpu.get_barrier_semaphore()
    greet = [m_peer] + tp_peers + b_peers + cross_x + a_peers
    for device in greet:
        pl.semaphore_signal(barrier, inc=1, device_id=device, device_id_type=MESH)

    loads = [0]

    def fetch(src, dst):
        copy = pltpu.make_async_copy(src, dst, load.at[loads[0]])
        loads[0] += 1
        copy.start()
        return copy

    early = [fetch(w_embed, emb_v), fetch(w_qkv, wqkv_v), fetch(mod_scale, scale_v), fetch(mod_shift, shift_v)]
    parts = []
    for k in range(PARTS):
        depth = pl.ds(k * DEPTH, DEPTH)
        parts.append((fetch(pixels.at[:, depth], pix_v.at[k]), fetch(w_encode.at[depth], enc_v.at[k])))
    wlat_load = fetch(w_latent, wlat_v)
    late = [
        fetch(source, src_v), fetch(gate, gate_v), fetch(q_gain, qg_v), fetch(k_gain, kg_v), fetch(w_out, wout_v)
    ]

    for copy in early:
        copy.wait()
    block = (3 * s) // 8 - s // 62
    base = pl.ds(pl.multiple_of(block * HD, HD), LANES)
    mean = jnp.mean(emb_v[...].astype(F32), axis=1, keepdims=True)
    wide[0:LAT, :] = (emb_v[:, base].astype(F32) - mean) * scale_v[:, base]
    wide[LAT:HD, :] = jnp.where(
        lax.broadcasted_iota(jnp.int32, (LAT, LANES), 0) < 2, jnp.broadcast_to(shift_v[:, base], (LAT, LANES)), 0.0
    )
    offset = s * MCOLS - block * HD
    rolled = pltpu.roll(wide[...], (LANES - offset) % LANES, 1)[:, 0:HD]
    high, low = split(rolled.T[0:MCOLS, :])
    high, low = high.astype(BF16), low.astype(BF16)
    shift_high, shift_low = split(rolled[LAT : LAT + 16, 0:MCOLS])
    shift_high, shift_low = shift_high.astype(BF16), shift_low.astype(BF16)
    lane_p = lax.broadcasted_iota(jnp.int32, (ROWS, HD), 1)
    row_p = lax.broadcasted_iota(jnp.int32, (LAT, HD), 0)
    biases = jnp.zeros((LAT, HD), F32)
    for i in range(3):
        part = dot(wqkv_v[i], high, TN) + dot(wqkv_v[i], low, TN)
        wp[i * ROWS : (i + 1) * ROWS, :] = jnp.where(
            lane_p < LAT, part[0:ROWS, :], pltpu.roll(part[ROWS:WID, :], LAT, 1)
        ).astype(BF16)
        bias = dot(shift_high, wqkv_v[i], NN) + dot(shift_low, wqkv_v[i], NN)
        for j in range(HEADS):
            biases = jnp.where(row_p == HEADS * i + j, bias[0:1, j * HD : (j + 1) * HD], biases)
    wp[WPACK - LAT : WPACK, :] = biases.astype(BF16)

    high, low = split(emb_v[...].astype(F32) - mean)
    both_terms = jnp.concatenate([high, low], axis=0)
    centred[...] = both_terms.astype(BF16)
    centred_t[...] = both_terms.T.astype(BF16)

    total = jnp.zeros((ROWS, 512), F32)
    for k in range(PARTS):
        parts[k][0].wait()
        parts[k][1].wait()
        total += dot(pix_v[k], enc_v[k], NN)
    hidden = jax.nn.silu(total).astype(BF16)
    wlat_load.wait()
    wide[...] = jnp.zeros_like(wide)
    wide[0:LAT, 0:ROWS] = dot(wlat_v[...], hidden, NT)
    lat_in[t] = pltpu.roll(wide[0:LAT, :], LAT * c, 1).astype(BF16)

    for copy in late:
        copy.wait()
    square[...] = jnp.zeros_like(square)
    square[:, 0:ROWS] = jnp.broadcast_to(src_v[...].astype(F32), (HD, ROWS))
    origin = square[...].T[0:ROWS, 0:1].astype(jnp.int32)
    latq[...] = jnp.zeros_like(latq)
    place = pl.ds(pl.multiple_of(a * SHARE, SHARE), SHARE)

    pl.semaphore_wait(barrier, len(greet))
    lat_tp = [push(lat_in.at[t], lat_in.at[t], device) for device in tp_peers]

    w_x = []
    for k in range(7):
        w_x.append(push(wp.at[pl.ds(pl.multiple_of(a_at[k] * SHARE, SHARE), SHARE)], x_in.at[a], a_peers[k]))
    x_in[a] = wp[place, :]
    for copy in w_x:
        copy.wait_recv()
    added = x_in[0].astype(F32)
    for k in range(1, 8):
        added += x_in[k].astype(F32)
    y_in[b] = added.astype(BF16)
    w_b = [push(y_in.at[b], y_in.at[b], device) for device in b_peers]

    for copy in lat_tp:
        copy.wait_recv()
    summed = lat_in[0].astype(F32)
    for k in range(1, 4):
        summed += lat_in[k].astype(F32)
    lat = summed.astype(BF16)
    twice = jnp.concatenate([lat, lat], axis=0)
    squares = jnp.zeros((1, LANES), F32)
    for k in range(PARTS):
        center = dot(centred_t[k * DEPTH : (k + 1) * DEPTH, :], twice, NN)
        squares += jnp.sum(center * center, axis=0, keepdims=True)
    rstd = lax.rsqrt(squares * (1.0 / DIM) + EPS)
    rstd = jnp.broadcast_to(rstd, (LAT, LANES))
    row = lax.broadcasted_iota(jnp.int32, (LAT, LANES), 0)
    lane = lax.broadcasted_iota(jnp.int32, (LAT, LANES), 1)
    high, low = split(rstd)
    piece = lat.astype(F32)
    spare = (lane >= ROWS * (1 - c)) & (lane < ROWS * (1 - c) + LAT)
    for k in range(3):
        turn = (ROWS * (1 - c) - LAT * c - LAT * k + 2 * LANES) % LANES
        piece = jnp.where(spare & (row == k), pltpu.roll(high, turn, 1), piece)
        piece = jnp.where(spare & (row == k + 3), pltpu.roll(low, turn, 1), piece)
    slots[z, c, at] = piece.astype(BF16)
    lat_plane = spread_plane(slots)

    for copy in w_b:
        copy.wait_recv()
    added = y_in[0].astype(F32)
    for k in range(1, 8):
        added += y_in[k].astype(F32)
    wsum[place, :] = added.astype(BF16)
    w_g = [push(wsum.at[place], wsum.at[place], device) for device in a_peers]

    for copy in lat_plane:
        copy.wait_recv()
    lat_rest = spread_rest(slots)
    lat_c = [hand_over(slots, 0)]

    for copy in w_g:
        copy.wait_recv()
    biases = jnp.concatenate([wsum[WPACK - LAT : WPACK, :].astype(F32), jnp.zeros((HD - LAT, HD), F32)], axis=0).T
    lane_w = lax.broadcasted_iota(jnp.int32, (HD, HD), 1)
    for i in range(3):
        packed_rows = wsum[i * ROWS : (i + 1) * ROWS, :].astype(F32)
        both = jnp.concatenate([packed_rows, pltpu.roll(packed_rows, LAT, 1)], axis=0)
        for j in range(HEADS):
            n = HEADS * i + j
            side = jnp.where(lane_w < LAT + 2, biases[:, n : n + 1], 0.0)
            weights[n * HD : (n + 1) * HD, :] = jnp.where(lane_w < LAT, both[j * HD : (j + 1) * HD, :], side).astype(BF16)

    wide_m = lax.broadcasted_iota(jnp.int32, (MCOLS, HD), 1)
    terms = [
        dot(wout_v[:, h * HD : (h + 1) * HD], weights[2 * WID + h * HD : 2 * WID + (h + 1) * HD, :], NN)
        for h in range(HEADS)
    ]
    m_in[0, :, 0:HD] = jnp.where(wide_m < LAT, terms[0], pltpu.roll(terms[1], LAT, 1)).astype(BF16)
    m_in[0, :, HD:LANES] = jnp.where(wide_m < LAT, terms[2], terms[0] + terms[1] + terms[2]).astype(BF16)
    m_move = push(m_in.at[0], m_in.at[1], m_peer)

    lane_t = lax.broadcasted_iota(jnp.int32, (1, HD), 1)
    lane_c = lax.broadcasted_iota(jnp.int32, (1, CHUNK), 1)
    tail_row = lax.broadcasted_iota(jnp.int32, (16, CHUNK), 0)

    def prepare(k, g0, g1):
        for i in range(4):
            n = 4 * k + i
            lats, scales = [], []
            for zz in range(2):
                near = slots[zz, 0, (g1 if zz else g0) * 4 + i]
                far = slots[zz, 1, (g1 if zz else g0) * 4 + i]
                middle = jnp.where(lane_t < LAT, near[:, HD:].astype(F32), far[:, :HD].astype(F32))
                lats += [near[:, :HD].astype(F32), middle, far[:, HD:].astype(F32)]
                sl = near[0:16, HD:].astype(F32)
                sr = far[0:16, :HD].astype(F32)
                sl = sl[0:3] + sl[3:6]
                sr = sr[0:3] + sr[3:6]
                tl = pltpu.roll(sl, LAT, 1)
                tr = pltpu.roll(sr, LAT, 1)
                scales += [
                    jnp.where(lane_t < LAT, tl[0:1], sl[1:2]),
                    jnp.where(lane_t < LAT, tl[2:3], tr[0:1]),
                    jnp.where(lane_t < LAT, sr[1:2], tr[2:3]),
                ]
            lat_c32 = jnp.concatenate(lats, axis=1)
            scale_row = jnp.concatenate(scales, axis=1)
            lat_cb = lat_c32.astype(BF16)
            start = jnp.where(lane_c < 384, (i * 8 + g0 * 2) * ROWS, (32 + g1 * 8 + i * 2) * ROWS - 384)
            token = lane_c + start
            hit = jnp.where(origin == token, 1.0, 0.0).astype(BF16)
            latq[0:ROWS, 0:LAT] += dot(hit, lat_cb, NT)
            scaled = lat_c32 * scale_row
            vals[n, 0:LAT, :] = scaled.astype(BF16)
            vals[n, LAT:FEAT, :] = jnp.where(tail_row == 0, 1.0, 0.0).astype(BF16)
            high, low = split(1.0 / scale_row)
            spread = jnp.where(tail_row == 0, high, 0.0)
            spread = jnp.where(tail_row == 1, low, spread)
            lat_x = jnp.concatenate([lat_cb, spread.astype(BF16)], axis=0)
            for h in range(HEADS):
                raw = dot(weights[WID + h * HD : WID + (h + 1) * HD, 0:FEAT], lat_x, NN)
                power = jnp.mean(raw * raw, axis=0, keepdims=True)
                inv = lax.rsqrt(power * (scale_row * scale_row) + EPS)
                ih, il = split(inv)
                tail = jnp.where((tail_row == 0) | (tail_row == 2), ih, 0.0)
                tail = jnp.where(tail_row == 1, il, tail)
                keys[h, n, 0:LAT, :] = (scaled * inv).astype(BF16)
                keys[h, n, LAT:FEAT, :] = tail.astype(BF16)

    for k in range(4):
        for copy in lat_c[k]:
            copy.wait_recv()
        prepare(k, (y + 4 - k) % 4, (x + 4 - k) % 4)
        if k == 0:
            for j in range(1, 4):
                for copy in lat_rest[j - 1]:
                    copy.wait_recv()
                lat_c.append(hand_over(slots, j))
        if k == 1:
            m_move.wait_recv()
            m_slots[z, c, at] = m_in[1]
            m_plane = spread_plane(m_slots)

    rows = latq[0:ROWS, :].astype(BF16)
    lat_out[...] = latq[...].T[0:LAT, 0:ROWS].astype(BF16)
    twice = (latq[0:ROWS, :] + pltpu.roll(latq[0:ROWS, :], LAT, 1)).astype(BF16)
    squares = jnp.zeros((ROWS, 1), F32)
    for k in range(PARTS):
        center = dot(twice, centred[:, k * DEPTH : (k + 1) * DEPTH], NN)
        squares += jnp.sum(center * center, axis=1, keepdims=True)
    rstd = lax.rsqrt(squares * (1.0 / DIM) + EPS)
    unit = jnp.where(lax.broadcasted_iota(jnp.int32, (16, HD), 1) == LAT, 1.0, 0.0).astype(BF16)
    lane_q = lax.broadcasted_iota(jnp.int32, (ROWS, HD), 1)
    for h in range(HEADS):
        wq = weights[h * HD : (h + 1) * HD, :]
        wk = weights[WID + h * HD : WID + (h + 1) * HD, :]
        raw = rstd * dot(rows, wq, NT) + dot(unit, wq, NT)[0:1, :]
        q = raw * lax.rsqrt(jnp.mean(raw * raw, axis=1, keepdims=True) + EPS) * qg_v[...]
        high, low = split(q * kg_v[...] * (LOG2E / HD**0.5))
        folded = dot(high.astype(BF16), wk, NN) + dot(low.astype(BF16), wk, NN)
        bias_high, bias_low = split(folded[:, LAT : LAT + 1])
        value = jnp.where(lane_q < LAT, folded, 0.0)
        value = jnp.where((lane_q == LAT) | (lane_q == LAT + 1), bias_high, value)
        value = jnp.where(lane_q == LAT + 2, bias_low, value)
        queries[h] = value.astype(BF16)

    scores = [s_even, s_odd]
    running[...] = jnp.full_like(running, -jnp.inf)
    accum[...] = jnp.zeros_like(accum)

    def score(n, h, most):
        part = dot(queries[h][:, 0:FEAT], keys[h, n], NN)
        scores[h % 2][n] = part
        for k in range(CHUNK // HD):
            most = jnp.maximum(most, part[:, k * HD : (k + 1) * HD])
        return most

    def weigh(n, h, most):
        w = jnp.concatenate(
            [jnp.exp2(scores[h % 2][n, :, k * HD : (k + 1) * HD] - most).astype(BF16) for k in range(CHUNK // HD)],
            axis=1,
        )
        return dot(w, vals[n], NT)

    most = running[0]
    for n in range(CHUNKS):
        most = score(n, 0, most)
    running[0] = most
    o_heads = []
    for h in range(HEADS):
        top[h] = jnp.broadcast_to(jnp.max(running[h], axis=1, keepdims=True), (ROWS, HD))

        most = top[h]
        added = accum[h, :, 0:FEAT]
        if h + 1 < HEADS:
            following = running[h + 1]
        for n in range(CHUNKS):
            if h == 0 and n == 4:
                for copy in m_plane:
                    copy.wait_recv()
                m_rest = spread_rest(m_slots)
                m_c = list(hand_over(m_slots, 0))
            if h == 2 and n == CHUNKS // 2:
                for j in range(1, 4):
                    for copy in m_rest[j - 1]:
                        copy.wait_recv()
                    m_c += hand_over(m_slots, j)
            if h + 1 < HEADS:
                following = score(n, h + 1, following)
            added += weigh(n, h, most)
        accum[h, :, 0:FEAT] = added
        if h + 1 < HEADS:
            running[h + 1] = following
        mixed = accum[h] / accum[h, :, LAT : LAT + 1]
        lower = pltpu.roll(mixed[ROWS // 2 :, :], LAT, 1)
        packed[h, t] = jnp.where(lane_q[0 : ROWS // 2] < LAT, mixed[0 : ROWS // 2, :], lower).astype(BF16)
        o_heads.append([push(packed.at[h, t], packed.at[h, t], device) for device in tp_peers])

    for copy in m_c:
        copy.wait_recv()
    for slot in range(64):
        zz, cc, outer, step = slot // 32, (slot // 16) % 2, (slot // 4) % 4, slot % 4
        xx, yy = (outer, step) if zz else (step, outer)
        source_tp, column = 2 * zz + xx // 2, ((xx % 2) * 8 + yy * 2 + 1 - cc) * MCOLS
        assembled[source_tp, pl.ds(column, MCOLS), :] = m_slots[zz, cc, outer * 4 + step]
    quarter = pl.ds(pl.multiple_of(t * QUARTER, QUARTER), QUARTER)
    embedded = dot(rows[:, 0:LAT], emb_v[:, quarter], NN)
    one = jnp.where(lane_q == LAT, 1.0, 0.0)

    def unpacked(h, k):
        both = packed[h, k].astype(F32)
        return jnp.concatenate([both, pltpu.roll(both, LAT, 1)], axis=0)

    for copy in o_heads[0] + o_heads[1]:
        copy.wait_recv()
    total = jnp.zeros((ROWS, QUARTER), F32)
    for k in range(4):
        whole = jnp.where(lane_q < LAT, unpacked(0, k), pltpu.roll(unpacked(1, k), LAT, 1)).astype(BF16)
        total += dot(whole, assembled[k, :, 0:HD], NT)
    for copy in o_heads[2]:
        copy.wait_recv()
    for k in range(4):
        whole = jnp.where(lane_q < LAT, unpacked(2, k), one).astype(BF16)
        total += dot(whole, assembled[k, :, HD:LANES], NT)
    block_out[...] = (embedded + gate_v[:, quarter] * total).astype(BF16)
    for copy in sent:
        copy.wait_send()


def leave(lat_ref, block_ref, lat_to, block_to):
    lat_to[...] = lat_ref[...]
    block_to[...] = block_ref[...]


COPIES = 76
LOADS = 18


def per_device(
    pixels, w_encode, w_latent, source_row, w_embed, mod_shift, mod_scale, gate, q_gain, k_gain, w_qkv, w_out
):
    operands = (
        pixels, w_encode, w_latent.T, source_row.reshape(1, ROWS), w_embed, mod_shift.reshape(1, DIM),
        mod_scale.reshape(1, DIM), gate.reshape(1, DIM), q_gain.reshape(1, HD), k_gain.reshape(1, HD), w_qkv, w_out.T,
    )
    vmem = pltpu.VMEM
    scratch = [
        vmem((PARTS, ROWS, DEPTH), BF16),
        vmem((PARTS, DEPTH, 512), BF16),
        vmem((LAT, 512), BF16),
        vmem((1, ROWS), jnp.int32),
        vmem((LAT, DIM), BF16),
        vmem((1, DIM), F32),
        vmem((1, DIM), F32),
        vmem((1, DIM), F32),
        vmem((1, HD), F32),
        vmem((1, HD), F32),
        vmem((3, MCOLS, WID), BF16),
        vmem((MCOLS, WID), BF16),
        vmem((HD, LANES), F32),
        vmem((HD, DIM), BF16),
        vmem((DIM, HD), BF16),
        vmem((WPACK, HD), BF16),
        vmem((4, LAT, LANES), BF16),
        vmem((8, SHARE, HD), BF16),
        vmem((8, SHARE, HD), BF16),
        vmem((WPACK, HD), BF16),
        vmem((3 * WID, HD), BF16),
        vmem((2, 2, 16, LAT, LANES), BF16),
        vmem((2, MCOLS, LANES), BF16),
        vmem((2, 2, 16, MCOLS, LANES), BF16),
        vmem((LANES, HD), F32),
        vmem((HD, LANES), F32),
        vmem((HEADS, ROWS, HD), BF16),
        vmem((HEADS, CHUNKS, FEAT, CHUNK), BF16),
        vmem((CHUNKS, FEAT, CHUNK), BF16),
        vmem((CHUNKS, ROWS, CHUNK), F32),
        vmem((CHUNKS, ROWS, CHUNK), F32),
        vmem((HEADS, ROWS, HD), F32),
        vmem((HEADS, ROWS, HD), F32),
        vmem((HEADS, ROWS, HD), F32),
        vmem((HEADS, 4, ROWS // 2, HD), BF16),
        vmem((4, QUARTER, LANES), BF16),
        pltpu.SemaphoreType.DMA((LOADS,)),
        pltpu.SemaphoreType.DMA((COPIES,)),
        pltpu.SemaphoreType.DMA((COPIES,)),
    ]
    lat, out = pl.pallas_call(
        kernel,
        out_shape=(jax.ShapeDtypeStruct((LAT, ROWS), BF16), jax.ShapeDtypeStruct((ROWS, QUARTER), BF16)),
        in_specs=[pl.BlockSpec(memory_space=pl.ANY)] * len(operands),
        out_specs=(pl.BlockSpec(memory_space=pltpu.VMEM), pl.BlockSpec(memory_space=pltpu.VMEM)),
        scratch_shapes=scratch,
        compiler_params=pltpu.CompilerParams(collective_id=0, has_side_effects=True, vmem_limit_bytes=VMEM_LIMIT),
    )(*operands)
    lat, out = pl.pallas_call(
        leave,
        out_shape=(jax.ShapeDtypeStruct((LAT, ROWS), BF16), jax.ShapeDtypeStruct((ROWS, QUARTER), BF16)),
    )(lat, out)
    return lat.T, out


def solution(mesh):
    placed = (
        P("sec", None), P(None, "tp"), P("tp", None), P("sec"), P(), P(), P(), P(), P(), P(),
        P(None, "sec", "tp"), P("tp", "sec"),
    )
    return jax.shard_map(
        per_device, mesh=mesh, in_specs=placed, out_specs=(P("sec", None), P("sec", "tp")), check_vma=False
    )
```

```python
import jax
import jax.numpy as jnp
from jax import lax
from jax.experimental import pallas as pl
from jax.experimental.pallas import tpu as pltpu
from jax.sharding import PartitionSpec as P

MESH = pl.DeviceIdType.MESH
HD = 128
HEADS = 3
LAT = 64
ROWS = 192
LANES = 256
WID = HEADS * HD
DIM = 3072
FEAT = 80
CHUNK = 768
CHUNKS = 16
MCOLS = 48
QUARTER = 768
PARTS = 4
DEPTH = DIM // PARTS
F32 = jnp.float32
BF16 = jnp.bfloat16
NT = (((1,), (1,)), ((), ()))
NN = (((1,), (0,)), ((), ()))
TN = (((0,), (0,)), ((), ()))
EPS = 1e-6
WPACK = 640
SHARE = WPACK // 8
LOG2E = 1.4426950408889634
VMEM_LIMIT = 58 * 1024 * 1024


def dot(a, b, dims):
    return lax.dot_general(a, b, dims, preferred_element_type=F32)


def split(value):
    high = value.astype(BF16).astype(F32)
    return high, value - high


def kernel(
    pixels, w_encode, w_latent, source, w_embed, mod_shift, mod_scale, gate, q_gain, k_gain, w_qkv, w_out,
    lat_out, block_out,
    pix_v, enc_v, wlat_v, src_v, emb_v, shift_v, scale_v, gate_v, qg_v, kg_v, wqkv_v, wout_v,
    wide, centred, centred_t, wp, lat_in, x_in, y_in, wsum, weights,
    slots, m_in, m_slots, latq, square, queries, keys, vals, s_even, s_odd, running, top, accum,
    packed, assembled,
    load, send, recv,
):
    s = lax.axis_index("sec")
    t = lax.axis_index("tp")
    z = s // 32
    x = (s // 8) % 4
    y = (s // 2) % 4
    c = s % 2
    b = z * 4 + y
    at = z * (x * 4 + y) + (1 - z) * (y * 4 + x)
    sibling = {"sec": s + 1 - 2 * c}
    tp_peers = [{"tp": (t + k) % 4} for k in (2, 1, 3)]
    x_at = [(x + k) % 4 for k in range(1, 4)]
    x_peers = [{"sec": s + (xx - x) * 8} for xx in x_at]
    b_at = [(b + k) % 8 for k in (2, 6, 1, 3, 5, 7, 4)]
    b_peers = [{"sec": (bb // 4) * 32 + x * 8 + (bb % 4) * 2 + c} for bb in b_at]
    y_peers = [{"sec": s + ((y + k) % 4 - y) * 2} for k in range(1, 4)]
    cross_x = [{"sec": s + (1 - 2 * z) * 32 + (xx - x) * 8} for xx in x_at]
    inner = z * y + (1 - z) * x
    stride = 8 - 6 * z
    plane_peers = [
        {"sec": s + far * (1 - 2 * z) * 32 + ((inner + k) % 4 - inner) * stride}
        for far, k in ((1, 2), (0, 2), (1, 1), (1, 3), (0, 1), (0, 3), (1, 0))
    ]
    m_peer = {"tp": s // 16, "sec": (t // 2) * 32 + (2 * (t % 2) + x % 2) * 8 + y * 2 + 1 - c}
    a = x * 2 + c
    a_at = [(a + k) % 8 for k in (4, 5, 3, 2, 6, 1, 7)]
    a_peers = [{"sec": z * 32 + (aa // 2) * 8 + y * 2 + aa % 2} for aa in a_at]

    sent = []
    used = [0]

    def push(src, dst, device):
        i = used[0]
        used[0] += 1
        copy = pltpu.make_async_remote_copy(
            src_ref=src, dst_ref=dst, send_sem=send.at[i], recv_sem=recv.at[i], device_id=device, device_id_type=MESH
        )
        copy.start()
        sent.append(copy)
        return copy

    def spread_plane(ref):
        return [push(ref.at[z, c, at], ref.at[z, c, at], device) for device in plane_peers]

    by_y = pl.ds(y * 4, 4)
    by_x = pl.ds(x * 4, 4)

    def spread_rest(ref):
        pairs = {}
        for k in (1, 0, 2):
            pairs[k] = (
                push(ref.at[0, c, by_y], ref.at[0, c, by_y], y_peers[k]),
                push(ref.at[1, c, by_x], ref.at[1, c, by_x], x_peers[k]),
            )
        return pairs

    def hand_over(ref, k):
        from_y = pl.ds(((y + 4 - k) % 4) * 4, 4)
        from_x = pl.ds(((x + 4 - k) % 4) * 4, 4)
        return (
            push(ref.at[0, c, from_y], ref.at[0, c, from_y], sibling),
            push(ref.at[1, c, from_x], ref.at[1, c, from_x], sibling),
        )

    barrier = pltpu.get_barrier_semaphore()
    greet = [m_peer] + tp_peers + b_peers + cross_x + a_peers
    for device in greet:
        pl.semaphore_signal(barrier, inc=1, device_id=device, device_id_type=MESH)

    loads = [0]

    def fetch(src, dst):
        copy = pltpu.make_async_copy(src, dst, load.at[loads[0]])
        loads[0] += 1
        copy.start()
        return copy

    early = [fetch(w_embed, emb_v), fetch(w_qkv, wqkv_v), fetch(mod_scale, scale_v), fetch(mod_shift, shift_v)]
    parts = []
    for k in range(PARTS):
        depth = pl.ds(k * DEPTH, DEPTH)
        parts.append((fetch(pixels.at[:, depth], pix_v.at[k]), fetch(w_encode.at[depth], enc_v.at[k])))
    wlat_load = fetch(w_latent, wlat_v)
    late = [
        fetch(source, src_v), fetch(gate, gate_v), fetch(q_gain, qg_v), fetch(k_gain, kg_v), fetch(w_out, wout_v)
    ]

    for copy in early:
        copy.wait()
    block = (3 * s) // 8 - s // 62
    base = pl.ds(pl.multiple_of(block * HD, HD), LANES)
    mean = jnp.mean(emb_v[...].astype(F32), axis=1, keepdims=True)
    wide[0:LAT, :] = (emb_v[:, base].astype(F32) - mean) * scale_v[:, base]
    wide[LAT:HD, :] = jnp.where(
        lax.broadcasted_iota(jnp.int32, (LAT, LANES), 0) < 2, jnp.broadcast_to(shift_v[:, base], (LAT, LANES)), 0.0
    )
    offset = s * MCOLS - block * HD
    rolled = pltpu.roll(wide[...], (LANES - offset) % LANES, 1)[:, 0:HD]
    high, low = split(rolled.T[0:MCOLS, :])
    high, low = high.astype(BF16), low.astype(BF16)
    shift_high, shift_low = split(rolled[LAT : LAT + 16, 0:MCOLS])
    shift_high, shift_low = shift_high.astype(BF16), shift_low.astype(BF16)
    lane_p = lax.broadcasted_iota(jnp.int32, (ROWS, HD), 1)
    row_p = lax.broadcasted_iota(jnp.int32, (LAT, HD), 0)
    biases = jnp.zeros((LAT, HD), F32)
    for i in range(3):
        part = dot(wqkv_v[i], high, TN) + dot(wqkv_v[i], low, TN)
        wp[i * ROWS : (i + 1) * ROWS, :] = jnp.where(
            lane_p < LAT, part[0:ROWS, :], pltpu.roll(part[ROWS:WID, :], LAT, 1)
        ).astype(BF16)
        bias = dot(shift_high, wqkv_v[i], NN) + dot(shift_low, wqkv_v[i], NN)
        for j in range(HEADS):
            biases = jnp.where(row_p == HEADS * i + j, bias[0:1, j * HD : (j + 1) * HD], biases)
    wp[WPACK - LAT : WPACK, :] = biases.astype(BF16)

    high, low = split(emb_v[...].astype(F32) - mean)
    both_terms = jnp.concatenate([high, low], axis=0)
    centred[...] = both_terms.astype(BF16)
    centred_t[...] = both_terms.T.astype(BF16)

    total = jnp.zeros((ROWS, 512), F32)
    for k in range(PARTS):
        parts[k][0].wait()
        parts[k][1].wait()
        total += dot(pix_v[k], enc_v[k], NN)
    hidden = jax.nn.silu(total).astype(BF16)
    wlat_load.wait()
    wide[...] = jnp.zeros_like(wide)
    wide[0:LAT, 0:ROWS] = dot(wlat_v[...], hidden, NT)
    lat_in[t] = pltpu.roll(wide[0:LAT, :], LAT * c, 1).astype(BF16)

    for copy in late:
        copy.wait()
    square[...] = jnp.zeros_like(square)
    square[:, 0:ROWS] = jnp.broadcast_to(src_v[...].astype(F32), (HD, ROWS))
    origin = square[...].T[0:ROWS, 0:1].astype(jnp.int32)
    latq[...] = jnp.zeros_like(latq)
    place = pl.ds(pl.multiple_of(a * SHARE, SHARE), SHARE)

    pl.semaphore_wait(barrier, len(greet))
    lat_tp = [push(lat_in.at[t], lat_in.at[t], device) for device in tp_peers]

    w_x = []
    for k in range(7):
        w_x.append(push(wp.at[pl.ds(pl.multiple_of(a_at[k] * SHARE, SHARE), SHARE)], x_in.at[a], a_peers[k]))
    x_in[a] = wp[place, :]
    for copy in w_x:
        copy.wait_recv()
    added = x_in[0].astype(F32)
    for k in range(1, 8):
        added += x_in[k].astype(F32)
    y_in[b] = added.astype(BF16)
    w_b = [push(y_in.at[b], y_in.at[b], device) for device in b_peers]

    for copy in lat_tp:
        copy.wait_recv()
    summed = lat_in[0].astype(F32)
    for k in range(1, 4):
        summed += lat_in[k].astype(F32)
    lat = summed.astype(BF16)
    twice = jnp.concatenate([lat, lat], axis=0)
    squares = jnp.zeros((1, LANES), F32)
    for k in range(PARTS):
        center = dot(centred_t[k * DEPTH : (k + 1) * DEPTH, :], twice, NN)
        squares += jnp.sum(center * center, axis=0, keepdims=True)
    rstd = lax.rsqrt(squares * (1.0 / DIM) + EPS)
    rstd = jnp.broadcast_to(rstd, (LAT, LANES))
    row = lax.broadcasted_iota(jnp.int32, (LAT, LANES), 0)
    lane = lax.broadcasted_iota(jnp.int32, (LAT, LANES), 1)
    high, low = split(rstd)
    piece = lat.astype(F32)
    spare = (lane >= ROWS * (1 - c)) & (lane < ROWS * (1 - c) + LAT)
    for k in range(3):
        turn = (ROWS * (1 - c) - LAT * c - LAT * k + 2 * LANES) % LANES
        piece = jnp.where(spare & (row == k), pltpu.roll(high, turn, 1), piece)
        piece = jnp.where(spare & (row == k + 3), pltpu.roll(low, turn, 1), piece)
    slots[z, c, at] = piece.astype(BF16)
    lat_plane = spread_plane(slots)

    for copy in w_b:
        copy.wait_recv()
    added = y_in[0].astype(F32)
    for k in range(1, 8):
        added += y_in[k].astype(F32)
    wsum[place, :] = added.astype(BF16)
    w_g = [push(wsum.at[place], wsum.at[place], device) for device in a_peers]

    for copy in lat_plane:
        copy.wait_recv()
    lat_rest = spread_rest(slots)
    lat_c = [hand_over(slots, 0)]

    for copy in w_g:
        copy.wait_recv()
    biases = jnp.concatenate([wsum[WPACK - LAT : WPACK, :].astype(F32), jnp.zeros((HD - LAT, HD), F32)], axis=0).T
    lane_w = lax.broadcasted_iota(jnp.int32, (HD, HD), 1)
    for i in range(3):
        packed_rows = wsum[i * ROWS : (i + 1) * ROWS, :].astype(F32)
        both = jnp.concatenate([packed_rows, pltpu.roll(packed_rows, LAT, 1)], axis=0)
        for j in range(HEADS):
            n = HEADS * i + j
            side = jnp.where(lane_w < LAT + 2, biases[:, n : n + 1], 0.0)
            weights[n * HD : (n + 1) * HD, :] = jnp.where(lane_w < LAT, both[j * HD : (j + 1) * HD, :], side).astype(BF16)

    wide_m = lax.broadcasted_iota(jnp.int32, (MCOLS, HD), 1)
    terms = [
        dot(wout_v[:, h * HD : (h + 1) * HD], weights[2 * WID + h * HD : 2 * WID + (h + 1) * HD, :], NN)
        for h in range(HEADS)
    ]
    m_in[0, :, 0:HD] = jnp.where(wide_m < LAT, terms[0], pltpu.roll(terms[1], LAT, 1)).astype(BF16)
    m_in[0, :, HD:LANES] = jnp.where(wide_m < LAT, terms[2], terms[0] + terms[1] + terms[2]).astype(BF16)
    m_move = push(m_in.at[0], m_in.at[1], m_peer)

    lane_t = lax.broadcasted_iota(jnp.int32, (1, HD), 1)
    lane_c = lax.broadcasted_iota(jnp.int32, (1, CHUNK), 1)
    tail_row = lax.broadcasted_iota(jnp.int32, (16, CHUNK), 0)

    def prepare(k, g0, g1):
        for i in range(4):
            n = 4 * k + i
            lats, scales = [], []
            for zz in range(2):
                near = slots[zz, 0, (g1 if zz else g0) * 4 + i]
                far = slots[zz, 1, (g1 if zz else g0) * 4 + i]
                middle = jnp.where(lane_t < LAT, near[:, HD:].astype(F32), far[:, :HD].astype(F32))
                lats += [near[:, :HD].astype(F32), middle, far[:, HD:].astype(F32)]
                sl = near[0:16, HD:].astype(F32)
                sr = far[0:16, :HD].astype(F32)
                sl = sl[0:3] + sl[3:6]
                sr = sr[0:3] + sr[3:6]
                tl = pltpu.roll(sl, LAT, 1)
                tr = pltpu.roll(sr, LAT, 1)
                scales += [
                    jnp.where(lane_t < LAT, tl[0:1], sl[1:2]),
                    jnp.where(lane_t < LAT, tl[2:3], tr[0:1]),
                    jnp.where(lane_t < LAT, sr[1:2], tr[2:3]),
                ]
            lat_c32 = jnp.concatenate(lats, axis=1)
            scale_row = jnp.concatenate(scales, axis=1)
            lat_cb = lat_c32.astype(BF16)
            start = jnp.where(lane_c < 384, (i * 8 + g0 * 2) * ROWS, (32 + g1 * 8 + i * 2) * ROWS - 384)
            token = lane_c + start
            hit = jnp.where(origin == token, 1.0, 0.0).astype(BF16)
            latq[0:ROWS, 0:LAT] += dot(hit, lat_cb, NT)
            scaled = lat_c32 * scale_row
            vals[n, 0:LAT, :] = scaled.astype(BF16)
            vals[n, LAT:FEAT, :] = jnp.where(tail_row == 0, 1.0, 0.0).astype(BF16)
            high, low = split(1.0 / scale_row)
            spread = jnp.where(tail_row == 0, high, 0.0)
            spread = jnp.where(tail_row == 1, low, spread)
            lat_x = jnp.concatenate([lat_cb, spread.astype(BF16)], axis=0)
            for h in range(HEADS):
                raw = dot(weights[WID + h * HD : WID + (h + 1) * HD, 0:FEAT], lat_x, NN)
                power = jnp.mean(raw * raw, axis=0, keepdims=True)
                inv = lax.rsqrt(power * (scale_row * scale_row) + EPS)
                ih, il = split(inv)
                tail = jnp.where((tail_row == 0) | (tail_row == 2), ih, 0.0)
                tail = jnp.where(tail_row == 1, il, tail)
                keys[h, n, 0:LAT, :] = (scaled * inv).astype(BF16)
                keys[h, n, LAT:FEAT, :] = tail.astype(BF16)

    for k in range(4):
        for copy in lat_c[k]:
            copy.wait_recv()
        prepare(k, (y + 4 - k) % 4, (x + 4 - k) % 4)
        if k == 0:
            for j in range(1, 4):
                for copy in lat_rest[j - 1]:
                    copy.wait_recv()
                lat_c.append(hand_over(slots, j))
        if k == 1:
            m_move.wait_recv()
            m_slots[z, c, at] = m_in[1]
            m_plane = spread_plane(m_slots)

    rows = latq[0:ROWS, :].astype(BF16)
    lat_out[...] = latq[...].T[0:LAT, 0:ROWS].astype(BF16)
    twice = (latq[0:ROWS, :] + pltpu.roll(latq[0:ROWS, :], LAT, 1)).astype(BF16)
    squares = jnp.zeros((ROWS, 1), F32)
    for k in range(PARTS):
        center = dot(twice, centred[:, k * DEPTH : (k + 1) * DEPTH], NN)
        squares += jnp.sum(center * center, axis=1, keepdims=True)
    rstd = lax.rsqrt(squares * (1.0 / DIM) + EPS)
    unit = jnp.where(lax.broadcasted_iota(jnp.int32, (16, HD), 1) == LAT, 1.0, 0.0).astype(BF16)
    lane_q = lax.broadcasted_iota(jnp.int32, (ROWS, HD), 1)
    for h in range(HEADS):
        wq = weights[h * HD : (h + 1) * HD, :]
        wk = weights[WID + h * HD : WID + (h + 1) * HD, :]
        raw = rstd * dot(rows, wq, NT) + dot(unit, wq, NT)[0:1, :]
        q = raw * lax.rsqrt(jnp.mean(raw * raw, axis=1, keepdims=True) + EPS) * qg_v[...]
        high, low = split(q * kg_v[...] * (LOG2E / HD**0.5))
        folded = dot(high.astype(BF16), wk, NN) + dot(low.astype(BF16), wk, NN)
        bias_high, bias_low = split(folded[:, LAT : LAT + 1])
        value = jnp.where(lane_q < LAT, folded, 0.0)
        value = jnp.where((lane_q == LAT) | (lane_q == LAT + 1), bias_high, value)
        value = jnp.where(lane_q == LAT + 2, bias_low, value)
        queries[h] = value.astype(BF16)

    scores = [s_even, s_odd]
    running[...] = jnp.full_like(running, -jnp.inf)
    accum[...] = jnp.zeros_like(accum)

    def score(n, h, most):
        part = dot(queries[h][:, 0:FEAT], keys[h, n], NN)
        scores[h % 2][n] = part
        for k in range(CHUNK // HD):
            most = jnp.maximum(most, part[:, k * HD : (k + 1) * HD])
        return most

    def weigh(n, h, most):
        w = jnp.concatenate(
            [jnp.exp2(scores[h % 2][n, :, k * HD : (k + 1) * HD] - most).astype(BF16) for k in range(CHUNK // HD)],
            axis=1,
        )
        return dot(w, vals[n], NT)

    most = running[0]
    for n in range(CHUNKS):
        most = score(n, 0, most)
    running[0] = most
    o_heads = []
    for h in range(HEADS):
        top[h] = jnp.broadcast_to(jnp.max(running[h], axis=1, keepdims=True), (ROWS, HD))

        most = top[h]
        added = accum[h, :, 0:FEAT]
        if h + 1 < HEADS:
            following = running[h + 1]
        for n in range(CHUNKS):
            if h == 0 and n == 4:
                for copy in m_plane:
                    copy.wait_recv()
                m_rest = spread_rest(m_slots)
                m_c = list(hand_over(m_slots, 0))
            if h == 2 and n == CHUNKS // 2:
                for j in range(1, 4):
                    for copy in m_rest[j - 1]:
                        copy.wait_recv()
                    m_c += hand_over(m_slots, j)
            if h + 1 < HEADS:
                following = score(n, h + 1, following)
            added += weigh(n, h, most)
        accum[h, :, 0:FEAT] = added
        if h + 1 < HEADS:
            running[h + 1] = following
        mixed = accum[h] / accum[h, :, LAT : LAT + 1]
        lower = pltpu.roll(mixed[ROWS // 2 :, :], LAT, 1)
        packed[h, t] = jnp.where(lane_q[0 : ROWS // 2] < LAT, mixed[0 : ROWS // 2, :], lower).astype(BF16)
        o_heads.append([push(packed.at[h, t], packed.at[h, t], device) for device in tp_peers])

    for copy in m_c:
        copy.wait_recv()
    for slot in range(64):
        zz, cc, outer, step = slot // 32, (slot // 16) % 2, (slot // 4) % 4, slot % 4
        xx, yy = (outer, step) if zz else (step, outer)
        source_tp, column = 2 * zz + xx // 2, ((xx % 2) * 8 + yy * 2 + 1 - cc) * MCOLS
        assembled[source_tp, pl.ds(column, MCOLS), :] = m_slots[zz, cc, outer * 4 + step]
    quarter = pl.ds(pl.multiple_of(t * QUARTER, QUARTER), QUARTER)
    embedded = dot(rows[:, 0:LAT], emb_v[:, quarter], NN)
    one = jnp.where(lane_q == LAT, 1.0, 0.0)

    def unpacked(h, k):
        both = packed[h, k].astype(F32)
        return jnp.concatenate([both, pltpu.roll(both, LAT, 1)], axis=0)

    for copy in o_heads[0] + o_heads[1]:
        copy.wait_recv()
    total = jnp.zeros((ROWS, QUARTER), F32)
    for k in range(4):
        whole = jnp.where(lane_q < LAT, unpacked(0, k), pltpu.roll(unpacked(1, k), LAT, 1)).astype(BF16)
        total += dot(whole, assembled[k, :, 0:HD], NT)
    for copy in o_heads[2]:
        copy.wait_recv()
    for k in range(4):
        whole = jnp.where(lane_q < LAT, unpacked(2, k), one).astype(BF16)
        total += dot(whole, assembled[k, :, HD:LANES], NT)
    block_out[...] = (embedded + gate_v[:, quarter] * total).astype(BF16)
    for copy in sent:
        copy.wait_send()


def leave(lat_ref, block_ref, lat_to, block_to):
    lat_to[...] = lat_ref[...]
    block_to[...] = block_ref[...]


COPIES = 76
LOADS = 18


def per_device(
    pixels, w_encode, w_latent, source_row, w_embed, mod_shift, mod_scale, gate, q_gain, k_gain, w_qkv, w_out
):
    operands = (
        pixels, w_encode, w_latent.T, source_row.reshape(1, ROWS), w_embed, mod_shift.reshape(1, DIM),
        mod_scale.reshape(1, DIM), gate.reshape(1, DIM), q_gain.reshape(1, HD), k_gain.reshape(1, HD), w_qkv, w_out.T,
    )
    vmem = pltpu.VMEM
    scratch = [
        vmem((PARTS, ROWS, DEPTH), BF16),
        vmem((PARTS, DEPTH, 512), BF16),
        vmem((LAT, 512), BF16),
        vmem((1, ROWS), jnp.int32),
        vmem((LAT, DIM), BF16),
        vmem((1, DIM), F32),
        vmem((1, DIM), F32),
        vmem((1, DIM), F32),
        vmem((1, HD), F32),
        vmem((1, HD), F32),
        vmem((3, MCOLS, WID), BF16),
        vmem((MCOLS, WID), BF16),
        vmem((HD, LANES), F32),
        vmem((HD, DIM), BF16),
        vmem((DIM, HD), BF16),
        vmem((WPACK, HD), BF16),
        vmem((4, LAT, LANES), BF16),
        vmem((8, SHARE, HD), BF16),
        vmem((8, SHARE, HD), BF16),
        vmem((WPACK, HD), BF16),
        vmem((3 * WID, HD), BF16),
        vmem((2, 2, 16, LAT, LANES), BF16),
        vmem((2, MCOLS, LANES), BF16),
        vmem((2, 2, 16, MCOLS, LANES), BF16),
        vmem((LANES, HD), F32),
        vmem((HD, LANES), F32),
        vmem((HEADS, ROWS, HD), BF16),
        vmem((HEADS, CHUNKS, FEAT, CHUNK), BF16),
        vmem((CHUNKS, FEAT, CHUNK), BF16),
        vmem((CHUNKS, ROWS, CHUNK), F32),
        vmem((CHUNKS, ROWS, CHUNK), F32),
        vmem((HEADS, ROWS, HD), F32),
        vmem((HEADS, ROWS, HD), F32),
        vmem((HEADS, ROWS, HD), F32),
        vmem((HEADS, 4, ROWS // 2, HD), BF16),
        vmem((4, QUARTER, LANES), BF16),
        pltpu.SemaphoreType.DMA((LOADS,)),
        pltpu.SemaphoreType.DMA((COPIES,)),
        pltpu.SemaphoreType.DMA((COPIES,)),
    ]
    lat, out = pl.pallas_call(
        kernel,
        out_shape=(jax.ShapeDtypeStruct((LAT, ROWS), BF16), jax.ShapeDtypeStruct((ROWS, QUARTER), BF16)),
        in_specs=[pl.BlockSpec(memory_space=pl.ANY)] * len(operands),
        out_specs=(pl.BlockSpec(memory_space=pltpu.VMEM), pl.BlockSpec(memory_space=pltpu.VMEM)),
        scratch_shapes=scratch,
        compiler_params=pltpu.CompilerParams(collective_id=0, has_side_effects=True, vmem_limit_bytes=VMEM_LIMIT),
    )(*operands)
    lat, out = pl.pallas_call(
        leave,
        out_shape=(jax.ShapeDtypeStruct((LAT, ROWS), BF16), jax.ShapeDtypeStruct((ROWS, QUARTER), BF16)),
    )(lat, out)
    return lat.T, out


def solution(mesh):
    placed = (
        P("sec", None), P(None, "tp"), P("tp", None), P("sec"), P(), P(), P(), P(), P(), P(),
        P(None, "sec", "tp"), P("tp", "sec"),
    )
    return jax.shard_map(
        per_device, mesh=mesh, in_specs=placed, out_specs=(P("sec", None), P("sec", "tp")), check_vma=False
    )
```

```python
import jax
import jax.numpy as jnp
from jax import lax
from jax.experimental import pallas as pl
from jax.experimental.pallas import tpu as pltpu
from jax.sharding import PartitionSpec as P

MESH = pl.DeviceIdType.MESH
HD = 128
HEADS = 3
LAT = 64
ROWS = 192
LANES = 256
WID = HEADS * HD
DIM = 3072
FEAT = 80
CHUNK = 768
CHUNKS = 16
MCOLS = 48
QUARTER = 768
PARTS = 4
DEPTH = DIM // PARTS
F32 = jnp.float32
BF16 = jnp.bfloat16
NT = (((1,), (1,)), ((), ()))
NN = (((1,), (0,)), ((), ()))
TN = (((0,), (0,)), ((), ()))
EPS = 1e-6
WPACK = 640
SHARE = WPACK // 8
LOG2E = 1.4426950408889634
VMEM_LIMIT = 58 * 1024 * 1024


def dot(a, b, dims):
    return lax.dot_general(a, b, dims, preferred_element_type=F32)


def split(value):
    high = value.astype(BF16).astype(F32)
    return high, value - high


def kernel(
    pixels, w_encode, w_latent, source, w_embed, mod_shift, mod_scale, gate, q_gain, k_gain, w_qkv, w_out,
    lat_out, block_out,
    pix_v, enc_v, wlat_v, src_v, emb_v, shift_v, scale_v, gate_v, qg_v, kg_v, wqkv_v, wout_v,
    wide, centred, centred_t, wp, lat_in, x_in, y_in, wsum, weights,
    slots, m_in, m_slots, latq, square, queries, keys, vals, s_even, s_odd, running, top, accum,
    packed, assembled,
    load, send, recv,
):
    s = lax.axis_index("sec")
    t = lax.axis_index("tp")
    z = s // 32
    x = (s // 8) % 4
    y = (s // 2) % 4
    c = s % 2
    b = z * 4 + y
    at = z * (x * 4 + y) + (1 - z) * (y * 4 + x)
    sibling = {"sec": s + 1 - 2 * c}
    tp_peers = [{"tp": (t + k) % 4} for k in (2, 1, 3)]
    x_at = [(x + k) % 4 for k in range(1, 4)]
    x_peers = [{"sec": s + (xx - x) * 8} for xx in x_at]
    b_at = [(b + k) % 8 for k in (2, 6, 1, 3, 5, 7, 4)]
    b_peers = [{"sec": (bb // 4) * 32 + x * 8 + (bb % 4) * 2 + c} for bb in b_at]
    y_peers = [{"sec": s + ((y + k) % 4 - y) * 2} for k in range(1, 4)]
    cross_x = [{"sec": s + (1 - 2 * z) * 32 + (xx - x) * 8} for xx in x_at]
    inner = z * y + (1 - z) * x
    stride = 8 - 6 * z
    plane_peers = [
        {"sec": s + far * (1 - 2 * z) * 32 + ((inner + k) % 4 - inner) * stride}
        for far, k in ((1, 2), (0, 2), (1, 1), (1, 3), (0, 1), (0, 3), (1, 0))
    ]
    m_peer = {"tp": s // 16, "sec": (t // 2) * 32 + (2 * (t % 2) + x % 2) * 8 + y * 2 + 1 - c}
    a = x * 2 + c
    a_at = [(a + k) % 8 for k in (4, 5, 3, 2, 6, 1, 7)]
    a_peers = [{"sec": z * 32 + (aa // 2) * 8 + y * 2 + aa % 2} for aa in a_at]

    sent = []
    used = [0]

    def push(src, dst, device):
        i = used[0]
        used[0] += 1
        copy = pltpu.make_async_remote_copy(
            src_ref=src, dst_ref=dst, send_sem=send.at[i], recv_sem=recv.at[i], device_id=device, device_id_type=MESH
        )
        copy.start()
        sent.append(copy)
        return copy

    def spread_plane(ref):
        return [push(ref.at[z, c, at], ref.at[z, c, at], device) for device in plane_peers]

    by_y = pl.ds(y * 4, 4)
    by_x = pl.ds(x * 4, 4)

    def spread_rest(ref):
        pairs = {}
        for k in (1, 0, 2):
            pairs[k] = (
                push(ref.at[0, c, by_y], ref.at[0, c, by_y], y_peers[k]),
                push(ref.at[1, c, by_x], ref.at[1, c, by_x], x_peers[k]),
            )
        return pairs

    def hand_over(ref, k):
        from_y = pl.ds(((y + 4 - k) % 4) * 4, 4)
        from_x = pl.ds(((x + 4 - k) % 4) * 4, 4)
        return (
            push(ref.at[0, c, from_y], ref.at[0, c, from_y], sibling),
            push(ref.at[1, c, from_x], ref.at[1, c, from_x], sibling),
        )

    barrier = pltpu.get_barrier_semaphore()
    greet = [m_peer] + tp_peers + b_peers + cross_x + a_peers
    for device in greet:
        pl.semaphore_signal(barrier, inc=1, device_id=device, device_id_type=MESH)

    loads = [0]

    def fetch(src, dst):
        copy = pltpu.make_async_copy(src, dst, load.at[loads[0]])
        loads[0] += 1
        copy.start()
        return copy

    early = [fetch(w_embed, emb_v), fetch(w_qkv, wqkv_v), fetch(mod_scale, scale_v), fetch(mod_shift, shift_v)]
    parts = []
    for k in range(PARTS):
        depth = pl.ds(k * DEPTH, DEPTH)
        parts.append((fetch(pixels.at[:, depth], pix_v.at[k]), fetch(w_encode.at[depth], enc_v.at[k])))
    wlat_load = fetch(w_latent, wlat_v)
    late = [
        fetch(source, src_v), fetch(gate, gate_v), fetch(q_gain, qg_v), fetch(k_gain, kg_v), fetch(w_out, wout_v)
    ]

    for copy in early:
        copy.wait()
    block = (3 * s) // 8 - s // 62
    base = pl.ds(pl.multiple_of(block * HD, HD), LANES)
    mean = jnp.mean(emb_v[...].astype(F32), axis=1, keepdims=True)
    wide[0:LAT, :] = (emb_v[:, base].astype(F32) - mean) * scale_v[:, base]
    wide[LAT:HD, :] = jnp.where(
        lax.broadcasted_iota(jnp.int32, (LAT, LANES), 0) < 2, jnp.broadcast_to(shift_v[:, base], (LAT, LANES)), 0.0
    )
    offset = s * MCOLS - block * HD
    rolled = pltpu.roll(wide[...], (LANES - offset) % LANES, 1)[:, 0:HD]
    high, low = split(rolled.T[0:MCOLS, :])
    high, low = high.astype(BF16), low.astype(BF16)
    shift_high, shift_low = split(rolled[LAT : LAT + 16, 0:MCOLS])
    shift_high, shift_low = shift_high.astype(BF16), shift_low.astype(BF16)
    lane_p = lax.broadcasted_iota(jnp.int32, (ROWS, HD), 1)
    row_p = lax.broadcasted_iota(jnp.int32, (LAT, HD), 0)
    biases = jnp.zeros((LAT, HD), F32)
    for i in range(3):
        part = dot(wqkv_v[i], high, TN) + dot(wqkv_v[i], low, TN)
        wp[i * ROWS : (i + 1) * ROWS, :] = jnp.where(
            lane_p < LAT, part[0:ROWS, :], pltpu.roll(part[ROWS:WID, :], LAT, 1)
        ).astype(BF16)
        bias = dot(shift_high, wqkv_v[i], NN) + dot(shift_low, wqkv_v[i], NN)
        for j in range(HEADS):
            biases = jnp.where(row_p == HEADS * i + j, bias[0:1, j * HD : (j + 1) * HD], biases)
    wp[WPACK - LAT : WPACK, :] = biases.astype(BF16)

    high, low = split(emb_v[...].astype(F32) - mean)
    both_terms = jnp.concatenate([high, low], axis=0)
    centred[...] = both_terms.astype(BF16)
    centred_t[...] = both_terms.T.astype(BF16)

    total = jnp.zeros((ROWS, 512), F32)
    for k in range(PARTS):
        parts[k][0].wait()
        parts[k][1].wait()
        total += dot(pix_v[k], enc_v[k], NN)
    hidden = jax.nn.silu(total).astype(BF16)
    wlat_load.wait()
    wide[...] = jnp.zeros_like(wide)
    wide[0:LAT, 0:ROWS] = dot(wlat_v[...], hidden, NT)
    lat_in[t] = pltpu.roll(wide[0:LAT, :], LAT * c, 1).astype(BF16)

    for copy in late:
        copy.wait()
    square[...] = jnp.zeros_like(square)
    square[:, 0:ROWS] = jnp.broadcast_to(src_v[...].astype(F32), (HD, ROWS))
    origin = square[...].T[0:ROWS, 0:1].astype(jnp.int32)
    latq[...] = jnp.zeros_like(latq)
    place = pl.ds(pl.multiple_of(a * SHARE, SHARE), SHARE)

    pl.semaphore_wait(barrier, len(greet))
    lat_tp = [push(lat_in.at[t], lat_in.at[t], device) for device in tp_peers]

    w_x = []
    for k in range(7):
        w_x.append(push(wp.at[pl.ds(pl.multiple_of(a_at[k] * SHARE, SHARE), SHARE)], x_in.at[a], a_peers[k]))
    x_in[a] = wp[place, :]
    for copy in w_x:
        copy.wait_recv()
    added = x_in[0].astype(F32)
    for k in range(1, 8):
        added += x_in[k].astype(F32)
    y_in[b] = added.astype(BF16)
    w_b = [push(y_in.at[b], y_in.at[b], device) for device in b_peers]

    for copy in lat_tp:
        copy.wait_recv()
    summed = lat_in[0].astype(F32)
    for k in range(1, 4):
        summed += lat_in[k].astype(F32)
    lat = summed.astype(BF16)
    twice = jnp.concatenate([lat, lat], axis=0)
    squares = jnp.zeros((1, LANES), F32)
    for k in range(PARTS):
        center = dot(centred_t[k * DEPTH : (k + 1) * DEPTH, :], twice, NN)
        squares += jnp.sum(center * center, axis=0, keepdims=True)
    rstd = lax.rsqrt(squares * (1.0 / DIM) + EPS)
    rstd = jnp.broadcast_to(rstd, (LAT, LANES))
    row = lax.broadcasted_iota(jnp.int32, (LAT, LANES), 0)
    lane = lax.broadcasted_iota(jnp.int32, (LAT, LANES), 1)
    high, low = split(rstd)
    piece = lat.astype(F32)
    spare = (lane >= ROWS * (1 - c)) & (lane < ROWS * (1 - c) + LAT)
    for k in range(3):
        turn = (ROWS * (1 - c) - LAT * c - LAT * k + 2 * LANES) % LANES
        piece = jnp.where(spare & (row == k), pltpu.roll(high, turn, 1), piece)
        piece = jnp.where(spare & (row == k + 3), pltpu.roll(low, turn, 1), piece)
    slots[z, c, at] = piece.astype(BF16)
    lat_plane = spread_plane(slots)

    for copy in w_b:
        copy.wait_recv()
    added = y_in[0].astype(F32)
    for k in range(1, 8):
        added += y_in[k].astype(F32)
    wsum[place, :] = added.astype(BF16)
    w_g = [push(wsum.at[place], wsum.at[place], device) for device in a_peers]

    for copy in lat_plane:
        copy.wait_recv()
    lat_rest = spread_rest(slots)
    lat_c = [hand_over(slots, 0)]

    for copy in w_g:
        copy.wait_recv()
    biases = jnp.concatenate([wsum[WPACK - LAT : WPACK, :].astype(F32), jnp.zeros((HD - LAT, HD), F32)], axis=0).T
    lane_w = lax.broadcasted_iota(jnp.int32, (HD, HD), 1)
    for i in range(3):
        packed_rows = wsum[i * ROWS : (i + 1) * ROWS, :].astype(F32)
        both = jnp.concatenate([packed_rows, pltpu.roll(packed_rows, LAT, 1)], axis=0)
        for j in range(HEADS):
            n = HEADS * i + j
            side = jnp.where(lane_w < LAT + 2, biases[:, n : n + 1], 0.0)
            weights[n * HD : (n + 1) * HD, :] = jnp.where(lane_w < LAT, both[j * HD : (j + 1) * HD, :], side).astype(BF16)

    wide_m = lax.broadcasted_iota(jnp.int32, (MCOLS, HD), 1)
    terms = [
        dot(wout_v[:, h * HD : (h + 1) * HD], weights[2 * WID + h * HD : 2 * WID + (h + 1) * HD, :], NN)
        for h in range(HEADS)
    ]
    m_in[0, :, 0:HD] = jnp.where(wide_m < LAT, terms[0], pltpu.roll(terms[1], LAT, 1)).astype(BF16)
    m_in[0, :, HD:LANES] = jnp.where(wide_m < LAT, terms[2], terms[0] + terms[1] + terms[2]).astype(BF16)
    m_move = push(m_in.at[0], m_in.at[1], m_peer)

    lane_t = lax.broadcasted_iota(jnp.int32, (1, HD), 1)
    lane_c = lax.broadcasted_iota(jnp.int32, (1, CHUNK), 1)
    tail_row = lax.broadcasted_iota(jnp.int32, (16, CHUNK), 0)

    def prepare(k, g0, g1):
        for i in range(4):
            n = 4 * k + i
            lats, scales = [], []
            for zz in range(2):
                near = slots[zz, 0, (g1 if zz else g0) * 4 + i]
                far = slots[zz, 1, (g1 if zz else g0) * 4 + i]
                middle = jnp.where(lane_t < LAT, near[:, HD:].astype(F32), far[:, :HD].astype(F32))
                lats += [near[:, :HD].astype(F32), middle, far[:, HD:].astype(F32)]
                sl = near[0:16, HD:].astype(F32)
                sr = far[0:16, :HD].astype(F32)
                sl = sl[0:3] + sl[3:6]
                sr = sr[0:3] + sr[3:6]
                tl = pltpu.roll(sl, LAT, 1)
                tr = pltpu.roll(sr, LAT, 1)
                scales += [
                    jnp.where(lane_t < LAT, tl[0:1], sl[1:2]),
                    jnp.where(lane_t < LAT, tl[2:3], tr[0:1]),
                    jnp.where(lane_t < LAT, sr[1:2], tr[2:3]),
                ]
            lat_c32 = jnp.concatenate(lats, axis=1)
            scale_row = jnp.concatenate(scales, axis=1)
            lat_cb = lat_c32.astype(BF16)
            start = jnp.where(lane_c < 384, (i * 8 + g0 * 2) * ROWS, (32 + g1 * 8 + i * 2) * ROWS - 384)
            token = lane_c + start
            hit = jnp.where(origin == token, 1.0, 0.0).astype(BF16)
            latq[0:ROWS, 0:LAT] += dot(hit, lat_cb, NT)
            scaled = lat_c32 * scale_row
            vals[n, 0:LAT, :] = scaled.astype(BF16)
            vals[n, LAT:FEAT, :] = jnp.where(tail_row == 0, 1.0, 0.0).astype(BF16)
            high, low = split(1.0 / scale_row)
            spread = jnp.where(tail_row == 0, high, 0.0)
            spread = jnp.where(tail_row == 1, low, spread)
            lat_x = jnp.concatenate([lat_cb, spread.astype(BF16)], axis=0)
            for h in range(HEADS):
                raw = dot(weights[WID + h * HD : WID + (h + 1) * HD, 0:FEAT], lat_x, NN)
                power = jnp.mean(raw * raw, axis=0, keepdims=True)
                inv = lax.rsqrt(power * (scale_row * scale_row) + EPS)
                ih, il = split(inv)
                tail = jnp.where((tail_row == 0) | (tail_row == 2), ih, 0.0)
                tail = jnp.where(tail_row == 1, il, tail)
                keys[h, n, 0:LAT, :] = (scaled * inv).astype(BF16)
                keys[h, n, LAT:FEAT, :] = tail.astype(BF16)

    for k in range(4):
        for copy in lat_c[k]:
            copy.wait_recv()
        prepare(k, (y + 4 - k) % 4, (x + 4 - k) % 4)
        if k == 0:
            for j in range(1, 4):
                for copy in lat_rest[j - 1]:
                    copy.wait_recv()
                lat_c.append(hand_over(slots, j))
        if k == 2:
            m_move.wait_recv()
            m_slots[z, c, at] = m_in[1]
            m_plane = spread_plane(m_slots)

    rows = latq[0:ROWS, :].astype(BF16)
    lat_out[...] = latq[...].T[0:LAT, 0:ROWS].astype(BF16)
    twice = (latq[0:ROWS, :] + pltpu.roll(latq[0:ROWS, :], LAT, 1)).astype(BF16)
    squares = jnp.zeros((ROWS, 1), F32)
    for k in range(PARTS):
        center = dot(twice, centred[:, k * DEPTH : (k + 1) * DEPTH], NN)
        squares += jnp.sum(center * center, axis=1, keepdims=True)
    rstd = lax.rsqrt(squares * (1.0 / DIM) + EPS)
    unit = jnp.where(lax.broadcasted_iota(jnp.int32, (16, HD), 1) == LAT, 1.0, 0.0).astype(BF16)
    lane_q = lax.broadcasted_iota(jnp.int32, (ROWS, HD), 1)
    for h in range(HEADS):
        wq = weights[h * HD : (h + 1) * HD, :]
        wk = weights[WID + h * HD : WID + (h + 1) * HD, :]
        raw = rstd * dot(rows, wq, NT) + dot(unit, wq, NT)[0:1, :]
        q = raw * lax.rsqrt(jnp.mean(raw * raw, axis=1, keepdims=True) + EPS) * qg_v[...]
        high, low = split(q * kg_v[...] * (LOG2E / HD**0.5))
        folded = dot(high.astype(BF16), wk, NN) + dot(low.astype(BF16), wk, NN)
        bias_high, bias_low = split(folded[:, LAT : LAT + 1])
        value = jnp.where(lane_q < LAT, folded, 0.0)
        value = jnp.where((lane_q == LAT) | (lane_q == LAT + 1), bias_high, value)
        value = jnp.where(lane_q == LAT + 2, bias_low, value)
        queries[h] = value.astype(BF16)

    scores = [s_even, s_odd]
    running[...] = jnp.full_like(running, -jnp.inf)
    accum[...] = jnp.zeros_like(accum)

    def score(n, h, most):
        part = dot(queries[h][:, 0:FEAT], keys[h, n], NN)
        scores[h % 2][n] = part
        for k in range(CHUNK // HD):
            most = jnp.maximum(most, part[:, k * HD : (k + 1) * HD])
        return most

    def weigh(n, h, most):
        w = jnp.concatenate(
            [jnp.exp2(scores[h % 2][n, :, k * HD : (k + 1) * HD] - most).astype(BF16) for k in range(CHUNK // HD)],
            axis=1,
        )
        return dot(w, vals[n], NT)

    most = running[0]
    for n in range(CHUNKS):
        most = score(n, 0, most)
    running[0] = most
    o_heads = []
    for h in range(HEADS):
        top[h] = jnp.broadcast_to(jnp.max(running[h], axis=1, keepdims=True), (ROWS, HD))

        most = top[h]
        added = accum[h, :, 0:FEAT]
        if h + 1 < HEADS:
            following = running[h + 1]
        for n in range(CHUNKS):
            if h == 0 and n == 10:
                for copy in m_plane:
                    copy.wait_recv()
                m_rest = spread_rest(m_slots)
                m_c = list(hand_over(m_slots, 0))
            if h + 1 < HEADS:
                following = score(n, h + 1, following)
            added += weigh(n, h, most)
        accum[h, :, 0:FEAT] = added
        if h + 1 < HEADS:
            running[h + 1] = following
        mixed = accum[h] / accum[h, :, LAT : LAT + 1]
        lower = pltpu.roll(mixed[ROWS // 2 :, :], LAT, 1)
        packed[h, t] = jnp.where(lane_q[0 : ROWS // 2] < LAT, mixed[0 : ROWS // 2, :], lower).astype(BF16)
        o_heads.append([push(packed.at[h, t], packed.at[h, t], device) for device in tp_peers])

    for j in range(1, 4):
        for copy in m_rest[j - 1]:
            copy.wait_recv()
        m_c += hand_over(m_slots, j)
    for copy in m_c:
        copy.wait_recv()
    for slot in range(64):
        zz, cc, outer, step = slot // 32, (slot // 16) % 2, (slot // 4) % 4, slot % 4
        xx, yy = (outer, step) if zz else (step, outer)
        source_tp, column = 2 * zz + xx // 2, ((xx % 2) * 8 + yy * 2 + 1 - cc) * MCOLS
        assembled[source_tp, pl.ds(column, MCOLS), :] = m_slots[zz, cc, outer * 4 + step]
    quarter = pl.ds(pl.multiple_of(t * QUARTER, QUARTER), QUARTER)
    embedded = dot(rows[:, 0:LAT], emb_v[:, quarter], NN)
    one = jnp.where(lane_q == LAT, 1.0, 0.0)

    def unpacked(h, k):
        both = packed[h, k].astype(F32)
        return jnp.concatenate([both, pltpu.roll(both, LAT, 1)], axis=0)

    for copy in o_heads[0] + o_heads[1]:
        copy.wait_recv()
    total = jnp.zeros((ROWS, QUARTER), F32)
    for k in range(4):
        whole = jnp.where(lane_q < LAT, unpacked(0, k), pltpu.roll(unpacked(1, k), LAT, 1)).astype(BF16)
        total += dot(whole, assembled[k, :, 0:HD], NT)
    for copy in o_heads[2]:
        copy.wait_recv()
    for k in range(4):
        whole = jnp.where(lane_q < LAT, unpacked(2, k), one).astype(BF16)
        total += dot(whole, assembled[k, :, HD:LANES], NT)
    block_out[...] = (embedded + gate_v[:, quarter] * total).astype(BF16)
    for copy in sent:
        copy.wait_send()


def leave(lat_ref, block_ref, lat_to, block_to):
    lat_to[...] = lat_ref[...]
    block_to[...] = block_ref[...]


COPIES = 76
LOADS = 18


def per_device(
    pixels, w_encode, w_latent, source_row, w_embed, mod_shift, mod_scale, gate, q_gain, k_gain, w_qkv, w_out
):
    operands = (
        pixels, w_encode, w_latent.T, source_row.reshape(1, ROWS), w_embed, mod_shift.reshape(1, DIM),
        mod_scale.reshape(1, DIM), gate.reshape(1, DIM), q_gain.reshape(1, HD), k_gain.reshape(1, HD), w_qkv, w_out.T,
    )
    vmem = pltpu.VMEM
    scratch = [
        vmem((PARTS, ROWS, DEPTH), BF16),
        vmem((PARTS, DEPTH, 512), BF16),
        vmem((LAT, 512), BF16),
        vmem((1, ROWS), jnp.int32),
        vmem((LAT, DIM), BF16),
        vmem((1, DIM), F32),
        vmem((1, DIM), F32),
        vmem((1, DIM), F32),
        vmem((1, HD), F32),
        vmem((1, HD), F32),
        vmem((3, MCOLS, WID), BF16),
        vmem((MCOLS, WID), BF16),
        vmem((HD, LANES), F32),
        vmem((HD, DIM), BF16),
        vmem((DIM, HD), BF16),
        vmem((WPACK, HD), BF16),
        vmem((4, LAT, LANES), BF16),
        vmem((8, SHARE, HD), BF16),
        vmem((8, SHARE, HD), BF16),
        vmem((WPACK, HD), BF16),
        vmem((3 * WID, HD), BF16),
        vmem((2, 2, 16, LAT, LANES), BF16),
        vmem((2, MCOLS, LANES), BF16),
        vmem((2, 2, 16, MCOLS, LANES), BF16),
        vmem((LANES, HD), F32),
        vmem((HD, LANES), F32),
        vmem((HEADS, ROWS, HD), BF16),
        vmem((HEADS, CHUNKS, FEAT, CHUNK), BF16),
        vmem((CHUNKS, FEAT, CHUNK), BF16),
        vmem((CHUNKS, ROWS, CHUNK), F32),
        vmem((CHUNKS, ROWS, CHUNK), F32),
        vmem((HEADS, ROWS, HD), F32),
        vmem((HEADS, ROWS, HD), F32),
        vmem((HEADS, ROWS, HD), F32),
        vmem((HEADS, 4, ROWS // 2, HD), BF16),
        vmem((4, QUARTER, LANES), BF16),
        pltpu.SemaphoreType.DMA((LOADS,)),
        pltpu.SemaphoreType.DMA((COPIES,)),
        pltpu.SemaphoreType.DMA((COPIES,)),
    ]
    lat, out = pl.pallas_call(
        kernel,
        out_shape=(jax.ShapeDtypeStruct((LAT, ROWS), BF16), jax.ShapeDtypeStruct((ROWS, QUARTER), BF16)),
        in_specs=[pl.BlockSpec(memory_space=pl.ANY)] * len(operands),
        out_specs=(pl.BlockSpec(memory_space=pltpu.VMEM), pl.BlockSpec(memory_space=pltpu.VMEM)),
        scratch_shapes=scratch,
        compiler_params=pltpu.CompilerParams(collective_id=0, has_side_effects=True, vmem_limit_bytes=VMEM_LIMIT),
    )(*operands)
    lat, out = pl.pallas_call(
        leave,
        out_shape=(jax.ShapeDtypeStruct((LAT, ROWS), BF16), jax.ShapeDtypeStruct((ROWS, QUARTER), BF16)),
    )(lat, out)
    return lat.T, out


def solution(mesh):
    placed = (
        P("sec", None), P(None, "tp"), P("tp", None), P("sec"), P(), P(), P(), P(), P(), P(),
        P(None, "sec", "tp"), P("tp", "sec"),
    )
    return jax.shard_map(
        per_device, mesh=mesh, in_specs=placed, out_specs=(P("sec", None), P("sec", "tp")), check_vma=False
    )
```
